32 devices in a mesh: dp: 8 (over y, x, core), mp: 4 (over z).
Axes of the slice: x: 2, y: 2, z: 4, core: 2. Of those that a mesh axis runs over, the one named last changes fastest.
Arguments:
- hidden_in: bfloat16 [16, 1024, 768], P('dp', 'mp'), may hold values from -6 to 6
- out_grad: bfloat16 [16, 1024, 768], P('dp', 'mp'), may hold values from -6 to 6
- seg_ids: int32 [16, 1024], P('dp'), may hold values from 0 to 3, as said below
- row_len: int32 [16], P('dp'), may hold values from 512 to 1024
- slot_mask: int32 [16, 16], P('dp'), may hold values 0 or 1
- mem_keys: bfloat16 [16, 32, 768], P('dp', None, 'mp'), may hold values from -6 to 6
- mem_values: bfloat16 [16, 32, 768], P('dp', None, 'mp'), may hold values from -6 to 6
- w_qkv: float32 [3, 768, 768], P(None, 'dp', 'mp'), may hold values from -0.21875 to 0.21875
- m_qkv: float32 [3, 768, 768], P(None, 'dp', 'mp'), as said below
- v_qkv: float32 [3, 768, 768], P(None, 'dp', 'mp'), may hold values from 8192 to 131072, as said below
- w_attn_out: float32 [768, 768], P('mp', 'dp'), may hold values from -1.25 to 1.25
- m_attn_out: float32 [768, 768], P('mp', 'dp'), as said below
- v_attn_out: float32 [768, 768], P('mp', 'dp'), may hold values from 512 to 8192, as said below
- w_up: float32 [768, 3072], P('dp', 'mp'), may hold values from -0.21875 to 0.21875
- m_up: float32 [768, 3072], P('dp', 'mp'), as said below
- v_up: float32 [768, 3072], P('dp', 'mp'), may hold values from 512 to 8192, as said below
- w_down: float32 [3072, 768], P('mp', 'dp'), may hold values from -0.109375 to 0.109375
- m_down: float32 [3072, 768], P('mp', 'dp'), as said below
- v_down: float32 [3072, 768], P('mp', 'dp'), may hold values from 2048 to 32768, as said below
- gains: float32 [2, 768], replicated, may hold values from 0.5 to 1.5
- m_gains: float32 [2, 768], replicated, as said below
- v_gains: float32 [2, 768], replicated, may hold values from 8192 to 131072, as said below
- rel_table: float32 [32, 12], replicated, may hold values from -4 to 4
- m_rel: float32 [32, 12], replicated, as said below
- v_rel: float32 [32, 12], replicated, may hold values from 8192 to 131072, as said below
Outputs:
- output: bfloat16 [16, 1024, 768], P('dp', 'mp')
- grad_input: float32 [16, 1024, 768], P('dp', 'mp')
- qkv_new: float32 [3, 768, 768], P(None, 'dp', 'mp')
- qkv_first: float32 [3, 768, 768], P(None, 'dp', 'mp')
- qkv_second: float32 [3, 768, 768], P(None, 'dp', 'mp')
- qkv_copy: bfloat16 [3, 768, 768], P(None, 'dp', 'mp')
- attn_out_new: float32 [768, 768], P('mp', 'dp')
- attn_out_first: float32 [768, 768], P('mp', 'dp')
- attn_out_second: float32 [768, 768], P('mp', 'dp')
- attn_out_copy: bfloat16 [768, 768], P('mp', 'dp')
- up_new: float32 [768, 3072], P('dp', 'mp')
- up_first: float32 [768, 3072], P('dp', 'mp')
- up_second: float32 [768, 3072], P('dp', 'mp')
- up_copy: bfloat16 [768, 3072], P('dp', 'mp')
- down_new: float32 [3072, 768], P('mp', 'dp')
- down_first: float32 [3072, 768], P('mp', 'dp')
- down_second: float32 [3072, 768], P('mp', 'dp')
- down_copy: bfloat16 [3072, 768], P('mp', 'dp')
- gains_new: float32 [2, 768], replicated
- gains_first: float32 [2, 768], replicated
- gains_second: float32 [2, 768], replicated
- rel_new: float32 [32, 12], replicated
- rel_first: float32 [32, 12], replicated
- rel_second: float32 [32, 12], replicated
The draws below stay inside these ranges and needn't reach their ends.
Inputs may be any that keep to these rules, and one draw needn't show every extreme that they name: `seg_ids`: in every row the document numbers start at 0 and never fall; in each aligned block of 2 rows one row, drawn from the seed, is a single document with row_len 1024. `m_qkv`: both signs. `v_qkv`: positive. `m_attn_out`: both signs. `v_attn_out`: positive. `m_up`: both signs. `v_up`: positive. `m_down`: both signs. `v_down`: positive. `m_gains`: both signs. `v_gains`: positive. `m_rel`: both signs. `v_rel`: positive.
All inputs are finite; a program needn't handle non-finite values. No bound on the sum of `slot_mask` on one device may be relied on, other than what follows from the above.
Results may differ from the reference program's by a relative error of at most 0.017.
Values may be sent and summed in bfloat16 or wider, within the bound.
A program may use at most 256 MiB of HBM per device.

```python
import math
import jax
import jax.numpy as jnp
from jax import lax

D = 768
HEADS = 12
HEAD_DIM = 64
FF = 3072
BUCKETS = 32
SEQ = 1024
MEM = 16
DOC_MEAN = 256
STEP = 10
ROWS_DEV = 2
HD = 768
SLOTS = 32
ROWS = 16
TOKENS = 16384


def row_layout(key):
    key_len, key_pick, key_cut = jax.random.split(key, 3)
    lengths = jax.random.randint(key_len, (ROWS,), SEQ // 2, SEQ + 1).astype(jnp.int32)
    pick_row = jax.random.randint(key_pick, (ROWS // ROWS_DEV,), 0, ROWS_DEV).astype(jnp.int32)
    chosen = jnp.arange(ROWS, dtype=jnp.int32) % ROWS_DEV == jnp.repeat(pick_row, ROWS_DEV)
    lengths = jnp.where(chosen, SEQ, lengths).astype(jnp.int32)
    column = jnp.arange(SEQ, dtype=jnp.int32)[None, :]
    starts = jax.random.randint(key_cut, (ROWS, SEQ), 0, DOC_MEAN) == 0
    starts = starts | (column % DOC_MEAN == 0)
    starts = starts & (column > 0) & jnp.logical_not(chosen[:, None])
    segments = jnp.cumsum(starts.astype(jnp.int32), axis=1).astype(jnp.int32)
    segments = jnp.minimum(segments, SEQ // DOC_MEAN - 1).astype(jnp.int32)
    return (segments, lengths)


def draw_seg_ids(key, part):
    segments, lengths = row_layout(key)
    return segments


def draw_row_len(key, part):
    segments, lengths = row_layout(key)
    return lengths


def first_moment(key, array_shape, mean_square):
    return math.sqrt(mean_square) * jax.random.uniform(key, array_shape, jnp.float32, -1.5, 1.5)


def second_moment(key, array_shape, mean_square):
    spread = jnp.exp(jax.random.uniform(key, array_shape, jnp.float32, math.log(0.5), math.log(8.0)))
    return mean_square * spread


def draw_m_qkv(key, part):
    key = jax.random.fold_in(key, 11)
    return first_moment(key, (3, D, HD), TOKENS)


def draw_v_qkv(key, part):
    key = jax.random.fold_in(key, 12)
    return second_moment(key, (3, D, HD), TOKENS)


def draw_m_attn_out(key, part):
    key = jax.random.fold_in(key, 13)
    return first_moment(key, (HD, D), TOKENS // 16)


def draw_v_attn_out(key, part):
    key = jax.random.fold_in(key, 14)
    return second_moment(key, (HD, D), TOKENS // 16)


def draw_m_up(key, part):
    key = jax.random.fold_in(key, 15)
    return first_moment(key, (D, FF), TOKENS // 16)


def draw_v_up(key, part):
    key = jax.random.fold_in(key, 16)
    return second_moment(key, (D, FF), TOKENS // 16)


def draw_m_down(key, part):
    key = jax.random.fold_in(key, 17)
    return first_moment(key, (FF, D), TOKENS // 4)


def draw_v_down(key, part):
    key = jax.random.fold_in(key, 18)
    return second_moment(key, (FF, D), TOKENS // 4)


def draw_m_gains(key, part):
    key = jax.random.fold_in(key, 19)
    return first_moment(key, (2, D), TOKENS)


def draw_v_gains(key, part):
    key = jax.random.fold_in(key, 20)
    return second_moment(key, (2, D), TOKENS)


def draw_m_rel(key, part):
    key = jax.random.fold_in(key, 21)
    return first_moment(key, (BUCKETS, HEADS), TOKENS)


def draw_v_rel(key, part):
    key = jax.random.fold_in(key, 22)
    return second_moment(key, (BUCKETS, HEADS), TOKENS)


def set_ends(entries, stream_key, low, high):
    spot = [jax.random.randint(jax.random.fold_in(stream_key, axis), (), 0, length) for axis, length in enumerate(entries.shape)]
    widest = entries.shape.index(max(entries.shape))
    next_to = spot[:widest] + [(spot[widest] + 1) % entries.shape[widest]] + spot[widest + 1:]
    return entries.at[tuple(spot)].set(low).at[tuple(next_to)].set(high)


def levels(own_key, extent, cuts, low, largest):
    gain, own = 1.0, jax.random.fold_in(own_key, 6)
    for dim, shards_of in cuts:
        heights = jnp.exp(jax.random.uniform(jax.random.fold_in(own, dim), (shards_of,), jnp.float32, low / len(cuts), largest / len(cuts)))
        gain = gain * jnp.repeat(heights, extent[dim] // shards_of).reshape([-1 if axis == dim else 1 for axis in range(len(extent))])
    return gain


def normal_values(own_key, extent, deviation, reach, shards=(), held_as=jnp.bfloat16):
    values = jax.random.normal(own_key, extent, jnp.float32) * deviation
    if len(shards) > 0:
        values = levels(own_key, extent, shards, -0.22, 0.18) * values
    return jnp.clip(values, min=-reach, max=reach).astype(held_as)


def setup_inputs(seed: int = 0) -> dict:
    key_list = jax.random.split(jax.random.key(seed), 26)
    return {
        "hidden_in": normal_values(key_list[0], (ROWS, SEQ, D), 1.0, 6.0, ((0, 8), (1, 4))),
        "out_grad": normal_values(key_list[1], (ROWS, SEQ, D), 1.0, 6.0, ((0, 8), (1, 4))),
        "seg_ids": draw_seg_ids(jax.random.fold_in(key_list[25], 71), 0),
        "row_len": draw_row_len(jax.random.fold_in(key_list[25], 71), 0),
        "slot_mask": set_ends((jax.random.randint(key_list[4], (ROWS, MEM), 0, 4) < 3).astype(jnp.int32), jax.random.fold_in(key_list[4], 1), 0, 1),
        "mem_keys": normal_values(key_list[5], (ROWS, SLOTS, HD), 1.0, 6.0, ((0, 8), (2, 4))),
        "mem_values": normal_values(key_list[6], (ROWS, SLOTS, HD), 1.0, 6.0, ((0, 8), (2, 4))),
        "w_qkv": normal_values(key_list[7], (3, D, HD), D ** -0.5, 0.21875, ((1, 8), (2, 4)), jnp.float32),
        "m_qkv": draw_m_qkv(jax.random.fold_in(key_list[25], 71), 0),
        "v_qkv": draw_v_qkv(jax.random.fold_in(key_list[25], 71), 0),
        "w_attn_out": normal_values(key_list[10], (HD, D), (HD // 32) ** -0.5, 1.25, ((0, 4), (1, 8)), jnp.float32),
        "m_attn_out": draw_m_attn_out(jax.random.fold_in(key_list[25], 71), 0),
        "v_attn_out": draw_v_attn_out(jax.random.fold_in(key_list[25], 71), 0),
        "w_up": normal_values(key_list[13], (D, FF), D ** -0.5, 0.21875, ((0, 8), (1, 4)), jnp.float32),
        "m_up": draw_m_up(jax.random.fold_in(key_list[25], 71), 0),
        "v_up": draw_v_up(jax.random.fold_in(key_list[25], 71), 0),
        "w_down": normal_values(key_list[16], (FF, D), FF ** -0.5, 0.109375, ((0, 4), (1, 8)), jnp.float32),
        "m_down": draw_m_down(jax.random.fold_in(key_list[25], 71), 0),
        "v_down": draw_v_down(jax.random.fold_in(key_list[25], 71), 0),
        "gains": jnp.clip(1.0 + 0.1 * jax.random.normal(key_list[19], (2, D), jnp.float32), 0.5, 1.5),
        "m_gains": draw_m_gains(jax.random.fold_in(key_list[25], 71), 0),
        "v_gains": draw_v_gains(jax.random.fold_in(key_list[25], 71), 0),
        "rel_table": normal_values(key_list[22], (BUCKETS, HEADS), 1.0, 4.0, (), jnp.float32),
        "m_rel": draw_m_rel(jax.random.fold_in(key_list[25], 71), 0),
        "v_rel": draw_v_rel(jax.random.fold_in(key_list[25], 71), 0),
    }


@jax.custom_vjp
def low(v):
    return lax.optimization_barrier(v.astype(jnp.bfloat16)).astype(jnp.float32)

@jax.custom_vjp
def low_back(v):
    return v

def low_keep(v):
    return (low(v), None)

def low_pass(kept, grad):
    return (grad,)

def back_keep(v):
    return (v, None)

def back_low(kept, grad):
    return (low(grad),)
low.defvjp(low_keep, low_pass)
low_back.defvjp(back_keep, back_low)
NORM_EPS = 1e-06
MOMENT_DECAY = 0.5
ADAM_EPS = 1e-08
MATRIX_RATE = 0.05
SMALL_RATE = 0.5
WEIGHT_DECAY = 0.01
FAR_BOUNDS = (12, 16, 23, 32, 46, 64, 91)
NEG_FILL = -1e+30
FULL_PRECISION = lax.Precision.HIGHEST

def bucket_of(distance):
    far_dist = jnp.abs(distance)
    far_bucket = jnp.full(far_dist.shape, 8, jnp.int32)
    for far_bound in FAR_BOUNDS:
        far_bucket = far_bucket + (far_dist >= far_bound).astype(jnp.int32)
    one_side = jnp.where(far_dist < 8, far_dist, far_bucket).astype(jnp.int32)
    return one_side + jnp.where(distance > 0, 16, 0).astype(jnp.int32)

def gelu_exact(values):
    return jax.nn.gelu(values, approximate=False)

def row_forward(inputs, w_qkv, w_attn_out, w_up, w_down, gains, rel_table, seg_row, length, pair_on, mk_row, mv_row):
    seq_span = inputs.shape[0]
    slots = mk_row.shape[0]
    positions = jnp.arange(seq_span, dtype=jnp.int32)
    is_live = positions < length
    doc_group = jnp.where(is_live, seg_row, -1).astype(jnp.int32)
    slot_on = jnp.repeat(pair_on, 2) > 0
    allowed = jnp.concatenate([is_live[:, None] & slot_on[None, :], doc_group[:, None] == doc_group[None, :]], axis=1)
    rel_bias = jnp.transpose(rel_table[bucket_of(positions[None, :] - positions[:, None])], (2, 0, 1))
    bias_full = jnp.concatenate([jnp.zeros((HEADS, seq_span, slots), jnp.float32), rel_bias], axis=2)
    normed = low(inputs * lax.rsqrt(lax.optimization_barrier(jnp.mean(inputs * inputs, axis=-1, keepdims=True)) + NORM_EPS) * gains[0])
    project = jnp.einsum('sd,cdh->csh', normed, low(w_qkv), precision=FULL_PRECISION)
    project = low_back(low(project))
    queries = project[0].reshape(seq_span, HEADS, HEAD_DIM)
    key_rows = jnp.concatenate([mk_row.reshape(slots, HEADS, HEAD_DIM), project[1].reshape(seq_span, HEADS, HEAD_DIM)], axis=0)
    value_rows = jnp.concatenate([mv_row.reshape(slots, HEADS, HEAD_DIM), project[2].reshape(seq_span, HEADS, HEAD_DIM)], axis=0)
    scores = jnp.einsum('qhd,khd->hqk', queries, key_rows, precision=FULL_PRECISION) * HEAD_DIM ** (-0.5) + bias_full
    scores = low_back(scores)
    masked = jnp.where(allowed[None], scores, NEG_FILL)
    row_peak = lax.optimization_barrier(jnp.max(masked, axis=-1, keepdims=True))
    exp_terms = jnp.exp(masked - row_peak)
    prob_low = low(exp_terms / lax.optimization_barrier(jnp.sum(exp_terms, axis=-1, keepdims=True)))
    context = jnp.einsum('hqk,khd->qhd', prob_low, value_rows, precision=FULL_PRECISION).reshape(seq_span, HEADS * HEAD_DIM)
    context = low_back(low(context))
    mid = inputs + low_back(jnp.dot(context, low(w_attn_out), precision=FULL_PRECISION))
    normed_two = low(mid * lax.rsqrt(lax.optimization_barrier(jnp.mean(mid * mid, axis=-1, keepdims=True)) + NORM_EPS) * gains[1])
    pre_act = low_back(jnp.dot(normed_two, low(w_up), precision=FULL_PRECISION))
    hidden = low(gelu_exact(pre_act))
    return mid + low_back(jnp.dot(hidden, low(w_down), precision=FULL_PRECISION))

def adamw(weight, gradient, first_mom, second, step_rate, decay_rate):
    first_new = MOMENT_DECAY * first_mom + (1.0 - MOMENT_DECAY) * gradient
    second_new = MOMENT_DECAY * second + (1.0 - MOMENT_DECAY) * gradient * gradient
    bias_fix = 1.0 - MOMENT_DECAY ** STEP
    update = first_new / bias_fix / (jnp.sqrt(second_new / bias_fix) + ADAM_EPS)
    return (weight - step_rate * (update + decay_rate * weight), first_new, second_new)

def reference(hidden_in, out_grad, seg_ids, row_len, slot_mask, mem_keys, mem_values, w_qkv, m_qkv, v_qkv, w_attn_out, m_attn_out, v_attn_out, w_up, m_up, v_up, w_down, m_down, v_down, gains, m_gains, v_gains, rel_table, m_rel, v_rel):
    weights = (w_qkv, w_attn_out, w_up, w_down, gains, rel_table)

    def one_row(totals, packed):
        inputs, cotangent, seg_row, length, pair_on, mk_row, mv_row = packed

        def forward(row_in, *params):
            return row_forward(row_in, *params, seg_row, length, pair_on, mk_row.astype(jnp.float32), mv_row.astype(jnp.float32))
        result, pullback = jax.vjp(forward, inputs.astype(jnp.float32), *weights)
        row_grads = pullback(cotangent.astype(jnp.float32))
        totals = jax.tree.map(jnp.add, totals, tuple(row_grads[1:]))
        return (totals, (result.astype(jnp.bfloat16), row_grads[0]))
    zero_grads = tuple((jnp.zeros_like(weight) for weight in weights))
    totals, (output, grad_input) = lax.scan(one_row, zero_grads, (hidden_in, out_grad, seg_ids, row_len, slot_mask, mem_keys, mem_values))
    qkv_new, qkv_first, qkv_second = adamw(w_qkv, totals[0], m_qkv, v_qkv, MATRIX_RATE, WEIGHT_DECAY)
    attn_out_new, attn_out_first, attn_out_second = adamw(w_attn_out, totals[1], m_attn_out, v_attn_out, MATRIX_RATE, WEIGHT_DECAY)
    up_new, up_first, up_second = adamw(w_up, totals[2], m_up, v_up, MATRIX_RATE, WEIGHT_DECAY)
    down_new, down_first, down_second = adamw(w_down, totals[3], m_down, v_down, MATRIX_RATE, WEIGHT_DECAY)
    gains_new, gains_first, gains_second = adamw(gains, totals[4], m_gains, v_gains, SMALL_RATE, 0.0)
    rel_new, rel_first, rel_second = adamw(rel_table, totals[5], m_rel, v_rel, SMALL_RATE, 0.0)
    return (output, grad_input, qkv_new, qkv_first, qkv_second, qkv_new.astype(jnp.bfloat16), attn_out_new, attn_out_first, attn_out_second, attn_out_new.astype(jnp.bfloat16), up_new, up_first, up_second, up_new.astype(jnp.bfloat16), down_new, down_first, down_second, down_new.astype(jnp.bfloat16), gains_new, gains_first, gains_second, rel_new, rel_first, rel_second)
```

```python
import functools

import jax
import jax.numpy as jnp
import numpy as np
from jax import lax
from jax.experimental import pallas as pl
from jax.experimental.pallas import tpu as pltpu
from jax.sharding import Mesh
from jax.sharding import PartitionSpec as P

HEAD_DIM = 64
STEP = 10


NORM_EPS = 1e-06
MOMENT_DECAY = 0.5
ADAM_EPS = 1e-08
MATRIX_RATE = 0.05
SMALL_RATE = 0.5
WEIGHT_DECAY = 0.01
FAR_BOUNDS = (12, 16, 23, 32, 46, 64, 91)
NEG_FILL = -1e30


def bucket_of(distance):
    far_dist = jnp.abs(distance)
    far_bucket = jnp.full(far_dist.shape, 8, jnp.int32)
    for far_bound in FAR_BOUNDS:
        far_bucket = far_bucket + (far_dist >= far_bound).astype(jnp.int32)
    one_side = jnp.where(far_dist < 8, far_dist, far_bucket)
    return one_side + jnp.where(distance > 0, 16, 0).astype(jnp.int32)


def gelu_exact(values):
    return jax.nn.gelu(values, approximate=False)


def rms_inverse(values):
    return lax.rsqrt(jnp.mean(values * values, axis=-1, keepdims=True) + NORM_EPS)


def norm_back(grad_out, normed_hat, inverse, gain_row):
    scaled = grad_out * gain_row
    return inverse * (scaled - normed_hat * jnp.mean(scaled * normed_hat, axis=-1, keepdims=True))


def adamw(weight, gradient, first_mom, second, step_rate, decay_rate):
    first_new = MOMENT_DECAY * first_mom + (1.0 - MOMENT_DECAY) * gradient
    second_new = MOMENT_DECAY * second + (1.0 - MOMENT_DECAY) * gradient * gradient
    bias_fix = 1.0 - MOMENT_DECAY**STEP
    update = first_new / bias_fix / (jnp.sqrt(second_new / bias_fix) + ADAM_EPS)
    return (weight - step_rate * (update + decay_rate * weight), first_new, second_new)


def row_masks(seg_row, length, pair_on):
    positions = jnp.arange(seg_row.shape[0], dtype=jnp.int32)
    is_live = positions < length
    doc_group = jnp.where(is_live, seg_row, -1).astype(jnp.int32)
    slot_on = jnp.repeat(pair_on, 2) > 0
    return (is_live[:, None] & slot_on[None, :], doc_group[:, None] == doc_group[None, :])


def block_scores(q_block, mk_row, k_row, mem_ok, tok_ok, bias_block, score_scale):
    mem_raw = (
        jnp.einsum("hqe,hke->hqk", q_block, mk_row, preferred_element_type=jnp.float32)
        * score_scale
    )
    tok_raw = (
        jnp.einsum("hqe,hke->hqk", q_block, k_row, preferred_element_type=jnp.float32) * score_scale
        + bias_block
    )
    return (jnp.where(mem_ok[None], mem_raw, NEG_FILL), jnp.where(tok_ok[None], tok_raw, NEG_FILL))


def on_device(
    hidden_in,
    out_grad,
    seg_ids,
    row_len,
    slot_mask,
    mem_keys,
    mem_values,
    w_qkv,
    m_qkv,
    v_qkv,
    w_attn_out,
    m_attn_out,
    v_attn_out,
    w_up,
    m_up,
    v_up,
    w_down,
    m_down,
    v_down,
    gains,
    m_gains,
    v_gains,
    rel_table,
    m_rel,
    v_rel,
):
    qkv_low, attn_out_low, up_low, down_low = (
        lax.all_gather(w_qkv.astype(jnp.bfloat16), "dp", axis=1, tiled=True),
        lax.all_gather(w_attn_out.astype(jnp.bfloat16), "dp", axis=1, tiled=True),
        lax.all_gather(w_up.astype(jnp.bfloat16), "dp", axis=0, tiled=True),
        lax.all_gather(w_down.astype(jnp.bfloat16), "dp", axis=1, tiled=True),
    )
    row_count = hidden_in.shape[0]
    seq_span = seg_ids.shape[1]
    bucket_total, head_total = rel_table.shape
    head_local = head_total // lax.axis_size("mp")
    head_size = HEAD_DIM
    model_width = gains.shape[1]
    slots = mem_keys.shape[1]
    score_scale = head_size ** (-0.5)
    block_rows = min(512, seq_span)
    mp_index = lax.axis_index("mp")
    positions = jnp.arange(seq_span, dtype=jnp.int32)
    bucket_grid = bucket_of(positions[None, :] - positions[:, None])
    table_local = lax.dynamic_slice_in_dim(rel_table, mp_index * head_local, head_local, 1)
    rel_bias = jnp.zeros((head_local, seq_span, seq_span), jnp.float32)
    for bucket_number in range(bucket_total):
        rel_bias = rel_bias + jnp.where(
            (bucket_grid == bucket_number)[None], table_local[bucket_number][:, None, None], 0.0
        )
    qkv_heads = qkv_low.reshape(3, model_width, head_local, head_size)
    attn_out_heads = attn_out_low.reshape(head_local, head_size, model_width)
    inputs = hidden_in.astype(jnp.float32)
    inverse_one = rms_inverse(inputs)
    hat_one = inputs * inverse_one
    normed_one = (hat_one * gains[0]).astype(jnp.bfloat16)
    normed_full = lax.all_gather(normed_one, "mp", axis=1, tiled=True)
    project = jnp.einsum(
        "rsd,cdhe->crhse", normed_full, qkv_heads, preferred_element_type=jnp.float32
    ).astype(jnp.bfloat16)
    queries, key_new, value_new = (project[0], project[1], project[2])
    mem_key_rows = jnp.transpose(
        mem_keys.reshape(row_count, slots, head_local, head_size), (0, 2, 1, 3)
    )
    mem_value_rows = jnp.transpose(
        mem_values.reshape(row_count, slots, head_local, head_size), (0, 2, 1, 3)
    )

    def forward_row(packed):
        q_row, k_row, v_row, mk_row, mv_row, seg_row, length, pair_on = packed
        mem_allowed, tok_allowed = row_masks(seg_row, length, pair_on)
        contexts = []
        maxima = []
        for first_row in range(0, seq_span, block_rows):
            last_row = first_row + block_rows
            mem_s, tok_s = block_scores(
                q_row[:, first_row:last_row],
                mk_row,
                k_row,
                mem_allowed[first_row:last_row],
                tok_allowed[first_row:last_row],
                rel_bias[:, first_row:last_row],
                score_scale,
            )
            row_peak = jnp.maximum(
                jnp.max(mem_s, axis=-1, keepdims=True), jnp.max(tok_s, axis=-1, keepdims=True)
            )
            mem_exp = jnp.exp(mem_s - row_peak)
            tok_exp = jnp.exp(tok_s - row_peak)
            exp_total = jnp.sum(mem_exp, axis=-1, keepdims=True) + jnp.sum(
                tok_exp, axis=-1, keepdims=True
            )
            mem_prob = (mem_exp / exp_total).astype(jnp.bfloat16)
            tok_prob = (tok_exp / exp_total).astype(jnp.bfloat16)
            block_context = jnp.einsum(
                "hqk,hke->hqe", mem_prob, mv_row, preferred_element_type=jnp.float32
            )
            block_context = block_context + jnp.einsum(
                "hqk,hke->hqe", tok_prob, v_row, preferred_element_type=jnp.float32
            )
            contexts.append(block_context.astype(jnp.bfloat16))
            maxima.append((row_peak + jnp.log(exp_total))[:, :, 0])
        return (jnp.concatenate(contexts, axis=1), jnp.concatenate(maxima, axis=1))

    context, log_totals = lax.map(
        forward_row,
        (queries, key_new, value_new, mem_key_rows, mem_value_rows, seg_ids, row_len, slot_mask),
    )
    attn_term = jnp.einsum(
        "rhse,hed->rsd", context, attn_out_heads, preferred_element_type=jnp.float32
    )
    attn_local = lax.psum_scatter(attn_term, "mp", scatter_dimension=1, tiled=True)
    mid = inputs + attn_local
    inverse_two = rms_inverse(mid)
    hat_two = mid * inverse_two
    normed_two = (hat_two * gains[1]).astype(jnp.bfloat16)
    ffn_source = lax.all_gather(normed_two, "mp", axis=1, tiled=True)
    up_full, down_full = (up_low, down_low)
    pre_act = jnp.einsum("rsd,df->rsf", ffn_source, up_full, preferred_element_type=jnp.float32)
    act_value, act_back = jax.vjp(gelu_exact, pre_act)
    act_low = act_value.astype(jnp.bfloat16)
    ffn_term = jnp.einsum("rsf,fd->rsd", act_low, down_full, preferred_element_type=jnp.float32)
    ffn_local = lax.psum_scatter(
        ffn_term.astype(jnp.bfloat16), "mp", scatter_dimension=1, tiled=True
    ).astype(jnp.float32)
    output = (mid + ffn_local).astype(jnp.bfloat16)
    grad_top = out_grad.astype(jnp.float32)
    grad_source = lax.all_gather(out_grad, "mp", axis=1, tiled=True)
    down_grad = jnp.einsum("rsf,rsd->fd", act_low, grad_source, preferred_element_type=jnp.float32)
    grad_act = jnp.einsum("rsd,fd->rsf", grad_source, down_full, preferred_element_type=jnp.float32)
    grad_pre = act_back(grad_act)[0].astype(jnp.bfloat16)
    up_grad = jnp.einsum("rsd,rsf->df", ffn_source, grad_pre, preferred_element_type=jnp.float32)
    grad_normed_part = jnp.einsum(
        "rsf,df->rsd", grad_pre, up_full, preferred_element_type=jnp.float32
    )
    grad_normed_two = lax.psum_scatter(grad_normed_part, "mp", scatter_dimension=1, tiled=True)
    gain_two_grad = jnp.sum(grad_normed_two * hat_two, axis=(0, 1))
    grad_mid = grad_top + norm_back(grad_normed_two, hat_two, inverse_two, gains[1])
    grad_mid_low = grad_mid.astype(jnp.bfloat16)
    grad_attn_full = lax.all_gather(grad_mid_low, "mp", axis=1, tiled=True)
    attn_out_grad = jnp.einsum(
        "rhse,rsd->hed", context, grad_attn_full, preferred_element_type=jnp.float32
    )
    attn_out_grad = attn_out_grad.reshape(head_local * head_size, model_width)
    grad_context = jnp.einsum(
        "rsd,hed->rhse", grad_attn_full, attn_out_heads, preferred_element_type=jnp.float32
    ).astype(jnp.bfloat16)

    def backward_row(bias_total, packed):
        q_row, k_row, v_row, mk_row, mv_row, seg_row, length, pair_on, lse_row, grad_row = packed
        mem_allowed, tok_allowed = row_masks(seg_row, length, pair_on)
        key_acc = jnp.zeros(k_row.shape, jnp.float32)
        value_acc = jnp.zeros(v_row.shape, jnp.float32)
        query_parts = []
        bias_parts = []
        for first_row in range(0, seq_span, block_rows):
            last_row = first_row + block_rows
            q_block = q_row[:, first_row:last_row]
            mem_s, tok_s = block_scores(
                q_block,
                mk_row,
                k_row,
                mem_allowed[first_row:last_row],
                tok_allowed[first_row:last_row],
                rel_bias[:, first_row:last_row],
                score_scale,
            )
            lse_block = lse_row[:, first_row:last_row, None]
            mem_prob = jnp.exp(mem_s - lse_block)
            tok_prob = jnp.exp(tok_s - lse_block)
            grad_block = grad_row[:, first_row:last_row]
            mem_gprob = jnp.einsum(
                "hqe,hke->hqk", grad_block, mv_row, preferred_element_type=jnp.float32
            )
            tok_gprob = jnp.einsum(
                "hqe,hke->hqk", grad_block, v_row, preferred_element_type=jnp.float32
            )
            row_dot = jnp.sum(mem_prob * mem_gprob, axis=-1, keepdims=True) + jnp.sum(
                tok_prob * tok_gprob, axis=-1, keepdims=True
            )
            mem_gscore = (mem_prob * (mem_gprob - row_dot)).astype(jnp.bfloat16)
            tok_gscore = (tok_prob * (tok_gprob - row_dot)).astype(jnp.bfloat16)
            query_grad = jnp.einsum(
                "hqk,hke->hqe", mem_gscore, mk_row, preferred_element_type=jnp.float32
            )
            query_grad = query_grad + jnp.einsum(
                "hqk,hke->hqe", tok_gscore, k_row, preferred_element_type=jnp.float32
            )
            query_parts.append((query_grad * score_scale).astype(jnp.bfloat16))
            key_acc = key_acc + jnp.einsum(
                "hqk,hqe->hke", tok_gscore, q_block, preferred_element_type=jnp.float32
            )
            value_acc = value_acc + jnp.einsum(
                "hqk,hqe->hke",
                tok_prob.astype(jnp.bfloat16),
                grad_block,
                preferred_element_type=jnp.float32,
            )
            bias_parts.append(tok_gscore.astype(jnp.float32))
        bias_total = bias_total + jnp.concatenate(bias_parts, axis=1)
        row_grads = (
            jnp.concatenate(query_parts, axis=1),
            (key_acc * score_scale).astype(jnp.bfloat16),
            value_acc.astype(jnp.bfloat16),
        )
        return (bias_total, row_grads)

    bias_grad, (grad_q, grad_k, grad_v) = lax.scan(
        backward_row,
        jnp.zeros((head_local, seq_span, seq_span), jnp.float32),
        (
            queries,
            key_new,
            value_new,
            mem_key_rows,
            mem_value_rows,
            seg_ids,
            row_len,
            slot_mask,
            log_totals,
            grad_context,
        ),
    )
    grad_project = jnp.stack([grad_q, grad_k, grad_v])
    qkv_grad = jnp.einsum(
        "rsd,crhse->cdhe", normed_full, grad_project, preferred_element_type=jnp.float32
    )
    qkv_grad = qkv_grad.reshape(3, model_width, head_local * head_size)
    grad_normed_term = jnp.einsum(
        "crhse,cdhe->rsd", grad_project, qkv_heads, preferred_element_type=jnp.float32
    )
    grad_normed_one = lax.psum_scatter(
        grad_normed_term.astype(jnp.bfloat16), "mp", scatter_dimension=1, tiled=True
    ).astype(jnp.float32)
    gain_one_grad = jnp.sum(grad_normed_one * hat_one, axis=(0, 1))
    grad_input = grad_mid + norm_back(grad_normed_one, hat_one, inverse_one, gains[0])
    bucket_sums = []
    for bucket_number in range(bucket_total):
        bucket_sums.append(
            jnp.sum(jnp.where((bucket_grid == bucket_number)[None], bias_grad, 0.0), axis=(1, 2))
        )
    table_local_grad = jnp.stack(bucket_sums)
    table_grad = lax.dynamic_update_slice(
        jnp.zeros((bucket_total, head_total), jnp.float32),
        table_local_grad,
        (jnp.int32(0), mp_index * head_local),
    )
    gains_grad, table_grad = lax.psum(
        (jnp.stack([gain_one_grad, gain_two_grad]), table_grad), ("dp", "mp")
    )
    qkv_sum, attn_out_sum, up_sum, down_sum = (
        lax.psum_scatter(qkv_grad, "dp", scatter_dimension=1, tiled=True),
        lax.psum_scatter(attn_out_grad, "dp", scatter_dimension=1, tiled=True),
        lax.psum_scatter(up_grad, "dp", scatter_dimension=0, tiled=True),
        lax.psum_scatter(down_grad, "dp", scatter_dimension=1, tiled=True),
    )
    qkv_new, qkv_first, qkv_second = adamw(w_qkv, qkv_sum, m_qkv, v_qkv, MATRIX_RATE, WEIGHT_DECAY)
    attn_out_new, attn_out_first, attn_out_second = adamw(
        w_attn_out, attn_out_sum, m_attn_out, v_attn_out, MATRIX_RATE, WEIGHT_DECAY
    )
    up_new, up_first, up_second = adamw(w_up, up_sum, m_up, v_up, MATRIX_RATE, WEIGHT_DECAY)
    down_new, down_first, down_second = adamw(
        w_down, down_sum, m_down, v_down, MATRIX_RATE, WEIGHT_DECAY
    )
    gains_new, gains_first, gains_second = adamw(
        gains, gains_grad, m_gains, v_gains, SMALL_RATE, 0.0
    )
    rel_new, rel_first, rel_second = adamw(rel_table, table_grad, m_rel, v_rel, SMALL_RATE, 0.0)
    return (
        output,
        grad_input,
        qkv_new,
        qkv_first,
        qkv_second,
        qkv_new.astype(jnp.bfloat16),
        attn_out_new,
        attn_out_first,
        attn_out_second,
        attn_out_new.astype(jnp.bfloat16),
        up_new,
        up_first,
        up_second,
        up_new.astype(jnp.bfloat16),
        down_new,
        down_first,
        down_second,
        down_new.astype(jnp.bfloat16),
        gains_new,
        gains_first,
        gains_second,
        rel_new,
        rel_first,
        rel_second,
    )


BF = jnp.bfloat16
F32 = jnp.float32
MESH_ID = pl.DeviceIdType.MESH
BIG = 1e30
KEY_PAD = 128
WIDE = 256
SQRT_HALF = 0.5**0.5
INV_SQRT_2PI = 0.3989422804014327
LINK_SEMS = 160
VMEM_LIMIT = 63 * 2**20


def dot(a, b):
    return lax.dot_general(a, b, (((1,), (0,)), ((), ())), preferred_element_type=F32)


def dot_t(a, b):
    return lax.dot_general(a, b, (((1,), (1,)), ((), ())), preferred_element_type=F32)


def split3(v):
    hi = v.astype(BF)
    rest = v - hi.astype(F32)
    mid = rest.astype(BF)
    low = (rest - mid.astype(F32)).astype(BF)
    return hi, mid, low


class Links:
    def __init__(self, send_sems, recv_sems):
        self.send_sems, self.recv_sems = send_sems, recv_sems
        self.count = 0
        self.sent = []

    def send(self, src, dst, device):
        k = self.count
        self.count += 1
        copy = pltpu.make_async_remote_copy(
            src, dst, self.send_sems.at[k], self.recv_sems.at[k], device_id=device, device_id_type=MESH_ID
        )
        copy.start()
        self.sent.append(copy)
        return k

    def send_or_keep(self, src, dst, device, is_self, send_at, recv_at):
        copy = pltpu.make_async_remote_copy(
            src, dst, self.send_sems.at[send_at], self.recv_sems.at[recv_at], device_id=device, device_id_type=MESH_ID
        )

        @pl.when(is_self)
        def _():
            pltpu.make_async_copy(src, dst, self.recv_sems.at[recv_at]).start()

        @pl.when(jnp.logical_not(is_self))
        def _():
            copy.start()

        self.sent.append((copy, is_self))

    def send_unless(self, src, dst, device, is_self, send_at, recv_at):
        copy = pltpu.make_async_remote_copy(
            src, dst, self.send_sems.at[send_at], self.recv_sems.at[recv_at], device_id=device, device_id_type=MESH_ID
        )

        @pl.when(jnp.logical_not(is_self))
        def _():
            copy.start()

        self.sent.append((copy, is_self))

    def arrived(self, dst, k):
        pltpu.make_async_copy(dst, dst, self.recv_sems.at[k]).wait()

    def drain(self):
        for item in self.sent:
            if isinstance(item, tuple):
                copy, is_self = item

                @pl.when(jnp.logical_not(is_self))
                def _(copy=copy):
                    copy.wait_send()

            else:
                item.wait_send()
        self.sent = []


class Place:
    def __init__(self):
        self.y, self.x = lax.axis_index("y"), lax.axis_index("x")
        self.c, self.z = lax.axis_index("c"), lax.axis_index("z")
        self.to_x, self.to_y = {"x": 1 - self.x}, {"y": 1 - self.y}
        self.to_c = {"c": 1 - self.c}

    def to_z(self, k):
        return {"z": lax.rem(self.z + k, 4)}

    def from_z(self, k):
        return lax.rem(self.z + 4 - k, 4)

    def greet(self):
        barrier = pltpu.get_barrier_semaphore()
        peers = [self.to_x, self.to_y, self.to_c]
        for k in (1, 2, 3):
            peers.append(self.to_z(k))
            peers.append({"z": lax.rem(self.z + k, 4), "c": 1 - self.c})
        for peer in peers:
            pl.semaphore_signal(barrier, inc=1, device_id=peer, device_id_type=MESH_ID)
        pl.semaphore_wait(barrier, len(peers))


class Gather:
    def __init__(self, place, links, shard, whole, local_sem):
        self.p, self.links, self.shard, self.whole, self.local_sem = place, links, shard, whole, local_sem

    @staticmethod
    def rows(y, x, c):
        return y * 4 + x * 2 + c

    def start_z(self):
        p, links = self.p, self.links
        own = self.whole.at[p.z, self.rows(p.y, p.x, p.c)]
        self.own_copy = pltpu.make_async_copy(self.shard, own, self.local_sem)
        self.own_copy.start()
        self.k_z = {k: links.send(self.shard, own, p.to_z(k)) for k in (2, 1, 3)}

    def start_xy(self):
        p, links = self.p, self.links
        own = self.whole.at[p.z, self.rows(p.y, p.x, p.c)]
        self.k_x = {0: links.send(self.shard, own, p.to_x)}
        self.k_y = {0: links.send(self.shard, own, p.to_y)}

    def column(self):
        p, links = self.p, self.links
        for k in (1, 3, 2):
            block = self.whole.at[p.from_z(k), self.rows(p.y, p.x, p.c)]
            links.arrived(block, self.k_z[k])
            self.k_x[k] = links.send(block, block, p.to_x)
            self.k_y[k] = links.send(block, block, p.to_y)
        self.own_copy.wait()
        block = self.whole.at[:, self.rows(p.y, p.x, p.c)]
        self.k_c = [links.send(block, block, p.to_c)]

    def plane(self):
        p, links = self.p, self.links
        self.k_d = {}
        for k in (0, 1):
            block = self.whole.at[p.from_z(k), self.rows(p.y, 1 - p.x, p.c)]
            links.arrived(block, self.k_x[k])
            self.k_d[k] = links.send(block, block, p.to_y)
        for k in (3, 2):
            block = self.whole.at[p.from_z(k), self.rows(1 - p.y, p.x, p.c)]
            links.arrived(block, self.k_y[k])
            self.k_d[k] = links.send(block, block, p.to_x)
        for k in (3, 2):
            links.arrived(self.whole.at[p.from_z(k), self.rows(p.y, 1 - p.x, p.c)], self.k_x[k])
        for k in (0, 1):
            links.arrived(self.whole.at[p.from_z(k), self.rows(1 - p.y, p.x, p.c)], self.k_y[k])
        for y, x in ((p.y, 1 - p.x), (1 - p.y, p.x)):
            block = self.whole.at[:, self.rows(y, x, p.c)]
            self.k_c.append(links.send(block, block, p.to_c))

    def corner(self):
        p, links = self.p, self.links
        for k in (0, 1, 3, 2):
            links.arrived(self.whole.at[p.from_z(k), self.rows(1 - p.y, 1 - p.x, p.c)], self.k_d[k])
        block = self.whole.at[:, self.rows(1 - p.y, 1 - p.x, p.c)]
        self.k_c.append(links.send(block, block, p.to_c))

    def finish(self):
        p = self.p
        spots = ((p.y, p.x), (p.y, 1 - p.x), (1 - p.y, p.x), (1 - p.y, 1 - p.x))
        for (y, x), k in zip(spots, self.k_c):
            self.links.arrived(self.whole.at[:, self.rows(y, x, 1 - p.c)], k)


class Reduce:
    def __init__(self, place, links, grads, land):
        self.p, self.links, self.g, self.land = place, links, grads, land
        self.k_c, self.k_first, self.k_second = {}, {}, {}
        self.at_z = links.count
        links.count += 4

    def start(self, q):
        p = self.p
        spot = self.land.at[q // 2, pl.ds(q % 2 * 4, 4)]
        self.k_c[q] = self.links.send(self.g.at[q, :, 1 - p.c], spot, p.to_c)

    def add(self, q, n, row, col):
        at = (q, n, self.p.c)
        self.g[at] = (self.g[at].astype(F32) + self.land[row, col].astype(F32)).astype(BF)

    def core(self, q):
        p, links = self.p, self.links
        links.arrived(self.land.at[q // 2, pl.ds(q % 2 * 4, 4)], self.k_c[q])
        for n in range(4):
            self.add(q, n, q // 2, q % 2 * 4 + n)
        self.k_first[q] = []
        for i in (0, 1):
            n, peer = (2 * i + 1 - p.x, p.to_x) if q < 2 else (2 * (1 - p.y) + i, p.to_y)
            self.k_first[q].append(links.send(self.g.at[q, n, p.c], self.land.at[2, 2 * q + i], peer))

    def plane(self, q):
        p, links = self.p, self.links
        for i in (0, 1):
            links.arrived(self.land.at[2, 2 * q + i], self.k_first[q][i])
            self.add(q, 2 * i + p.x if q < 2 else 2 * p.y + i, 2, 2 * q + i)
        n, peer = (2 * (1 - p.y) + p.x, p.to_y) if q < 2 else (2 * p.y + 1 - p.x, p.to_x)
        self.k_second[q] = links.send(self.g.at[q, n, p.c], self.land.at[3, q], peer)

    def column(self, q):
        p, links = self.p, self.links
        here = 2 * p.y + p.x
        links.arrived(self.land.at[3, q], self.k_second[q])
        self.add(q, here, 3, q)
        links.send_unless(
            self.g.at[q, here, p.c], self.land.at[3, 4 + p.z], {"z": q}, p.z == q, self.at_z + q, self.at_z + p.z
        )

    def finish(self, out):
        p = self.p
        total = self.g[p.z, 2 * p.y + p.x, p.c].astype(F32)
        for k in (1, 2, 3):
            source = p.from_z(k)
            self.links.arrived(self.land.at[3, 4 + source], self.at_z + source)
            total = total + self.land[3, 4 + source].astype(F32)
        out[...] = total


def band_tiles(group, chunk):
    tiles = []
    for i in range(2):
        for j in range(2):
            block = 2 * group + j
            if chunk < 2:
                apart = 2 * chunk + i - block
                if abs(apart) <= 1:
                    tiles.append((i, j, apart + 1, None))
            else:
                other = 2 * (chunk - 2) + i
                if block == 3 and other == 0:
                    tiles.append((i, j, 2, 0))
                if block == 0 and other == 3:
                    tiles.append((i, j, 0, 1))
    return tiles


def add_band(s, band, group, chunk, core):
    tiles = band_tiles(group, chunk)
    if not tiles:
        return s
    rows = []
    for i in range(2):
        cols = []
        for j in range(2):
            part = s[i * 128 : (i + 1) * 128, j * 128 : (j + 1) * 128]
            for a, b, third, need in tiles:
                if (a, b) == (i, j):
                    near = band[third * 128 : (third + 1) * 128, :]
                    if need is not None:
                        near = near * jnp.where(core == need, 1.0, 0.0)
                    part = part + near
            cols.append(part)
        rows.append(jnp.concatenate(cols, axis=1))
    return jnp.concatenate(rows, axis=0)


def far_masks(core, span):
    key = lax.broadcasted_iota(jnp.int32, (8, span), 0)
    block = lax.broadcasted_iota(jnp.int32, (8, span), 1) // 128
    other = key - 4
    left = ((key < 4) & (key <= block - 2)) | ((key >= 4) & (core == 1) & ~((block == 0) & (other == 3)))
    right = ((key < 4) & (key >= block + 2)) | ((key >= 4) & (core == 0) & ~((block == 3) & (other == 0)))
    return left, right


def rows_of(parts, span):
    row = lax.broadcasted_iota(jnp.int32, (8, span), 0)
    out = jnp.zeros((8, span), F32)
    for n, part in enumerate(parts):
        out = jnp.where(row == n, part.astype(F32), out)
    return out.astype(BF)


def far_rows(left, right, far_left, far_right):
    hi, mid, low = split3(jnp.where(left, far_left, jnp.where(right, far_right, 0.0)))
    return jnp.concatenate([hi.astype(F32), mid.astype(F32), low.astype(F32)], axis=0).astype(BF)


def fwd_head(R, h, core, far_left, far_right):
    span, keys = R.QT.shape[2], R.KVT.shape[2]
    toks = keys - KEY_PAD
    R.ka[0:64, :] = R.KVT[h, 0:64, :]
    R.Ka[...] = R.ka[...].T
    R.va[0:64, :] = R.KVT[h, 64:128, :]
    R.qa[0:64, :] = R.QT[h]
    left, right = far_masks(core, span)
    R.qa[80:104, :] = far_rows(left, right, far_left, far_right)
    R.band[...] = band_of(R.wave[pl.ds(h, 1), :])
    band = R.band
    chunks = [(n, slice(n * WIDE, (n + 1) * WIDE)) for n in range(toks // WIDE)]
    last = slice(toks, toks + 32)
    for group in range(span // WIDE):
        cols = slice(group * WIDE, (group + 1) * WIDE)
        query = R.qa[:, cols]
        peak = None
        for n, rows in chunks:
            s = add_band(dot(R.Ka[rows, :], query), band, group, n, core)
            R.S[rows, :] = s
            top = jnp.max(s, axis=0, keepdims=True)
            peak = top if peak is None else jnp.maximum(peak, top)
        s = dot(R.Ka[last, :], query)
        R.S[last, :] = s
        peak = jnp.maximum(peak, jnp.max(s, axis=0, keepdims=True))
        for _, rows in chunks:
            R.P[rows, :] = jnp.exp(R.S[rows, :] - peak).astype(BF)
        R.P[last, :] = jnp.exp(R.S[last, :] - peak).astype(BF)
        o = dot(R.va[0:72, :], R.P[...])
        total = o[64:65, :]
        R.ctxT[h, :, cols] = (o[0:64, :] * (1.0 / total)).astype(BF)
        R.lse[pl.ds(h, 1), cols] = peak + jnp.log(total)


def bwd_head(R, h, j, core, far_left, far_right):
    span, keys = R.QT.shape[2], R.KVT.shape[2]
    toks = keys - KEY_PAD
    R.ka[0:64, :] = R.KVT[h, 0:64, :]
    R.Ka[...] = R.ka[...].T
    R.va[0:64, :] = R.KVT[h, 64:128, :]
    R.Va[...] = R.va[...].T
    R.qa[0:64, :] = R.QT[h]
    left, right = far_masks(core, span)
    R.qa[80:104, :] = far_rows(left, right, far_left, far_right)
    R.qa[72:80, :] = rows_of(split3(-R.lse[pl.ds(h, 1), :]), span)
    grad = R.dOT[h]
    R.da[0:64, :] = grad
    row_dot = jnp.sum(grad.astype(F32) * R.ctxT[h].astype(F32), axis=0, keepdims=True)
    R.da[64:72, :] = rows_of(split3(-row_dot), span)
    R.band[...] = band_of(R.wave[pl.ds(h, 1), :])
    band = R.band
    groups = span // WIDE
    query_sum = [None] * groups
    near = [None, None, None]
    for n in range(toks // WIDE + 1):
        is_mem = n * WIDE == toks
        rows = slice(toks, toks + 32) if is_mem else slice(n * WIDE, (n + 1) * WIDE)
        key_sum = value_sum = None
        for group in range(groups):
            cols = slice(group * WIDE, (group + 1) * WIDE)
            s = dot(R.Ka[rows, :], R.qa[:, cols])
            if not is_mem:
                s = add_band(s, band, group, n, core)
            p = jnp.exp(s)
            ds = p * dot(R.Va[rows, :], R.da[:, cols])
            ds_low = ds.astype(BF)
            if is_mem:
                filled = jnp.concatenate([ds_low, jnp.zeros((KEY_PAD - 32, WIDE), BF)], axis=0)
                part = dot(R.ka[0:96, toks:keys], filled)
            else:
                v = dot_t(p.astype(BF), R.da[0:64, cols])
                k = dot_t(ds_low, R.qa[0:64, cols])
                value_sum = v if value_sum is None else value_sum + v
                key_sum = k if key_sum is None else key_sum + k
                for a, b, third, need in band_tiles(group, n):
                    t = ds[a * 128 : (a + 1) * 128, b * 128 : (b + 1) * 128]
                    if need is not None:
                        t = t * jnp.where(core == need, 1.0, 0.0)
                    near[third] = t if near[third] is None else near[third] + t
                part = dot(R.ka[0:96, rows], ds_low)
            query_sum[group] = part if query_sum[group] is None else query_sum[group] + part
        if not is_mem:
            both = jnp.concatenate([key_sum, value_sum], axis=1)
            if n * WIDE < span:
                R.kv_own[j, rows, :] = both
            else:
                R.kv_out[h, slice(n * WIDE - span, (n + 1) * WIDE - span), :] = both.astype(BF)
    turned = jnp.concatenate(query_sum, axis=1)
    R.dq[j] = (turned[0:64, :] * HEAD_DIM**-0.5).T.astype(BF)
    far = turned[80:88, :]
    lane = lax.broadcasted_iota(jnp.int32, (1, 128), 1)
    sum_left = jnp.sum(jnp.where(left, far, 0.0))
    sum_right = jnp.sum(jnp.where(right, far, 0.0))
    ends = jnp.where(lane == 0, sum_left, jnp.where(lane == 1, sum_right, 0.0))
    R.small[pl.ds(8 + h, 1), 0:640] = jnp.concatenate([unband(jnp.concatenate(near, axis=0)), ends], axis=1)


class Refs:
    def __init__(self, **refs):
        self.__dict__.update(refs)


def weights(R, n, z, cols):
    part = R.W[n, z, :, :, cols]
    return part.reshape(part.shape[0] * part.shape[1], part.shape[2])


class RowMove:
    def __init__(self, place, links, src, dst):
        self.links, self.dst = links, dst
        slot = lax.rem(place.z, 2)
        at = links.count
        links.count += 2
        for i in (0, 1):
            target_z, target_c = 2 * place.c + i, place.z // 2
            links.send_or_keep(
                src.at[i],
                dst.at[slot],
                {"c": target_c, "z": target_z},
                (target_c == place.c) & (target_z == place.z),
                at + i,
                at + slot,
            )
        self.at = at

    def wait(self, slot):
        self.links.arrived(self.dst.at[slot], self.at + slot)


def norm_parts(values):
    inverse = lax.rsqrt(jnp.mean(values * values, axis=-1, keepdims=True) + NORM_EPS)
    return inverse, values * inverse


def mask_rows(R, place):
    span, keys = R.QT.shape[2], R.KVT.shape[2]
    toks = keys - KEY_PAD
    mine = jnp.where(place.z // 2 == place.c, R.code[lax.rem(place.z, 2)], R.code_in[...])
    R.code_in[...] = mine
    own = R.code_in[:, pl.ds(pl.multiple_of(place.c * span, span), span)]
    other = R.code_in[:, pl.ds(pl.multiple_of((1 - place.c) * span, span), span)]
    line = jnp.concatenate([own, other, R.code_in[:, toks:keys]], axis=1)
    row = lax.broadcasted_iota(jnp.int32, (8, keys), 0)
    as_doc = (row - 1).astype(F32)
    kind = jnp.where(row < 5, jnp.where(line == as_doc, 1.0, 0.0), 0.0)
    kind = jnp.where((row == 5) & (line == 11.0), 1.0, kind)
    kind = jnp.where((row == 6) & (line >= 10.0), 1.0, kind)
    R.ka[64:72, :] = kind.astype(BF)
    R.ka[72:80, :] = jnp.where(row < 3, 1.0, 0.0).astype(BF)
    block = lax.broadcasted_iota(jnp.int32, (8, keys), 1) // 128
    hot = jnp.where((block == row) & (block < toks // 128), 1.0, 0.0)
    R.ka[80:104, :] = jnp.concatenate([hot, hot, hot], axis=0).astype(BF)
    R.ka[104:128, :] = jnp.zeros((24, keys), BF)
    R.va[64:72, :] = jnp.where(row < 3, 1.0, 0.0).astype(BF)
    R.va[72:128, :] = jnp.zeros((56, keys), BF)
    qrow = lax.broadcasted_iota(jnp.int32, (8, span), 0)
    hide = jnp.where((qrow < 5) & (own != (qrow - 1).astype(F32)), -BIG, 0.0)
    hide = jnp.where(qrow == 5, -BIG, hide)
    hide = jnp.where((qrow == 6) & (own == -1.0), -BIG, hide)
    R.qa[64:72, :] = hide.astype(BF)
    R.qa[72:128, :] = jnp.zeros((56, span), BF)
    R.da[64:128, :] = jnp.zeros((64, span), BF)
    R.P[toks + 32 : keys, :] = jnp.zeros((KEY_PAD - 32, WIDE), BF)


def band_of(wave):
    spread = jnp.broadcast_to(wave, (128, 512))
    parts = [pltpu.roll(spread, 128 * n, 1, stride=1, stride_axis=0)[:, 0:128] for n in range(3)]
    return jnp.concatenate(parts, axis=0)


def unband(near):
    empty = jnp.zeros((8, 128), F32)
    total = None
    for n in range(16):
        part = jnp.concatenate(
            [near[8 * n : 8 * n + 8], empty, near[256 + 8 * n : 264 + 8 * n], near[128 + 8 * n : 136 + 8 * n]], axis=1
        )
        if n:
            part = pltpu.roll(part, 512 - 8 * n, 1)
        total = part if total is None else total + part
    row = lax.broadcasted_iota(jnp.int32, (8, 512), 0)
    out = jnp.zeros((8, 512), F32)
    for n in range(8):
        out = out + jnp.where(row == n, total if n == 0 else pltpu.roll(total, 512 - n, 1), 0.0)
    return jnp.sum(out, axis=0, keepdims=True)


def layer_kernel(names, *refs):
    R = Refs(**dict(zip(names, refs)))
    place = Place()
    links = Links(R.send_sems, R.recv_sems)
    place.greet()
    heads, span = R.QT.shape[0], R.QT.shape[2]
    width = R.xin.shape[2]
    group = heads // 4
    kv_cols, q_cols = group * 128, group * HEAD_DIM
    qkv_cols = kv_cols + q_cols
    slots = R.xin.shape[0]
    piece = R.xin.shape[1]

    gather = [Gather(place, links, R.packed.at[n], R.W.at[n], R.local_sems.at[n]) for n in range(3)]
    gather[0].start_z()
    move_in = RowMove(place, links, R.hidden, R.xin)
    gather[0].start_xy()
    k_code = links.send(R.code.at[lax.rem(place.z, 2)], R.code_in, place.to_c)
    at_mem = links.count
    links.count += 4
    mem_spot = R.KVT.at[pl.ds(group * place.z, group), :, 2 * span : 2 * span + KEY_PAD]
    for r in (0, 1):
        for c in (0, 1):
            links.send_or_keep(
                R.mem.at[r],
                mem_spot,
                {"c": c, "z": 2 * place.c + r},
                (place.c == c) & (place.z == 2 * place.c + r),
                at_mem + 2 * r + c,
                at_mem + place.z,
            )
    gather[0].column()
    gather[1].start_z()
    gather[1].start_xy()

    for s in range(slots):
        move_in.wait(s)
        _, hat = norm_parts(R.xin[s].astype(F32))
        R.na[s * piece : (s + 1) * piece, :] = (hat * R.gains[0:1, :]).astype(BF)
    links.arrived(R.code_in, k_code)
    mask_rows(R, place)
    gather[0].plane()
    gather[1].column()
    gather[0].corner()
    gather[0].finish()

    k_kv = []
    for z in range(4):
        low = dot(R.na[...], weights(R, 0, z, slice(0, qkv_cols))).astype(BF)
        for j in range(group):
            R.KVT[group * z + j, :, 0:span] = low[:, j * 128 : (j + 1) * 128].T
        turned = (low[:, kv_cols:qkv_cols].astype(F32) * HEAD_DIM**-0.5).astype(BF).T
        for j in range(group):
            R.QT[group * z + j] = turned[j * HEAD_DIM : (j + 1) * HEAD_DIM, :]
        block = pl.ds(group * z, group)
        k_kv.append(links.send(R.KVT.at[block, :, 0:span], R.KVT.at[block, :, span : 2 * span], place.to_c))

    gather[2].start_z()
    gather[2].start_xy()
    move_grad = RowMove(place, links, R.out_grad, R.gin)
    gather[1].plane()

    for z in range(4):
        block = pl.ds(group * z, group)
        links.arrived(R.KVT.at[block, :, span : 2 * span], k_kv[z])
        links.arrived(R.KVT.at[block, :, 2 * span : 2 * span + KEY_PAD], at_mem + z)

        @pl.loop(group * z, group * (z + 1))
        def _(h):
            fwd_head(R, h, place.c, R.table[15, h], R.table[31, h])

        if z == 0:
            gather[2].column()
            gather[1].corner()
        elif z == 1:
            gather[2].plane()
        elif z == 2:
            gather[2].corner()
    gather[1].finish()

    for s in range(slots):
        rows = slice(s * piece, (s + 1) * piece)
        total = R.xin[s].astype(F32)
        for z in range(4):
            ctx = R.ctxT[group * z : group * (z + 1), :, rows].reshape(q_cols, piece).T
            total = total + dot_t(ctx, weights(R, 0, z, slice(qkv_cols, width)))
        R.mid[rows, :] = total
        _, hat = norm_parts(total)
        R.na[rows, :] = (hat * R.gains[1:2, :]).astype(BF)
    R.nT[...] = R.na[...].T
    gather[2].finish()
    for s in range(slots):
        move_grad.wait(s)
        R.gT[:, s * piece : (s + 1) * piece] = R.gin[s].T

    R.acc[...] = jnp.zeros_like(R.acc)
    R.gacc[...] = jnp.zeros_like(R.gacc)

    @pl.loop(0, 4)
    def _(z):
        for n in range(width // WIDE):
            cols = slice(n * WIDE, (n + 1) * WIDE)
            pre = dot(R.na[...], weights(R, 1, z, cols))
            phi = 0.5 + 0.5 * lax.erf(pre * SQRT_HALF)
            R.act[:, cols] = (pre * phi).astype(BF)
            slope = phi + pre * (jnp.exp(-0.5 * pre * pre) * INV_SQRT_2PI)
            back = dot(R.gin[...].reshape(span, width), weights(R, 2, z, cols))
            R.gp[:, cols] = (back * slope).astype(BF)
        R.acc[...] += dot_t(R.act[...], weights(R, 2, z, slice(0, width)))
        R.gacc[...] += dot_t(R.gp[...], weights(R, 1, z, slice(0, width)))
        R.G[2, z] = dot(R.gT[...], R.act[...]).astype(BF).reshape(4, 2, width // 8, width)
        R.G[1, z] = dot(R.nT[...], R.gp[...]).astype(BF).reshape(4, 2, width // 8, width)

    links.drain()
    for peer in (place.to_x, place.to_y, place.to_c, place.to_z(1), place.to_z(2), place.to_z(3)):
        pl.semaphore_signal(R.ready, inc=1, device_id=peer, device_id_type=MESH_ID)
    gain_two = jnp.zeros((1, width), F32)
    for s in range(slots):
        rows = slice(s * piece, (s + 1) * piece)
        mid = R.mid[rows, :]
        R.ob[s] = (mid + R.acc[rows, :]).astype(BF)
        inverse, hat = norm_parts(mid)
        grad = R.gacc[rows, :]
        gain_two = gain_two + jnp.sum(grad * hat, axis=0, keepdims=True)
        scaled = grad * R.gains[1:2, :]
        shift = hat * jnp.mean(scaled * hat, axis=-1, keepdims=True)
        top = R.gin[s].astype(F32) + inverse * (scaled - shift)
        R.mid[rows, :] = top
        R.na[rows, :] = top.astype(BF)
    R.small[...] = jnp.zeros_like(R.small)
    R.small[1:2, :] = gain_two
    move_out = RowMove(place, links, R.ob, R.output)
    R.gT[...] = R.na[...].T
    pl.semaphore_wait(R.ready, 6)
    up_sum = Reduce(place, links, R.G.at[1], R.W.at[1])
    down_sum = Reduce(place, links, R.G.at[2], R.W.at[2])
    qkv_sum = Reduce(place, links, R.G.at[0], R.land)
    for q in range(4):
        up_sum.start(q)
    for z in range(4):
        ctx = R.ctxT[group * z : group * (z + 1)].reshape(q_cols, span)
        part = dot_t(R.gT[...], ctx).astype(BF)
        R.G[0, z, :, :, :, qkv_cols:] = part.reshape(4, 2, width // 8, q_cols)
        turned = dot(R.na[...], weights(R, 0, z, slice(qkv_cols, width))).astype(BF).T
        for j in range(group):
            R.dOT[group * z + j] = turned[j * HEAD_DIM : (j + 1) * HEAD_DIM, :]
    for s in range(slots):
        _, hat = norm_parts(R.xin[s].astype(F32))
        R.nT[:, s * piece : (s + 1) * piece] = (hat * R.gains[0:1, :]).astype(BF).T
    R.gacc[...] = jnp.zeros_like(R.gacc)
    for q in range(4):
        up_sum.core(q)
    for q in range(4):
        down_sum.start(q)

    def project_back(z):
        links.arrived(R.kv_in.at[pl.ds(group * z, group)], k_back[z])
        parts = []
        for j in range(group):
            whole = R.kv_own[group * (z % 2) + j] + R.kv_in[group * z + j].astype(F32)
            parts.append(whole.astype(BF))
        for j in range(group):
            parts.append(R.dq[group * (z % 2) + j])
        grads = jnp.concatenate(parts, axis=1)
        made = dot(R.nT[...], grads).astype(BF)
        R.G[0, z, :, :, :, 0:qkv_cols] = made.reshape(4, 2, width // 8, qkv_cols)
        qkv_sum.start(z)
        R.gacc[...] += dot_t(grads, weights(R, 0, z, slice(0, qkv_cols)))

    k_back = []
    for z in range(4):
        block = pl.ds(group * z, group)

        @pl.loop(0, group)
        def _(j):
            h = group * z + j
            bwd_head(R, h, group * (z % 2) + j, place.c, R.table[15, h], R.table[31, h])

        k_back.append(links.send(R.kv_out.at[block], R.kv_in.at[block], place.to_c))
        if z > 0:
            project_back(z - 1)
        if z == 0:
            for q in range(4):
                up_sum.plane(q)
            for q in range(4):
                down_sum.core(q)
        elif z == 1:
            for q in range(4):
                up_sum.column(q)
            for q in range(4):
                down_sum.plane(q)
            qkv_sum.core(0)
        elif z == 2:
            up_sum.finish(R.gsum.at[1])
            for q in range(4):
                down_sum.column(q)
            qkv_sum.plane(0)
            qkv_sum.core(1)
        else:
            down_sum.finish(R.gsum.at[2])
            qkv_sum.column(0)
            qkv_sum.plane(1)
            qkv_sum.core(2)
    project_back(3)
    gain_one = jnp.zeros((1, width), F32)
    for s in range(slots):
        rows = slice(s * piece, (s + 1) * piece)
        inverse, hat = norm_parts(R.xin[s].astype(F32))
        grad = R.gacc[rows, :]
        gain_one = gain_one + jnp.sum(grad * hat, axis=0, keepdims=True)
        scaled = grad * R.gains[0:1, :]
        shift = hat * jnp.mean(scaled * hat, axis=-1, keepdims=True)
        R.gin[s] = (R.mid[rows, :] + inverse * (scaled - shift)).astype(BF)
    move_back = RowMove(place, links, R.gin, R.grad_in)
    R.small[0:1, :] = gain_one

    k = links.send(R.small, R.small_in.at[0], place.to_c)
    qkv_sum.core(3)
    qkv_sum.column(1)
    qkv_sum.plane(2)
    links.arrived(R.small_in.at[0], k)
    R.small_in[0] = R.small_in[0] + R.small[...]
    k = links.send(R.small_in.at[0], R.small_in.at[1], place.to_x)
    qkv_sum.plane(3)
    links.arrived(R.small_in.at[1], k)
    R.small_in[1] = R.small_in[1] + R.small_in[0]
    k = links.send(R.small_in.at[1], R.small_in.at[2], place.to_y)
    qkv_sum.column(2)
    links.arrived(R.small_in.at[2], k)
    R.small_z[place.z] = R.small_in[2] + R.small_in[1]
    own = R.small_z.at[place.z]
    k_small = {k: links.send(own, own, place.to_z(k)) for k in (1, 2, 3)}
    qkv_sum.column(3)
    for k in (1, 2, 3):
        links.arrived(R.small_z.at[place.from_z(k)], k_small[k])
    R.small_sum[...] = (R.small_z[0] + R.small_z[1]) + (R.small_z[2] + R.small_z[3])
    qkv_sum.finish(R.gsum.at[0])
    for s in range(slots):
        move_out.wait(s)
        move_back.wait(s)
    links.drain()


def wave_buckets():
    lane = np.arange(512)
    apart = np.where(lane < 128, -lane - 128, 384 - lane)
    far = np.abs(apart)
    bucket = np.where(far < 8, far, 8 + sum((far >= bound).astype(np.int32) for bound in FAR_BOUNDS))
    return bucket + np.where(apart > 0, 16, 0)


def on_moved(
    hidden_in,
    out_grad,
    seg_ids,
    row_len,
    slot_mask,
    mem_keys,
    mem_values,
    w_qkv,
    m_qkv,
    v_qkv,
    w_attn_out,
    m_attn_out,
    v_attn_out,
    w_up,
    m_up,
    v_up,
    w_down,
    m_down,
    v_down,
    gains,
    m_gains,
    v_gains,
    rel_table,
    m_rel,
    v_rel,
):
    rows, piece, width = hidden_in.shape
    seq = seg_ids.shape[1]
    span = seq // 2
    slots = mem_keys.shape[1]
    buckets, heads = rel_table.shape
    group = heads // 4
    shard = w_qkv.shape[1]
    live = jnp.arange(seq, dtype=jnp.int32)[None, :] < row_len[:, None]
    docs = jnp.where(live, seg_ids, -1)
    on = jnp.where(jnp.repeat(slot_mask, 2, axis=1) > 0, 10, 11)
    code = jnp.concatenate([docs, on, jnp.full((rows, KEY_PAD - slots), 11, jnp.int32)], axis=1)
    code = jnp.broadcast_to(code[:, None, :].astype(F32), (rows, 8, seq + KEY_PAD))

    def turned(mem):
        return jnp.transpose(mem.reshape(rows, slots, group, HEAD_DIM), (0, 2, 3, 1))

    mem = jnp.concatenate([turned(mem_keys), turned(mem_values)], axis=2)
    mem = jnp.pad(mem, ((0, 0), (0, 0), (0, 0), (0, KEY_PAD - slots)))
    w_low = w_qkv.astype(BF).reshape(3, shard, group, HEAD_DIM)
    first = jnp.concatenate(
        [
            jnp.concatenate([w_low[1], w_low[2]], axis=2).reshape(shard, group * 128),
            w_low[0].reshape(shard, group * HEAD_DIM),
            w_attn_out.astype(BF).T,
        ],
        axis=1,
    )
    packed = jnp.stack([first, w_up.astype(BF), w_down.astype(BF).T])
    hot = jnp.asarray(wave_buckets()[:, None] == np.arange(buckets)[None, :], F32)
    wave = jnp.einsum("bh,mb->hm", rel_table, hot, precision=lax.Precision.HIGHEST)
    wave = jnp.pad(wave, ((0, 16 - heads), (0, 0)))

    any_space = pl.BlockSpec(memory_space=pl.ANY)
    vmem = pl.BlockSpec(memory_space=pltpu.VMEM)
    smem = pl.BlockSpec(memory_space=pltpu.SMEM)
    keys = seq + KEY_PAD
    scratch = {
        "W": pltpu.VMEM((3, 4, 8, shard, width), BF),
        "G": pltpu.VMEM((3, 4, 4, 2, shard, width), BF),
        "land": pltpu.VMEM((4, 8, shard, width), BF),
        "KVT": pltpu.VMEM((heads, 128, keys), BF),
        "QT": pltpu.VMEM((heads, HEAD_DIM, span), BF),
        "ctxT": pltpu.VMEM((heads, HEAD_DIM, span), BF),
        "dOT": pltpu.VMEM((heads, HEAD_DIM, span), BF),
        "lse": pltpu.VMEM((16, span), F32),
        "xin": pltpu.VMEM((2, piece, width), BF),
        "gin": pltpu.VMEM((2, piece, width), BF),
        "ob": pltpu.VMEM((2, piece, width), BF),
        "na": pltpu.VMEM((span, width), BF),
        "nT": pltpu.VMEM((width, span), BF),
        "gT": pltpu.VMEM((width, span), BF),
        "act": pltpu.VMEM((span, width), BF),
        "gp": pltpu.VMEM((span, width), BF),
        "mid": pltpu.VMEM((span, width), F32),
        "acc": pltpu.VMEM((span, width), F32),
        "gacc": pltpu.VMEM((span, width), F32),
        "kv_own": pltpu.VMEM((2 * group, span, 128), F32),
        "kv_in": pltpu.VMEM((heads, span, 128), BF),
        "kv_out": pltpu.VMEM((heads, span, 128), BF),
        "dq": pltpu.VMEM((2 * group, span, HEAD_DIM), BF),
        "S": pltpu.VMEM((seq + 32, WIDE), F32),
        "P": pltpu.VMEM((keys, WIDE), BF),
        "ka": pltpu.VMEM((128, keys), BF),
        "va": pltpu.VMEM((128, keys), BF),
        "Ka": pltpu.VMEM((keys, 128), BF),
        "Va": pltpu.VMEM((keys, 128), BF),
        "qa": pltpu.VMEM((128, span), BF),
        "da": pltpu.VMEM((128, span), BF),
        "band": pltpu.VMEM((384, 128), F32),
        "code_in": pltpu.VMEM((8, keys), F32),
        "small": pltpu.VMEM((24, width), F32),
        "small_in": pltpu.VMEM((3, 24, width), F32),
        "small_z": pltpu.VMEM((4, 24, width), F32),
        "send_sems": pltpu.SemaphoreType.DMA((LINK_SEMS,)),
        "recv_sems": pltpu.SemaphoreType.DMA((LINK_SEMS,)),
        "local_sems": pltpu.SemaphoreType.DMA((3,)),
        "ready": pltpu.SemaphoreType.REGULAR,
    }
    operands = {
        "table": (rel_table, smem),
        "code": (code, vmem),
        "gains": (gains, vmem),
        "wave": (wave, vmem),
        "hidden": (hidden_in, any_space),
        "out_grad": (out_grad, any_space),
        "packed": (packed, any_space),
        "mem": (mem, any_space),
    }
    results = {
        "output": (jax.ShapeDtypeStruct(hidden_in.shape, BF), any_space),
        "grad_in": (jax.ShapeDtypeStruct(hidden_in.shape, BF), any_space),
        "gsum": (jax.ShapeDtypeStruct((3, shard, width), F32), vmem),
        "small_sum": (jax.ShapeDtypeStruct((24, width), F32), vmem),
    }
    names = [*operands, *results, *scratch]
    output, grad_input, gsum, small = pl.pallas_call(
        functools.partial(layer_kernel, names),
        out_shape=[shape for shape, _ in results.values()],
        in_specs=[spec for _, spec in operands.values()],
        out_specs=[spec for _, spec in results.values()],
        scratch_shapes=list(scratch.values()),
        compiler_params=pltpu.CompilerParams(
            collective_id=0, has_side_effects=True, vmem_limit_bytes=VMEM_LIMIT
        ),
    )(*[array for array, _ in operands.values()])
    gains_grad = small[0:2]
    table_grad = jnp.einsum("hm,mb->bh", small[8 : 8 + heads, 0:512], hot, precision=lax.Precision.HIGHEST)
    far = jnp.zeros((buckets, heads), F32).at[15].set(small[8 : 8 + heads, 512])
    table_grad = table_grad + far.at[31].set(small[8 : 8 + heads, 513])
    kv = gsum[0, :, 0 : group * 128].reshape(shard, group, 2, HEAD_DIM)
    qkv_sum = jnp.stack(
        [
            gsum[0, :, group * 128 : group * 192],
            kv[:, :, 0].reshape(shard, group * HEAD_DIM),
            kv[:, :, 1].reshape(shard, group * HEAD_DIM),
        ]
    )
    qkv = adamw(w_qkv, qkv_sum, m_qkv, v_qkv, MATRIX_RATE, WEIGHT_DECAY)
    attn_out = adamw(
        w_attn_out, gsum[0, :, group * 192 :].T, m_attn_out, v_attn_out, MATRIX_RATE, WEIGHT_DECAY
    )
    up = adamw(w_up, gsum[1], m_up, v_up, MATRIX_RATE, WEIGHT_DECAY)
    down = adamw(w_down, gsum[2].T, m_down, v_down, MATRIX_RATE, WEIGHT_DECAY)
    gain = adamw(gains, gains_grad, m_gains, v_gains, SMALL_RATE, 0.0)
    rel = adamw(rel_table, table_grad, m_rel, v_rel, SMALL_RATE, 0.0)
    out = [output, grad_input.astype(F32)]
    for new, moment, second in (qkv, attn_out, up, down):
        out += [new, moment, second, new.astype(BF)]
    return (*out, *gain, *rel)


def solution(mesh):
    if dict(mesh.shape) == {"dp": 8, "mp": 4}:
        mesh = Mesh(mesh.devices.reshape(2, 2, 2, 4), ("y", "x", "c", "z"))
        return placed_on(mesh, on_moved, ("y", "x", "c"), "z")
    return placed_on(mesh, on_device, "dp", "mp")


def placed_on(mesh, body, dp, mp):
    placed = (
        P(dp, mp, None),
        P(dp, mp, None),
        P(dp, None),
        P(dp),
        P(dp, None),
        P(dp, None, mp),
        P(dp, None, mp),
        P(None, dp, mp),
        P(None, dp, mp),
        P(None, dp, mp),
        P(mp, dp),
        P(mp, dp),
        P(mp, dp),
        P(dp, mp),
        P(dp, mp),
        P(dp, mp),
        P(mp, dp),
        P(mp, dp),
        P(mp, dp),
        P(),
        P(),
        P(),
        P(),
        P(),
        P(),
    )
    return jax.shard_map(
        body,
        mesh=mesh,
        in_specs=placed,
        out_specs=(
            P(dp, mp, None),
            P(dp, mp, None),
            P(None, dp, mp),
            P(None, dp, mp),
            P(None, dp, mp),
            P(None, dp, mp),
            P(mp, dp),
            P(mp, dp),
            P(mp, dp),
            P(mp, dp),
            P(dp, mp),
            P(dp, mp),
            P(dp, mp),
            P(dp, mp),
            P(mp, dp),
            P(mp, dp),
            P(mp, dp),
            P(mp, dp),
            P(),
            P(),
            P(),
            P(),
            P(),
            P(),
        ),
        check_vma=False,
    )
```

```python
import functools

import jax
import jax.numpy as jnp
import numpy as np
from jax import lax
from jax.experimental import pallas as pl
from jax.experimental.pallas import tpu as pltpu
from jax.sharding import Mesh
from jax.sharding import PartitionSpec as P

HEAD_DIM = 64
STEP = 10


NORM_EPS = 1e-06
MOMENT_DECAY = 0.5
ADAM_EPS = 1e-08
MATRIX_RATE = 0.05
SMALL_RATE = 0.5
WEIGHT_DECAY = 0.01
FAR_BOUNDS = (12, 16, 23, 32, 46, 64, 91)
NEG_FILL = -1e30


def bucket_of(distance):
    far_dist = jnp.abs(distance)
    far_bucket = jnp.full(far_dist.shape, 8, jnp.int32)
    for far_bound in FAR_BOUNDS:
        far_bucket = far_bucket + (far_dist >= far_bound).astype(jnp.int32)
    one_side = jnp.where(far_dist < 8, far_dist, far_bucket)
    return one_side + jnp.where(distance > 0, 16, 0).astype(jnp.int32)


def gelu_exact(values):
    return jax.nn.gelu(values, approximate=False)


def rms_inverse(values):
    return lax.rsqrt(jnp.mean(values * values, axis=-1, keepdims=True) + NORM_EPS)


def norm_back(grad_out, normed_hat, inverse, gain_row):
    scaled = grad_out * gain_row
    return inverse * (scaled - normed_hat * jnp.mean(scaled * normed_hat, axis=-1, keepdims=True))


def adamw(weight, gradient, first_mom, second, step_rate, decay_rate):
    first_new = MOMENT_DECAY * first_mom + (1.0 - MOMENT_DECAY) * gradient
    second_new = MOMENT_DECAY * second + (1.0 - MOMENT_DECAY) * gradient * gradient
    bias_fix = 1.0 - MOMENT_DECAY**STEP
    update = first_new / bias_fix / (jnp.sqrt(second_new / bias_fix) + ADAM_EPS)
    return (weight - step_rate * (update + decay_rate * weight), first_new, second_new)


def row_masks(seg_row, length, pair_on):
    positions = jnp.arange(seg_row.shape[0], dtype=jnp.int32)
    is_live = positions < length
    doc_group = jnp.where(is_live, seg_row, -1).astype(jnp.int32)
    slot_on = jnp.repeat(pair_on, 2) > 0
    return (is_live[:, None] & slot_on[None, :], doc_group[:, None] == doc_group[None, :])


def block_scores(q_block, mk_row, k_row, mem_ok, tok_ok, bias_block, score_scale):
    mem_raw = (
        jnp.einsum("hqe,hke->hqk", q_block, mk_row, preferred_element_type=jnp.float32)
        * score_scale
    )
    tok_raw = (
        jnp.einsum("hqe,hke->hqk", q_block, k_row, preferred_element_type=jnp.float32) * score_scale
        + bias_block
    )
    return (jnp.where(mem_ok[None], mem_raw, NEG_FILL), jnp.where(tok_ok[None], tok_raw, NEG_FILL))


def on_device(
    hidden_in,
    out_grad,
    seg_ids,
    row_len,
    slot_mask,
    mem_keys,
    mem_values,
    w_qkv,
    m_qkv,
    v_qkv,
    w_attn_out,
    m_attn_out,
    v_attn_out,
    w_up,
    m_up,
    v_up,
    w_down,
    m_down,
    v_down,
    gains,
    m_gains,
    v_gains,
    rel_table,
    m_rel,
    v_rel,
):
    qkv_low, attn_out_low, up_low, down_low = (
        lax.all_gather(w_qkv.astype(jnp.bfloat16), "dp", axis=1, tiled=True),
        lax.all_gather(w_attn_out.astype(jnp.bfloat16), "dp", axis=1, tiled=True),
        lax.all_gather(w_up.astype(jnp.bfloat16), "dp", axis=0, tiled=True),
        lax.all_gather(w_down.astype(jnp.bfloat16), "dp", axis=1, tiled=True),
    )
    row_count = hidden_in.shape[0]
    seq_span = seg_ids.shape[1]
    bucket_total, head_total = rel_table.shape
    head_local = head_total // lax.axis_size("mp")
    head_size = HEAD_DIM
    model_width = gains.shape[1]
    slots = mem_keys.shape[1]
    score_scale = head_size ** (-0.5)
    block_rows = min(512, seq_span)
    mp_index = lax.axis_index("mp")
    positions = jnp.arange(seq_span, dtype=jnp.int32)
    bucket_grid = bucket_of(positions[None, :] - positions[:, None])
    table_local = lax.dynamic_slice_in_dim(rel_table, mp_index * head_local, head_local, 1)
    rel_bias = jnp.zeros((head_local, seq_span, seq_span), jnp.float32)
    for bucket_number in range(bucket_total):
        rel_bias = rel_bias + jnp.where(
            (bucket_grid == bucket_number)[None], table_local[bucket_number][:, None, None], 0.0
        )
    qkv_heads = qkv_low.reshape(3, model_width, head_local, head_size)
    attn_out_heads = attn_out_low.reshape(head_local, head_size, model_width)
    inputs = hidden_in.astype(jnp.float32)
    inverse_one = rms_inverse(inputs)
    hat_one = inputs * inverse_one
    normed_one = (hat_one * gains[0]).astype(jnp.bfloat16)
    normed_full = lax.all_gather(normed_one, "mp", axis=1, tiled=True)
    project = jnp.einsum(
        "rsd,cdhe->crhse", normed_full, qkv_heads, preferred_element_type=jnp.float32
    ).astype(jnp.bfloat16)
    queries, key_new, value_new = (project[0], project[1], project[2])
    mem_key_rows = jnp.transpose(
        mem_keys.reshape(row_count, slots, head_local, head_size), (0, 2, 1, 3)
    )
    mem_value_rows = jnp.transpose(
        mem_values.reshape(row_count, slots, head_local, head_size), (0, 2, 1, 3)
    )

    def forward_row(packed):
        q_row, k_row, v_row, mk_row, mv_row, seg_row, length, pair_on = packed
        mem_allowed, tok_allowed = row_masks(seg_row, length, pair_on)
        contexts = []
        maxima = []
        for first_row in range(0, seq_span, block_rows):
            last_row = first_row + block_rows
            mem_s, tok_s = block_scores(
                q_row[:, first_row:last_row],
                mk_row,
                k_row,
                mem_allowed[first_row:last_row],
                tok_allowed[first_row:last_row],
                rel_bias[:, first_row:last_row],
                score_scale,
            )
            row_peak = jnp.maximum(
                jnp.max(mem_s, axis=-1, keepdims=True), jnp.max(tok_s, axis=-1, keepdims=True)
            )
            mem_exp = jnp.exp(mem_s - row_peak)
            tok_exp = jnp.exp(tok_s - row_peak)
            exp_total = jnp.sum(mem_exp, axis=-1, keepdims=True) + jnp.sum(
                tok_exp, axis=-1, keepdims=True
            )
            mem_prob = (mem_exp / exp_total).astype(jnp.bfloat16)
            tok_prob = (tok_exp / exp_total).astype(jnp.bfloat16)
            block_context = jnp.einsum(
                "hqk,hke->hqe", mem_prob, mv_row, preferred_element_type=jnp.float32
            )
            block_context = block_context + jnp.einsum(
                "hqk,hke->hqe", tok_prob, v_row, preferred_element_type=jnp.float32
            )
            contexts.append(block_context.astype(jnp.bfloat16))
            maxima.append((row_peak + jnp.log(exp_total))[:, :, 0])
        return (jnp.concatenate(contexts, axis=1), jnp.concatenate(maxima, axis=1))

    context, log_totals = lax.map(
        forward_row,
        (queries, key_new, value_new, mem_key_rows, mem_value_rows, seg_ids, row_len, slot_mask),
    )
    attn_term = jnp.einsum(
        "rhse,hed->rsd", context, attn_out_heads, preferred_element_type=jnp.float32
    )
    attn_local = lax.psum_scatter(attn_term, "mp", scatter_dimension=1, tiled=True)
    mid = inputs + attn_local
    inverse_two = rms_inverse(mid)
    hat_two = mid * inverse_two
    normed_two = (hat_two * gains[1]).astype(jnp.bfloat16)
    ffn_source = lax.all_gather(normed_two, "mp", axis=1, tiled=True)
    up_full, down_full = (up_low, down_low)
    pre_act = jnp.einsum("rsd,df->rsf", ffn_source, up_full, preferred_element_type=jnp.float32)
    act_value, act_back = jax.vjp(gelu_exact, pre_act)
    act_low = act_value.astype(jnp.bfloat16)
    ffn_term = jnp.einsum("rsf,fd->rsd", act_low, down_full, preferred_element_type=jnp.float32)
    ffn_local = lax.psum_scatter(
        ffn_term.astype(jnp.bfloat16), "mp", scatter_dimension=1, tiled=True
    ).astype(jnp.float32)
    output = (mid + ffn_local).astype(jnp.bfloat16)
    grad_top = out_grad.astype(jnp.float32)
    grad_source = lax.all_gather(out_grad, "mp", axis=1, tiled=True)
    down_grad = jnp.einsum("rsf,rsd->fd", act_low, grad_source, preferred_element_type=jnp.float32)
    grad_act = jnp.einsum("rsd,fd->rsf", grad_source, down_full, preferred_element_type=jnp.float32)
    grad_pre = act_back(grad_act)[0].astype(jnp.bfloat16)
    up_grad = jnp.einsum("rsd,rsf->df", ffn_source, grad_pre, preferred_element_type=jnp.float32)
    grad_normed_part = jnp.einsum(
        "rsf,df->rsd", grad_pre, up_full, preferred_element_type=jnp.float32
    )
    grad_normed_two = lax.psum_scatter(grad_normed_part, "mp", scatter_dimension=1, tiled=True)
    gain_two_grad = jnp.sum(grad_normed_two * hat_two, axis=(0, 1))
    grad_mid = grad_top + norm_back(grad_normed_two, hat_two, inverse_two, gains[1])
    grad_mid_low = grad_mid.astype(jnp.bfloat16)
    grad_attn_full = lax.all_gather(grad_mid_low, "mp", axis=1, tiled=True)
    attn_out_grad = jnp.einsum(
        "rhse,rsd->hed", context, grad_attn_full, preferred_element_type=jnp.float32
    )
    attn_out_grad = attn_out_grad.reshape(head_local * head_size, model_width)
    grad_context = jnp.einsum(
        "rsd,hed->rhse", grad_attn_full, attn_out_heads, preferred_element_type=jnp.float32
    ).astype(jnp.bfloat16)

    def backward_row(bias_total, packed):
        q_row, k_row, v_row, mk_row, mv_row, seg_row, length, pair_on, lse_row, grad_row = packed
        mem_allowed, tok_allowed = row_masks(seg_row, length, pair_on)
        key_acc = jnp.zeros(k_row.shape, jnp.float32)
        value_acc = jnp.zeros(v_row.shape, jnp.float32)
        query_parts = []
        bias_parts = []
        for first_row in range(0, seq_span, block_rows):
            last_row = first_row + block_rows
            q_block = q_row[:, first_row:last_row]
            mem_s, tok_s = block_scores(
                q_block,
                mk_row,
                k_row,
                mem_allowed[first_row:last_row],
                tok_allowed[first_row:last_row],
                rel_bias[:, first_row:last_row],
                score_scale,
            )
            lse_block = lse_row[:, first_row:last_row, None]
            mem_prob = jnp.exp(mem_s - lse_block)
            tok_prob = jnp.exp(tok_s - lse_block)
            grad_block = grad_row[:, first_row:last_row]
            mem_gprob = jnp.einsum(
                "hqe,hke->hqk", grad_block, mv_row, preferred_element_type=jnp.float32
            )
            tok_gprob = jnp.einsum(
                "hqe,hke->hqk", grad_block, v_row, preferred_element_type=jnp.float32
            )
            row_dot = jnp.sum(mem_prob * mem_gprob, axis=-1, keepdims=True) + jnp.sum(
                tok_prob * tok_gprob, axis=-1, keepdims=True
            )
            mem_gscore = (mem_prob * (mem_gprob - row_dot)).astype(jnp.bfloat16)
            tok_gscore = (tok_prob * (tok_gprob - row_dot)).astype(jnp.bfloat16)
            query_grad = jnp.einsum(
                "hqk,hke->hqe", mem_gscore, mk_row, preferred_element_type=jnp.float32
            )
            query_grad = query_grad + jnp.einsum(
                "hqk,hke->hqe", tok_gscore, k_row, preferred_element_type=jnp.float32
            )
            query_parts.append((query_grad * score_scale).astype(jnp.bfloat16))
            key_acc = key_acc + jnp.einsum(
                "hqk,hqe->hke", tok_gscore, q_block, preferred_element_type=jnp.float32
            )
            value_acc = value_acc + jnp.einsum(
                "hqk,hqe->hke",
                tok_prob.astype(jnp.bfloat16),
                grad_block,
                preferred_element_type=jnp.float32,
            )
            bias_parts.append(tok_gscore.astype(jnp.float32))
        bias_total = bias_total + jnp.concatenate(bias_parts, axis=1)
        row_grads = (
            jnp.concatenate(query_parts, axis=1),
            (key_acc * score_scale).astype(jnp.bfloat16),
            value_acc.astype(jnp.bfloat16),
        )
        return (bias_total, row_grads)

    bias_grad, (grad_q, grad_k, grad_v) = lax.scan(
        backward_row,
        jnp.zeros((head_local, seq_span, seq_span), jnp.float32),
        (
            queries,
            key_new,
            value_new,
            mem_key_rows,
            mem_value_rows,
            seg_ids,
            row_len,
            slot_mask,
            log_totals,
            grad_context,
        ),
    )
    grad_project = jnp.stack([grad_q, grad_k, grad_v])
    qkv_grad = jnp.einsum(
        "rsd,crhse->cdhe", normed_full, grad_project, preferred_element_type=jnp.float32
    )
    qkv_grad = qkv_grad.reshape(3, model_width, head_local * head_size)
    grad_normed_term = jnp.einsum(
        "crhse,cdhe->rsd", grad_project, qkv_heads, preferred_element_type=jnp.float32
    )
    grad_normed_one = lax.psum_scatter(
        grad_normed_term.astype(jnp.bfloat16), "mp", scatter_dimension=1, tiled=True
    ).astype(jnp.float32)
    gain_one_grad = jnp.sum(grad_normed_one * hat_one, axis=(0, 1))
    grad_input = grad_mid + norm_back(grad_normed_one, hat_one, inverse_one, gains[0])
    bucket_sums = []
    for bucket_number in range(bucket_total):
        bucket_sums.append(
            jnp.sum(jnp.where((bucket_grid == bucket_number)[None], bias_grad, 0.0), axis=(1, 2))
        )
    table_local_grad = jnp.stack(bucket_sums)
    table_grad = lax.dynamic_update_slice(
        jnp.zeros((bucket_total, head_total), jnp.float32),
        table_local_grad,
        (jnp.int32(0), mp_index * head_local),
    )
    gains_grad, table_grad = lax.psum(
        (jnp.stack([gain_one_grad, gain_two_grad]), table_grad), ("dp", "mp")
    )
    qkv_sum, attn_out_sum, up_sum, down_sum = (
        lax.psum_scatter(qkv_grad, "dp", scatter_dimension=1, tiled=True),
        lax.psum_scatter(attn_out_grad, "dp", scatter_dimension=1, tiled=True),
        lax.psum_scatter(up_grad, "dp", scatter_dimension=0, tiled=True),
        lax.psum_scatter(down_grad, "dp", scatter_dimension=1, tiled=True),
    )
    qkv_new, qkv_first, qkv_second = adamw(w_qkv, qkv_sum, m_qkv, v_qkv, MATRIX_RATE, WEIGHT_DECAY)
    attn_out_new, attn_out_first, attn_out_second = adamw(
        w_attn_out, attn_out_sum, m_attn_out, v_attn_out, MATRIX_RATE, WEIGHT_DECAY
    )
    up_new, up_first, up_second = adamw(w_up, up_sum, m_up, v_up, MATRIX_RATE, WEIGHT_DECAY)
    down_new, down_first, down_second = adamw(
        w_down, down_sum, m_down, v_down, MATRIX_RATE, WEIGHT_DECAY
    )
    gains_new, gains_first, gains_second = adamw(
        gains, gains_grad, m_gains, v_gains, SMALL_RATE, 0.0
    )
    rel_new, rel_first, rel_second = adamw(rel_table, table_grad, m_rel, v_rel, SMALL_RATE, 0.0)
    return (
        output,
        grad_input,
        qkv_new,
        qkv_first,
        qkv_second,
        qkv_new.astype(jnp.bfloat16),
        attn_out_new,
        attn_out_first,
        attn_out_second,
        attn_out_new.astype(jnp.bfloat16),
        up_new,
        up_first,
        up_second,
        up_new.astype(jnp.bfloat16),
        down_new,
        down_first,
        down_second,
        down_new.astype(jnp.bfloat16),
        gains_new,
        gains_first,
        gains_second,
        rel_new,
        rel_first,
        rel_second,
    )


BF = jnp.bfloat16
F32 = jnp.float32
MESH_ID = pl.DeviceIdType.MESH
BIG = 1e30
KEY_PAD = 128
WIDE = 256
SQRT_HALF = 0.5**0.5
INV_SQRT_2PI = 0.3989422804014327
LINK_SEMS = 200
VMEM_LIMIT = 63 * 2**20


def dot(a, b):
    return lax.dot_general(a, b, (((1,), (0,)), ((), ())), preferred_element_type=F32)


def dot_t(a, b):
    return lax.dot_general(a, b, (((1,), (1,)), ((), ())), preferred_element_type=F32)


def split3(v):
    hi = v.astype(BF)
    rest = v - hi.astype(F32)
    mid = rest.astype(BF)
    low = (rest - mid.astype(F32)).astype(BF)
    return hi, mid, low


class Links:
    def __init__(self, send_sems, recv_sems):
        self.send_sems, self.recv_sems = send_sems, recv_sems
        self.count = 0
        self.sent = []

    def take(self, n=1):
        self.count += n
        return self.count - n

    def send(self, src, dst, device, send_at=None, recv_at=None, when=None, else_keep=False):
        at = self.take() if send_at is None else send_at
        recv_at = at if recv_at is None else recv_at
        copy = pltpu.make_async_remote_copy(
            src, dst, self.send_sems.at[at], self.recv_sems.at[recv_at], device_id=device, device_id_type=MESH_ID
        )
        if when is None:
            copy.start()
        else:

            @pl.when(when)
            def _():
                copy.start()

            if else_keep:

                @pl.when(jnp.logical_not(when))
                def _():
                    pltpu.make_async_copy(src, dst, self.recv_sems.at[recv_at]).start()

        self.sent.append((copy, when))
        return at

    def arrived(self, dst, k):
        pltpu.make_async_copy(dst, dst, self.recv_sems.at[k]).wait()

    def left(self, since, until=None):
        for n in range(since, len(self.sent) if until is None else until):
            if self.sent[n] is None:
                continue
            copy, when = self.sent[n]
            if when is None:
                copy.wait_send()
            else:
                pl.when(when)(copy.wait_send)
            self.sent[n] = None


class Place:
    def __init__(self):
        self.y, self.x = lax.axis_index("y"), lax.axis_index("x")
        self.c, self.z = lax.axis_index("c"), lax.axis_index("z")
        self.to_x, self.to_y = {"x": 1 - self.x}, {"y": 1 - self.y}
        self.to_c, self.to_xy = {"c": 1 - self.c}, {"x": 1 - self.x, "y": 1 - self.y}
        z = self.z
        self.near = (z, z + 1 - 2 * lax.rem(z, 2), jnp.where(z < 2, 2, 1), jnp.where(z < 2, 3, 0))
        self.inner = (z == 1) | (z == 2)

    def greet(self):
        barrier = pltpu.get_barrier_semaphore()
        peers = [self.to_x, self.to_y, self.to_c, self.to_xy]
        for z in self.near[1:]:
            peers.append({"z": z})
            peers.append({"z": z, "c": 1 - self.c})
        for peer in peers:
            pl.semaphore_signal(barrier, inc=1, device_id=peer, device_id_type=MESH_ID)
        self.greeted = len(peers)

    def meet(self):
        pl.semaphore_wait(pltpu.get_barrier_semaphore(), self.greeted)


class Gather:
    def __init__(self, place, links, shard, whole, local_sem):
        self.p, self.links, self.shard, self.whole, self.local_sem = place, links, shard, whole, local_sem
        self.at_z = links.take(4)
        self.k_x, self.k_y, self.k_d, self.k_c = {}, {}, {}, {}
        self.out = {k: [] for k in range(4)}

    def spot(self, k, y, x):
        return self.whole.at[self.p.near[k], 2 * y + x, self.p.c]

    def send(self, k, *args, **kwargs):
        self.out[k].append(len(self.links.sent))
        return self.links.send(*args, **kwargs)

    def start_z(self):
        p = self.p
        own = self.spot(0, p.y, p.x)
        for k in (2, 1, 3):
            self.links.send(
                self.shard, own, {"z": p.near[k]}, self.at_z + k, self.at_z + p.z, p.inner if k == 3 else None
            )

    def start_own(self):
        p = self.p
        own = self.spot(0, p.y, p.x)
        self.own_copy = pltpu.make_async_copy(self.shard, own, self.local_sem)
        self.own_copy.start()
        self.k_x[0] = self.links.send(self.shard, own, p.to_x)
        self.k_y[0] = self.links.send(self.shard, own, p.to_y)

    def column(self, k):
        p = self.p
        block = self.spot(k, p.y, p.x)
        self.links.arrived(block, self.at_z + p.near[k])
        self.k_x[k] = self.send(k, block, block, p.to_x)
        self.k_y[k] = self.send(k, block, block, p.to_y)
        if k == 3:
            self.send(3, block, block, {"z": p.near[1]}, self.at_z, self.at_z + p.near[3], p.inner)

    def forward(self, k):
        p = self.p
        from_x, from_y = self.spot(k, p.y, 1 - p.x), self.spot(k, 1 - p.y, p.x)
        if k % 2 == 0:
            self.links.arrived(from_x, self.k_x[k])
            self.k_d[k] = self.send(k, from_x, from_x, p.to_y)
            self.links.arrived(from_y, self.k_y[k])
        else:
            self.links.arrived(from_y, self.k_y[k])
            self.k_d[k] = self.send(k, from_y, from_y, p.to_x)
            self.links.arrived(from_x, self.k_x[k])

    def cross(self, k):
        p = self.p
        self.links.arrived(self.spot(k, 1 - p.y, 1 - p.x), self.k_d[k])
        if k == 0:
            self.own_copy.wait()
        half = self.whole.at[p.near[k], :, p.c]
        self.k_c[k] = self.send(k, half, half, p.to_c)

    def finish(self, k):
        p = self.p
        self.links.arrived(self.whole.at[p.near[k], :, 1 - p.c], self.k_c[k])

    def release(self, k):
        for n in self.out[k]:
            self.links.left(n, n + 1)


class Reduce:
    def __init__(self, place, links, grads, land, turn):
        self.p, self.links, self.g, self.land, self.turn = place, links, grads, land, turn
        self.k_c, self.k_first, self.k_second = {}, {}, {}
        self.at_z = links.take(4)

    def start(self, k):
        p = self.p
        spot = self.land.at[k // 2, pl.ds(k % 2 * 4, 4)]
        self.k_c[k] = self.links.send(self.g.at[p.near[k], :, 1 - p.c], spot, p.to_c)

    def add(self, k, n, row, col):
        at = (self.p.near[k], n, self.p.c)
        self.g[at] = (self.g[at].astype(F32) + self.land[row, col].astype(F32)).astype(BF)

    def x_first(self, k):
        return (k + self.turn) % 2 == 0

    def core(self, k):
        p, links = self.p, self.links
        links.arrived(self.land.at[k // 2, pl.ds(k % 2 * 4, 4)], self.k_c[k])
        self.k_first[k] = []
        away = [2 * i + 1 - p.x if self.x_first(k) else 2 * (1 - p.y) + i for i in (0, 1)]
        stay = [2 * i + p.x if self.x_first(k) else 2 * p.y + i for i in (0, 1)]
        for i, n in enumerate(away):
            self.add(k, n, k // 2, k % 2 * 4 + n)
            self.k_first[k].append(
                links.send(
                    self.g.at[p.near[k], n, p.c],
                    self.land.at[2, 2 * k + i],
                    p.to_x if self.x_first(k) else p.to_y,
                )
            )
        for n in stay:
            self.add(k, n, k // 2, k % 2 * 4 + n)

    def plane(self, k):
        p, links = self.p, self.links
        for i in (0, 1):
            links.arrived(self.land.at[2, 2 * k + i], self.k_first[k][i])
            self.add(k, 2 * i + p.x if self.x_first(k) else 2 * p.y + i, 2, 2 * k + i)
        n, peer = (2 * (1 - p.y) + p.x, p.to_y) if self.x_first(k) else (2 * p.y + 1 - p.x, p.to_x)
        self.k_second[k] = links.send(self.g.at[p.near[k], n, p.c], self.land.at[3, k], peer)

    def column(self, k):
        p, links = self.p, self.links
        here = 2 * p.y + p.x
        links.arrived(self.land.at[3, k], self.k_second[k])
        self.add(k, here, 3, k)
        if k == 0:
            return
        mine = self.g.at[p.near[k], here, p.c]
        target = p.near[k]
        spot = p.z
        if k == 3:
            @pl.when(p.inner)
            def _():
                links.arrived(self.land.at[3, 4 + p.z], self.at_z + p.z)
                self.add(3, here, 3, 4 + p.z)

            target = jnp.where(p.inner, p.near[3], p.near[1])
            spot = jnp.where(p.inner, p.z, p.near[1])
        links.send(mine, self.land.at[3, 4 + spot], {"z": target}, self.at_z + k, self.at_z + spot)

    def finish(self, out):
        p = self.p
        total = self.g[p.z, 2 * p.y + p.x, p.c].astype(F32)
        for k in (1, 2):
            source = p.near[k]
            self.links.arrived(self.land.at[3, 4 + source], self.at_z + source)
            total = total + self.land[3, 4 + source].astype(F32)
        out[...] = total

        @pl.when(p.inner)
        def _():
            source = p.near[3]
            self.links.arrived(self.land.at[3, 4 + source], self.at_z + source)
            out[...] += self.land[3, 4 + source].astype(F32)


def band_tiles(group, chunk):
    tiles = []
    for i in range(2):
        for j in range(2):
            block = 2 * group + j
            if chunk < 2:
                apart = 2 * chunk + i - block
                if abs(apart) <= 1:
                    tiles.append((i, j, apart + 1, None))
            else:
                other = 2 * (chunk - 2) + i
                if block == 3 and other == 0:
                    tiles.append((i, j, 2, 0))
                if block == 0 and other == 3:
                    tiles.append((i, j, 0, 1))
    return tiles


def add_band(s, band, group, chunk, core):
    tiles = band_tiles(group, chunk)
    if not tiles:
        return s
    rows = []
    for i in range(2):
        cols = []
        for j in range(2):
            part = s[i * 128 : (i + 1) * 128, j * 128 : (j + 1) * 128]
            for a, b, third, need in tiles:
                if (a, b) == (i, j):
                    near = band[third * 128 : (third + 1) * 128, :]
                    if need is not None:
                        near = near * jnp.where(core == need, 1.0, 0.0)
                    part = part + near
            cols.append(part)
        rows.append(jnp.concatenate(cols, axis=1))
    return jnp.concatenate(rows, axis=0)


def far_masks(core, span):
    key = lax.broadcasted_iota(jnp.int32, (8, span), 0)
    block = lax.broadcasted_iota(jnp.int32, (8, span), 1) // 128
    other = key - 4
    left = ((key < 4) & (key <= block - 2)) | ((key >= 4) & (core == 1) & ~((block == 0) & (other == 3)))
    right = ((key < 4) & (key >= block + 2)) | ((key >= 4) & (core == 0) & ~((block == 3) & (other == 0)))
    return left, right


def rows_of(parts, span):
    row = lax.broadcasted_iota(jnp.int32, (8, span), 0)
    out = jnp.zeros((8, span), F32)
    for n, part in enumerate(parts):
        out = jnp.where(row == n, part.astype(F32), out)
    return out.astype(BF)


def far_rows(left, right, far_left, far_right):
    hi, mid, low = split3(jnp.where(left, far_left, jnp.where(right, far_right, 0.0)))
    return jnp.concatenate([hi.astype(F32), mid.astype(F32), low.astype(F32)], axis=0).astype(BF)


def fwd_head(R, h, core, far_left, far_right):
    span, keys = R.QT.shape[2], R.KVT.shape[2]
    toks = keys - KEY_PAD
    R.ka[0:64, :] = R.KVT[h, 0:64, :]
    R.Ka[...] = R.ka[...].T
    R.va[0:64, :] = R.KVT[h, 64:128, :]
    R.qa[0:64, :] = R.QT[h]
    left, right = far_masks(core, span)
    R.qa[80:104, :] = far_rows(left, right, far_left, far_right)
    R.band[...] = band_of(R.wave[pl.ds(h, 1), :])
    band = R.band
    chunks = [(n, slice(n * WIDE, (n + 1) * WIDE)) for n in range(toks // WIDE)]
    last = slice(toks, toks + 32)
    for group in range(span // WIDE):
        cols = slice(group * WIDE, (group + 1) * WIDE)
        query = R.qa[:, cols]
        peak = None
        for n, rows in chunks:
            s = add_band(dot(R.Ka[rows, :], query), band, group, n, core)
            R.S[rows, :] = s
            top = jnp.max(s, axis=0, keepdims=True)
            peak = top if peak is None else jnp.maximum(peak, top)
        s = dot(R.Ka[last, :], query)
        R.S[last, :] = s
        peak = jnp.maximum(peak, jnp.max(s, axis=0, keepdims=True))
        for _, rows in chunks:
            R.P[rows, :] = jnp.exp(R.S[rows, :] - peak).astype(BF)
        R.P[last, :] = jnp.exp(R.S[last, :] - peak).astype(BF)
        o = dot(R.va[0:72, :], R.P[...])
        total = o[64:65, :]
        R.ctxT[h, :, cols] = (o[0:64, :] * (1.0 / total)).astype(BF)
        R.lse[pl.ds(h, 1), cols] = peak + jnp.log(total)


def bwd_head(R, h, j, core, far_left, far_right):
    span, keys = R.QT.shape[2], R.KVT.shape[2]
    toks = keys - KEY_PAD
    R.ka[0:64, :] = R.KVT[h, 0:64, :]
    R.Ka[...] = R.ka[...].T
    R.va[0:64, :] = R.KVT[h, 64:128, :]
    R.Va[...] = R.va[...].T
    R.qa[0:64, :] = R.QT[h]
    left, right = far_masks(core, span)
    R.qa[80:104, :] = far_rows(left, right, far_left, far_right)
    R.qa[72:80, :] = rows_of(split3(-R.lse[pl.ds(h, 1), :]), span)
    grad = R.dOT[h]
    R.da[0:64, :] = grad
    row_dot = jnp.sum(grad.astype(F32) * R.ctxT[h].astype(F32), axis=0, keepdims=True)
    R.da[64:72, :] = rows_of(split3(-row_dot), span)
    R.band[...] = band_of(R.wave[pl.ds(h, 1), :])
    band = R.band
    groups = span // WIDE
    query_sum = [None] * groups
    near = [None, None, None]
    for n in range(toks // WIDE + 1):
        is_mem = n * WIDE == toks
        rows = slice(toks, toks + 32) if is_mem else slice(n * WIDE, (n + 1) * WIDE)
        key_sum = value_sum = None
        for group in range(groups):
            cols = slice(group * WIDE, (group + 1) * WIDE)
            s = dot(R.Ka[rows, :], R.qa[:, cols])
            if not is_mem:
                s = add_band(s, band, group, n, core)
            p = jnp.exp(s)
            ds = p * dot(R.Va[rows, :], R.da[:, cols])
            ds_low = ds.astype(BF)
            if is_mem:
                filled = jnp.concatenate([ds_low, jnp.zeros((KEY_PAD - 32, WIDE), BF)], axis=0)
                part = dot(R.ka[0:96, toks:keys], filled)
            else:
                v = dot_t(p.astype(BF), R.da[0:64, cols])
                k = dot_t(ds_low, R.qa[0:64, cols])
                value_sum = v if value_sum is None else value_sum + v
                key_sum = k if key_sum is None else key_sum + k
                for a, b, third, need in band_tiles(group, n):
                    t = ds[a * 128 : (a + 1) * 128, b * 128 : (b + 1) * 128]
                    if need is not None:
                        t = t * jnp.where(core == need, 1.0, 0.0)
                    near[third] = t if near[third] is None else near[third] + t
                part = dot(R.ka[0:96, rows], ds_low)
            query_sum[group] = part if query_sum[group] is None else query_sum[group] + part
        if not is_mem:
            both = jnp.concatenate([key_sum, value_sum], axis=1)
            if n * WIDE < span:
                R.kv_own[j, rows, :] = both
            else:
                R.kv_out[h, slice(n * WIDE - span, (n + 1) * WIDE - span), :] = both.astype(BF)
    turned = jnp.concatenate(query_sum, axis=1)
    R.dq[j] = (turned[0:64, :] * HEAD_DIM**-0.5).T.astype(BF)
    far = turned[80:88, :]
    lane = lax.broadcasted_iota(jnp.int32, (1, 128), 1)
    sum_left = jnp.sum(jnp.where(left, far, 0.0))
    sum_right = jnp.sum(jnp.where(right, far, 0.0))
    ends = jnp.where(lane == 0, sum_left, jnp.where(lane == 1, sum_right, 0.0))
    R.small[pl.ds(2 + h, 1), 0:640] = jnp.concatenate([unband(jnp.concatenate(near, axis=0)), ends], axis=1)


class Refs:
    def __init__(self, **refs):
        self.__dict__.update(refs)


def weights(R, n, z, cols):
    part = R.W[n, z, :, :, :, cols]
    return part.reshape(-1, part.shape[3])


class RowMove:
    def __init__(self, place, links, src, dst):
        self.links, self.dst = links, dst
        slot = lax.rem(place.z, 2)
        self.at = links.take(2)
        for i in (0, 1):
            target_z, target_c = 2 * place.c + i, place.z // 2
            links.send(
                src.at[i],
                dst.at[slot],
                {"c": target_c, "z": target_z},
                self.at + i,
                self.at + slot,
                (target_c != place.c) | (target_z != place.z),
                else_keep=True,
            )

    def wait(self, slot):
        self.links.arrived(self.dst.at[slot], self.at + slot)


def norm_parts(values):
    inverse = lax.rsqrt(jnp.mean(values * values, axis=-1, keepdims=True) + NORM_EPS)
    return inverse, values * inverse


def mask_rows(R, place):
    span, keys = R.QT.shape[2], R.KVT.shape[2]
    toks = keys - KEY_PAD
    mine = jnp.where(place.z // 2 == place.c, R.code[lax.rem(place.z, 2)], R.code_in[...])
    R.code_in[...] = mine
    own = R.code_in[:, pl.ds(pl.multiple_of(place.c * span, span), span)]
    other = R.code_in[:, pl.ds(pl.multiple_of((1 - place.c) * span, span), span)]
    line = jnp.concatenate([own, other, R.code_in[:, toks:keys]], axis=1)
    row = lax.broadcasted_iota(jnp.int32, (8, keys), 0)
    as_doc = (row - 1).astype(F32)
    kind = jnp.where(row < 5, jnp.where(line == as_doc, 1.0, 0.0), 0.0)
    kind = jnp.where((row == 5) & (line == 11.0), 1.0, kind)
    kind = jnp.where((row == 6) & (line >= 10.0), 1.0, kind)
    R.ka[64:72, :] = kind.astype(BF)
    R.ka[72:80, :] = jnp.where(row < 3, 1.0, 0.0).astype(BF)
    block = lax.broadcasted_iota(jnp.int32, (8, keys), 1) // 128
    hot = jnp.where((block == row) & (block < toks // 128), 1.0, 0.0)
    R.ka[80:104, :] = jnp.concatenate([hot, hot, hot], axis=0).astype(BF)
    R.ka[104:128, :] = jnp.zeros((24, keys), BF)
    R.va[64:72, :] = jnp.where(row < 3, 1.0, 0.0).astype(BF)
    R.va[72:128, :] = jnp.zeros((56, keys), BF)
    qrow = lax.broadcasted_iota(jnp.int32, (8, span), 0)
    hide = jnp.where((qrow < 5) & (own != (qrow - 1).astype(F32)), -BIG, 0.0)
    hide = jnp.where(qrow == 5, -BIG, hide)
    hide = jnp.where((qrow == 6) & (own == -1.0), -BIG, hide)
    R.qa[64:72, :] = hide.astype(BF)
    R.qa[72:128, :] = jnp.zeros((56, span), BF)
    R.da[64:128, :] = jnp.zeros((64, span), BF)
    R.P[toks + 32 : keys, :] = jnp.zeros((KEY_PAD - 32, WIDE), BF)


def band_of(wave):
    spread = jnp.broadcast_to(wave, (128, 512))
    parts = [pltpu.roll(spread, 128 * n, 1, stride=1, stride_axis=0)[:, 0:128] for n in range(3)]
    return jnp.concatenate(parts, axis=0)


def unband(near):
    empty = jnp.zeros((8, 128), F32)
    total = None
    for n in range(16):
        part = jnp.concatenate(
            [near[8 * n : 8 * n + 8], empty, near[256 + 8 * n : 264 + 8 * n], near[128 + 8 * n : 136 + 8 * n]], axis=1
        )
        if n:
            part = pltpu.roll(part, 512 - 8 * n, 1)
        total = part if total is None else total + part
    row = lax.broadcasted_iota(jnp.int32, (8, 512), 0)
    out = jnp.zeros((8, 512), F32)
    for n in range(8):
        out = out + jnp.where(row == n, total if n == 0 else pltpu.roll(total, 512 - n, 1), 0.0)
    return jnp.sum(out, axis=0, keepdims=True)


def prepare(R):
    rows, seq = R.seg_ids.shape
    slots, heads_wide = R.mem_keys.shape[1:]
    group = heads_wide // HEAD_DIM
    parts = []
    for j in range(group):
        cols = slice(j * HEAD_DIM, (j + 1) * HEAD_DIM)
        parts += [R.w_qkv[1, :, cols], R.w_qkv[2, :, cols]]
    parts += [R.w_qkv[0], R.w_attn_out[...].T]
    R.packed[0] = jnp.concatenate(parts, axis=1).astype(BF)
    R.packed[1] = R.w_up[...].astype(BF)
    R.packed[2] = R.w_down[...].astype(BF)
    R.mem[...] = jnp.zeros_like(R.mem)
    place = lax.broadcasted_iota(jnp.int32, (1, seq), 1)
    pair = lax.broadcasted_iota(jnp.int32, (slots // 2, KEY_PAD), 0)
    lane = lax.broadcasted_iota(jnp.int32, (slots // 2, KEY_PAD), 1)
    spread = jnp.where(lane // 2 == pair, 1.0, 0.0)
    on = dot(jnp.where(R.slot_mask[...] > 0, 1.0, 0.0), spread)
    for r in range(rows):
        for n, mem in enumerate((R.mem_keys, R.mem_values)):
            turned = mem[r].astype(F32).T.astype(BF)
            for j in range(group):
                R.mem[r, j, n * 64 : n * 64 + HEAD_DIM, 0:slots] = turned[j * HEAD_DIM : (j + 1) * HEAD_DIM, :]
        docs = jnp.where(place < R.row_len[r], R.seg_ids[r : r + 1, :], -1).astype(F32)
        R.code[r, :, 0:seq] = jnp.broadcast_to(docs, (8, seq))
        R.code[r, :, seq : seq + KEY_PAD] = jnp.broadcast_to(jnp.where(on[r : r + 1] > 0.5, 10.0, 11.0), (8, KEY_PAD))
    heads = R.rel_table.shape[0]
    made = lax.dot_general(
        R.rel_table[...],
        R.hot[...],
        (((1,), (0,)), ((), ())),
        precision=lax.Precision.HIGHEST,
        preferred_element_type=F32,
    )
    R.wave[0:heads, :] = made


def update_kernel(names, *refs):
    R = Refs(**dict(zip(names, refs)))
    group = R.w_qkv.shape[2] // HEAD_DIM
    kv_cols, qkv_cols = group * 128, group * 192
    R.output_out[...] = R.output[...]
    R.grad_input[...] = R.grad_in[...].astype(F32)

    def step(name, gradient, at=Ellipsis, rate=MATRIX_RATE, decay=WEIGHT_DECAY, copy=True):
        ref = lambda kind: getattr(R, kind + "_" + name)
        new, first, second = adamw(ref("w")[at], gradient, ref("m")[at], ref("v")[at], rate, decay)
        ref("new")[at] = new
        ref("first")[at] = first
        ref("second")[at] = second
        if copy:
            ref("copy")[at] = new.astype(BF)

    sums = R.gsum[0]
    step("qkv", sums[:, kv_cols:qkv_cols], 0)
    for n in (0, 1):
        parts = [sums[:, j * 128 + n * 64 : j * 128 + n * 64 + HEAD_DIM] for j in range(group)]
        step("qkv", jnp.concatenate(parts, axis=1), 1 + n)
    step("attn_out", sums[:, qkv_cols:].T)
    step("up", R.gsum[1])
    step("down", R.gsum[2])
    step("gains", R.small[0:2, :], rate=SMALL_RATE, decay=0.0, copy=False)
    heads = R.w_rel.shape[0]
    along = lax.dot_general(
        R.small[2 : 2 + heads, 0:512],
        R.hot[...],
        (((1,), (1,)), ((), ())),
        precision=lax.Precision.HIGHEST,
        preferred_element_type=F32,
    )
    bucket = lax.broadcasted_iota(jnp.int32, along.shape, 1)
    ends = R.small[2 : 2 + heads, 512:640]
    along = along + jnp.where(bucket == 15, ends[:, 0:1], 0.0) + jnp.where(bucket == 31, ends[:, 1:2], 0.0)
    step("rel", along, rate=SMALL_RATE, decay=0.0, copy=False)


def layer_kernel(names, *refs):
    R = Refs(**dict(zip(names, refs)))
    place = Place()
    links = Links(R.send_sems, R.recv_sems)
    place.greet()
    prepare(R)
    place.meet()
    heads, span = R.QT.shape[0], R.QT.shape[2]
    width = R.xin.shape[2]
    group = heads // 4
    kv_cols, q_cols = group * 128, group * HEAD_DIM
    qkv_cols = kv_cols + q_cols
    slots = R.xin.shape[0]
    piece = R.xin.shape[1]

    near = place.near
    first, up, down = gather = [Gather(place, links, R.packed.at[n], R.W.at[n], R.local_sems.at[n]) for n in range(3)]
    first.start_z()
    first.start_own()
    k_code = links.send(R.code.at[lax.rem(place.z, 2)], R.code_in, place.to_c)
    at_mem = links.take(4)
    mem_spot = R.KVT.at[pl.ds(group * place.z, group), :, 2 * span : 2 * span + KEY_PAD]
    for r in (0, 1):
        for c in (0, 1):
            links.send(
                R.mem.at[r],
                mem_spot,
                {"c": c, "z": 2 * place.c + r},
                at_mem + 2 * r + c,
                at_mem + place.z,
                (place.c != c) | (place.z != 2 * place.c + r),
                else_keep=True,
            )
    up.start_z()
    up.start_own()
    for k in (1, 2, 3):
        first.column(k)
    move_in = RowMove(place, links, R.hidden, R.xin)
    down.start_z()
    down.start_own()
    for k in range(4):
        first.forward(k)
    for k in range(4):
        first.cross(k)
    links.arrived(R.code_in, k_code)
    mask_rows(R, place)
    for k in (1, 2, 3):
        up.column(k)
    up.forward(0)
    up.forward(1)
    for s in range(slots):
        move_in.wait(s)
        _, hat = norm_parts(R.xin[s].astype(F32))
        R.na[s * piece : (s + 1) * piece, :] = (hat * R.gains[0:1, :]).astype(BF)

    def heads_of(k):
        return pl.ds(group * near[k], group)

    k_kv = []
    for k in range(4):
        first.finish(k)
        low = dot(R.na[...], weights(R, 0, near[k], slice(0, qkv_cols))).astype(BF)
        for j in range(group):
            R.KVT[group * near[k] + j, :, 0:span] = low[:, j * 128 : (j + 1) * 128].T
        turned = (low[:, kv_cols:qkv_cols].astype(F32) * HEAD_DIM**-0.5).astype(BF).T
        for j in range(group):
            R.QT[group * near[k] + j] = turned[j * HEAD_DIM : (j + 1) * HEAD_DIM, :]
        block = heads_of(k)
        k_kv.append(links.send(R.KVT.at[block, :, 0:span], R.KVT.at[block, :, span : 2 * span], place.to_c))
    up.forward(2)
    up.forward(3)
    move_grad = RowMove(place, links, R.out_grad, R.gin)
    for k in range(4):
        up.cross(k)
    for k in (1, 2, 3):
        down.column(k)

    for k in range(4):
        block = heads_of(k)
        links.arrived(R.KVT.at[block, :, span : 2 * span], k_kv[k])
        links.arrived(R.KVT.at[block, :, 2 * span : 2 * span + KEY_PAD], at_mem + near[k])

        @pl.loop(0, group)
        def _(j):
            h = group * near[k] + j
            fwd_head(R, h, place.c, R.far_bias[h, 15], R.far_bias[h, 31])

        if k == 0:
            down.forward(0)
            down.forward(1)
        elif k == 1:
            down.forward(2)
            down.cross(0)
            down.cross(1)
        elif k == 2:
            down.forward(3)
            down.cross(2)
        else:
            down.cross(3)

    for s in range(slots):
        rows = slice(s * piece, (s + 1) * piece)
        total = R.xin[s].astype(F32)
        for z in range(4):
            ctx = R.ctxT[group * z : group * (z + 1), :, rows].reshape(q_cols, piece).T
            total = total + dot_t(ctx, weights(R, 0, z, slice(qkv_cols, width)))
        R.mid[rows, :] = total
        _, hat = norm_parts(total)
        R.na[rows, :] = (hat * R.gains[1:2, :]).astype(BF)
    R.nT[...] = R.na[...].T

    for k in range(4):
        up.finish(k)
        down.finish(k)
        for n in range(width // WIDE):
            cols = slice(n * WIDE, (n + 1) * WIDE)
            pre = dot(R.na[...], weights(R, 1, near[k], cols))
            phi = 0.5 + 0.5 * lax.erf(pre * SQRT_HALF)
            R.act[k, :, cols] = (pre * phi).astype(BF)
            R.slope[k, :, cols] = (phi + pre * (jnp.exp(-0.5 * pre * pre) * INV_SQRT_2PI)).astype(BF)
        part = dot_t(R.act[k], weights(R, 2, near[k], slice(0, width)))
        if k == 0:
            R.acc[...] = part
        else:
            R.acc[...] += part
    for s in range(slots):
        R.ob[s] = (R.mid[s * piece : (s + 1) * piece, :] + R.acc[s * piece : (s + 1) * piece, :]).astype(BF)
    for s in range(slots):
        move_grad.wait(s)
        R.gT[:, s * piece : (s + 1) * piece] = R.gin[s].T
    move_out = RowMove(place, links, R.ob, R.output)

    up_sum = Reduce(place, links, R.W.at[1], R.land.at[1], 0)
    down_sum = Reduce(place, links, R.W.at[2], R.land.at[2], 1)
    qkv_sum = Reduce(place, links, R.W.at[0], R.land.at[0], 0)
    for k in range(4):
        for n in range(width // WIDE):
            cols = slice(n * WIDE, (n + 1) * WIDE)
            back = dot(R.gin[...].reshape(span, width), weights(R, 2, near[k], cols))
            R.gp[:, cols] = (back * R.slope[k, :, cols].astype(F32)).astype(BF)
        part = dot_t(R.gp[...], weights(R, 1, near[k], slice(0, width)))
        if k == 0:
            R.gacc[...] = part
        else:
            R.gacc[...] += part
        up.release(k)
        R.W[1, near[k]] = dot(R.nT[...], R.gp[...]).astype(BF).reshape(R.W.shape[2:])
        up_sum.start(k)
        down.release(k)
        R.W[2, near[k]] = dot(R.gT[...], R.act[k]).astype(BF).reshape(R.W.shape[2:])
        down_sum.start(k)
        if k > 0:
            up_sum.core(k - 1)
            down_sum.core(k - 1)

    gain_two = jnp.zeros((1, width), F32)
    for s in range(slots):
        rows = slice(s * piece, (s + 1) * piece)
        inverse, hat = norm_parts(R.mid[rows, :])
        grad = R.gacc[rows, :]
        gain_two = gain_two + jnp.sum(grad * hat, axis=0, keepdims=True)
        scaled = grad * R.gains[1:2, :]
        shift = hat * jnp.mean(scaled * hat, axis=-1, keepdims=True)
        top = R.gin[s].astype(F32) + inverse * (scaled - shift)
        R.mid[rows, :] = top
        R.na[rows, :] = top.astype(BF)
    R.small[...] = jnp.zeros_like(R.small)
    R.small[1:2, :] = gain_two
    R.gT[...] = R.na[...].T
    up_sum.core(3)
    down_sum.core(3)
    for k in range(4):
        first.release(k)
    for z in range(4):
        turned = dot(R.na[...], weights(R, 0, z, slice(qkv_cols, width))).astype(BF).T
        for j in range(group):
            R.dOT[group * z + j] = turned[j * HEAD_DIM : (j + 1) * HEAD_DIM, :]
        part = dot_t(R.gT[...], R.ctxT[group * z : group * (z + 1)].reshape(q_cols, span)).astype(BF)
        R.W[0, z, :, :, :, qkv_cols:] = part.reshape(4, 2, width // 8, q_cols)
    for s in range(slots):
        _, hat = norm_parts(R.xin[s].astype(F32))
        R.nT[:, s * piece : (s + 1) * piece] = (hat * R.gains[0:1, :]).astype(BF).T

    def project_back(k):
        links.arrived(R.kv_in.at[heads_of(k)], k_back[k])
        parts = []
        for j in range(group):
            whole = R.kv_own[j] + R.kv_in[group * near[k] + j].astype(F32)
            parts.append(whole.astype(BF))
        for j in range(group):
            parts.append(R.dq[j])
        grads = jnp.concatenate(parts, axis=1)
        part = dot_t(grads, weights(R, 0, near[k], slice(0, qkv_cols)))
        if k == 3:
            R.gacc[...] = part
        else:
            R.gacc[...] += part
        made = dot(R.nT[...], grads).astype(BF)
        R.W[0, near[k], :, :, :, 0:qkv_cols] = made.reshape(4, 2, width // 8, qkv_cols)
        qkv_sum.start(k)

    k_back = {}
    for k in (3, 2, 1, 0):

        @pl.loop(0, group)
        def _(j):
            h = group * near[k] + j
            bwd_head(R, h, j, place.c, R.far_bias[h, 15], R.far_bias[h, 31])

        k_back[k] = links.send(R.kv_out.at[heads_of(k)], R.kv_in.at[heads_of(k)], place.to_c)
        if k == 3:
            for n in (0, 1):
                up_sum.plane(n)
                down_sum.plane(n)
        elif k == 2:
            for n in (2, 3):
                up_sum.plane(n)
                down_sum.plane(n)
            for n in (0, 1):
                up_sum.column(n)
                down_sum.column(n)
            qkv_sum.core(3)
        elif k == 1:
            for n in (2, 3):
                up_sum.column(n)
                down_sum.column(n)
            qkv_sum.plane(3)
            qkv_sum.core(2)
        else:
            up_sum.finish(R.gsum.at[1])
            down_sum.finish(R.gsum.at[2])
            qkv_sum.column(3)
            qkv_sum.plane(2)
            qkv_sum.core(1)
        project_back(k)
    gain_one = jnp.zeros((1, width), F32)
    for s in range(slots):
        rows = slice(s * piece, (s + 1) * piece)
        inverse, hat = norm_parts(R.xin[s].astype(F32))
        grad = R.gacc[rows, :]
        gain_one = gain_one + jnp.sum(grad * hat, axis=0, keepdims=True)
        scaled = grad * R.gains[0:1, :]
        shift = hat * jnp.mean(scaled * hat, axis=-1, keepdims=True)
        R.gin[s] = (R.mid[rows, :] + inverse * (scaled - shift)).astype(BF)
    move_back = RowMove(place, links, R.gin, R.grad_in)
    R.small[0:1, :] = gain_one

    at = links.send(R.small, R.small_in.at[0], place.to_c)
    qkv_sum.plane(1)
    links.arrived(R.small_in.at[0], at)
    R.small_in[0] = R.small_in[0] + R.small[...]
    at_small = links.take(3)
    for k, peer in enumerate((place.to_x, place.to_y, place.to_xy)):
        links.send(R.small_in.at[0], R.small_in.at[1 + k], peer, at_small + k)
    qkv_sum.core(0)
    qkv_sum.column(2)
    for k in range(3):
        links.arrived(R.small_in.at[1 + k], at_small + k)
    row = R.small_in[0] + R.small_in[1]
    other = R.small_in[2] + R.small_in[3]
    R.small_z[place.z] = row + other
    own = R.small_z.at[place.z]
    at_small = links.take(4)
    for k in (1, 2, 3):
        links.send(own, own, {"z": near[k]}, at_small + k, at_small + place.z)
    qkv_sum.plane(0)
    qkv_sum.column(1)
    for k in (1, 2, 3):
        links.arrived(R.small_z.at[near[k]], at_small + near[k])
    R.small_sum[...] = (R.small_z[0] + R.small_z[1]) + (R.small_z[2] + R.small_z[3])
    qkv_sum.column(0)
    qkv_sum.finish(R.gsum.at[0])
    for s in range(slots):
        move_out.wait(s)
        move_back.wait(s)
    links.left(0)


def wave_buckets():
    lane = np.arange(512)
    apart = np.where(lane < 128, -lane - 128, 384 - lane)
    far = np.abs(apart)
    bucket = np.where(far < 8, far, 8 + sum((far >= bound).astype(np.int32) for bound in FAR_BOUNDS))
    return bucket + np.where(apart > 0, 16, 0)


def on_moved(
    hidden_in,
    out_grad,
    seg_ids,
    row_len,
    slot_mask,
    mem_keys,
    mem_values,
    w_qkv,
    m_qkv,
    v_qkv,
    w_attn_out,
    m_attn_out,
    v_attn_out,
    w_up,
    m_up,
    v_up,
    w_down,
    m_down,
    v_down,
    gains,
    m_gains,
    v_gains,
    rel_table,
    m_rel,
    v_rel,
):
    rows, piece, width = hidden_in.shape
    seq = seg_ids.shape[1]
    span = seq // 2
    buckets, heads = rel_table.shape
    group = heads // 4
    shard = w_qkv.shape[1]
    w_down, m_down, v_down = w_down.T, m_down.T, v_down.T
    rel_table, m_rel, v_rel = rel_table.T, m_rel.T, v_rel.T
    hot = jnp.asarray(np.arange(buckets)[:, None] == wave_buckets()[None, :], F32)

    any_space = pl.BlockSpec(memory_space=pl.ANY)
    vmem = pl.BlockSpec(memory_space=pltpu.VMEM)
    smem = pl.BlockSpec(memory_space=pltpu.SMEM)
    keys = seq + KEY_PAD
    scratch = {
        "W": pltpu.VMEM((3, 4, 4, 2, shard, width), BF),
        "land": pltpu.VMEM((3, 4, 8, shard, width), BF),
        "KVT": pltpu.VMEM((heads, 128, keys), BF),
        "QT": pltpu.VMEM((heads, HEAD_DIM, span), BF),
        "ctxT": pltpu.VMEM((heads, HEAD_DIM, span), BF),
        "dOT": pltpu.VMEM((heads, HEAD_DIM, span), BF),
        "lse": pltpu.VMEM((16, span), F32),
        "xin": pltpu.VMEM((2, piece, width), BF),
        "gin": pltpu.VMEM((2, piece, width), BF),
        "ob": pltpu.VMEM((2, piece, width), BF),
        "na": pltpu.VMEM((span, width), BF),
        "nT": pltpu.VMEM((width, span), BF),
        "gT": pltpu.VMEM((width, span), BF),
        "act": pltpu.VMEM((4, span, width), BF),
        "slope": pltpu.VMEM((4, span, width), BF),
        "gp": pltpu.VMEM((span, width), BF),
        "mid": pltpu.VMEM((span, width), F32),
        "acc": pltpu.VMEM((span, width), F32),
        "gacc": pltpu.VMEM((span, width), F32),
        "kv_own": pltpu.VMEM((group, span, 128), F32),
        "kv_in": pltpu.VMEM((heads, span, 128), BF),
        "kv_out": pltpu.VMEM((heads, span, 128), BF),
        "dq": pltpu.VMEM((group, span, HEAD_DIM), BF),
        "S": pltpu.VMEM((seq + 32, WIDE), F32),
        "P": pltpu.VMEM((keys, WIDE), BF),
        "ka": pltpu.VMEM((128, keys), BF),
        "va": pltpu.VMEM((128, keys), BF),
        "Ka": pltpu.VMEM((keys, 128), BF),
        "Va": pltpu.VMEM((keys, 128), BF),
        "qa": pltpu.VMEM((128, span), BF),
        "da": pltpu.VMEM((128, span), BF),
        "band": pltpu.VMEM((384, 128), F32),
        "code": pltpu.VMEM((rows, 8, keys), F32),
        "packed": pltpu.VMEM((3, shard, width), BF),
        "mem": pltpu.VMEM((rows, group, 128, KEY_PAD), BF),
        "wave": pltpu.VMEM((16, 512), F32),
        "code_in": pltpu.VMEM((8, keys), F32),
        "small": pltpu.VMEM((16, width), F32),
        "small_in": pltpu.VMEM((4, 16, width), F32),
        "small_z": pltpu.VMEM((4, 16, width), F32),
        "send_sems": pltpu.SemaphoreType.DMA((LINK_SEMS,)),
        "recv_sems": pltpu.SemaphoreType.DMA((LINK_SEMS,)),
        "local_sems": pltpu.SemaphoreType.DMA((3,)),
    }
    operands = {
        "far_bias": (rel_table, smem),
        "rel_table": (rel_table, vmem),
        "row_len": (row_len, smem),
        "seg_ids": (seg_ids, vmem),
        "slot_mask": (slot_mask, vmem),
        "mem_keys": (mem_keys, vmem),
        "mem_values": (mem_values, vmem),
        "w_qkv": (w_qkv, vmem),
        "w_attn_out": (w_attn_out, vmem),
        "w_up": (w_up, vmem),
        "w_down": (w_down, vmem),
        "hot": (hot, vmem),
        "gains": (gains, vmem),
        "hidden": (hidden_in, any_space),
        "out_grad": (out_grad, any_space),
    }
    results = {
        "output": (jax.ShapeDtypeStruct(hidden_in.shape, BF), any_space),
        "grad_in": (jax.ShapeDtypeStruct(hidden_in.shape, BF), any_space),
        "gsum": (jax.ShapeDtypeStruct((3, shard, width), F32), vmem),
        "small_sum": (jax.ShapeDtypeStruct((16, width), F32), vmem),
    }
    names = [*operands, *results, *scratch]
    output, grad_input, gsum, small = pl.pallas_call(
        functools.partial(layer_kernel, names),
        out_shape=[shape for shape, _ in results.values()],
        in_specs=[spec for _, spec in operands.values()],
        out_specs=[spec for _, spec in results.values()],
        scratch_shapes=list(scratch.values()),
        compiler_params=pltpu.CompilerParams(
            collective_id=0, has_side_effects=True, vmem_limit_bytes=VMEM_LIMIT
        ),
    )(*[array for array, _ in operands.values()])
    inputs = {"output": output, "grad_in": grad_input, "gsum": gsum, "small": small, "hot": hot}
    results = {
        "output_out": jax.ShapeDtypeStruct(hidden_in.shape, BF),
        "grad_input": jax.ShapeDtypeStruct(hidden_in.shape, F32),
    }
    for name, w, m, v in (
        ("qkv", w_qkv, m_qkv, v_qkv),
        ("attn_out", w_attn_out, m_attn_out, v_attn_out),
        ("up", w_up, m_up, v_up),
        ("down", w_down, m_down, v_down),
        ("gains", gains, m_gains, v_gains),
        ("rel", rel_table, m_rel, v_rel),
    ):
        inputs |= {"w_" + name: w, "m_" + name: m, "v_" + name: v}
        kinds = ("new", "first", "second") if name in ("gains", "rel") else ("new", "first", "second", "copy")
        for kind in kinds:
            results[kind + "_" + name] = jax.ShapeDtypeStruct(w.shape, BF if kind == "copy" else F32)
    made = pl.pallas_call(
        functools.partial(update_kernel, [*inputs, *results]),
        out_shape=list(results.values()),
        in_specs=[vmem] * len(inputs),
        out_specs=[vmem] * len(results),
        compiler_params=pltpu.CompilerParams(vmem_limit_bytes=VMEM_LIMIT),
    )(*inputs.values())
    return tuple(array.T if name.endswith(("_down", "_rel")) else array for name, array in zip(results, made))


def solution(mesh):
    if dict(mesh.shape) == {"dp": 8, "mp": 4}:
        mesh = Mesh(mesh.devices.reshape(2, 2, 2, 4), ("y", "x", "c", "z"))
        return placed_on(mesh, on_moved, ("y", "x", "c"), "z")
    return placed_on(mesh, on_device, "dp", "mp")


def placed_on(mesh, body, dp, mp):
    placed = (
        P(dp, mp, None),
        P(dp, mp, None),
        P(dp, None),
        P(dp),
        P(dp, None),
        P(dp, None, mp),
        P(dp, None, mp),
        P(None, dp, mp),
        P(None, dp, mp),
        P(None, dp, mp),
        P(mp, dp),
        P(mp, dp),
        P(mp, dp),
        P(dp, mp),
        P(dp, mp),
        P(dp, mp),
        P(mp, dp),
        P(mp, dp),
        P(mp, dp),
        P(),
        P(),
        P(),
        P(),
        P(),
        P(),
    )
    return jax.shard_map(
        body,
        mesh=mesh,
        in_specs=placed,
        out_specs=(
            P(dp, mp, None),
            P(dp, mp, None),
            P(None, dp, mp),
            P(None, dp, mp),
            P(None, dp, mp),
            P(None, dp, mp),
            P(mp, dp),
            P(mp, dp),
            P(mp, dp),
            P(mp, dp),
            P(dp, mp),
            P(dp, mp),
            P(dp, mp),
            P(dp, mp),
            P(mp, dp),
            P(mp, dp),
            P(mp, dp),
            P(mp, dp),
            P(),
            P(),
            P(),
            P(),
            P(),
            P(),
        ),
        check_vma=False,
    )
```

```python
import functools

import jax
import jax.numpy as jnp
import numpy as np
from jax import lax
from jax.experimental import pallas as pl
from jax.experimental.pallas import tpu as pltpu
from jax.sharding import Mesh
from jax.sharding import PartitionSpec as P

HEAD_DIM = 64
STEP = 10


NORM_EPS = 1e-06
MOMENT_DECAY = 0.5
ADAM_EPS = 1e-08
MATRIX_RATE = 0.05
SMALL_RATE = 0.5
WEIGHT_DECAY = 0.01
FAR_BOUNDS = (12, 16, 23, 32, 46, 64, 91)
NEG_FILL = -1e30


def bucket_of(distance):
    far_dist = jnp.abs(distance)
    far_bucket = jnp.full(far_dist.shape, 8, jnp.int32)
    for far_bound in FAR_BOUNDS:
        far_bucket = far_bucket + (far_dist >= far_bound).astype(jnp.int32)
    one_side = jnp.where(far_dist < 8, far_dist, far_bucket)
    return one_side + jnp.where(distance > 0, 16, 0).astype(jnp.int32)


def gelu_exact(values):
    return jax.nn.gelu(values, approximate=False)


def rms_inverse(values):
    return lax.rsqrt(jnp.mean(values * values, axis=-1, keepdims=True) + NORM_EPS)


def norm_back(grad_out, normed_hat, inverse, gain_row):
    scaled = grad_out * gain_row
    return inverse * (scaled - normed_hat * jnp.mean(scaled * normed_hat, axis=-1, keepdims=True))


def adamw(weight, gradient, first_mom, second, step_rate, decay_rate):
    first_new = MOMENT_DECAY * first_mom + (1.0 - MOMENT_DECAY) * gradient
    second_new = MOMENT_DECAY * second + (1.0 - MOMENT_DECAY) * gradient * gradient
    bias_fix = 1.0 - MOMENT_DECAY**STEP
    update = first_new / bias_fix / (jnp.sqrt(second_new / bias_fix) + ADAM_EPS)
    return (weight - step_rate * (update + decay_rate * weight), first_new, second_new)


def row_masks(seg_row, length, pair_on):
    positions = jnp.arange(seg_row.shape[0], dtype=jnp.int32)
    is_live = positions < length
    doc_group = jnp.where(is_live, seg_row, -1).astype(jnp.int32)
    slot_on = jnp.repeat(pair_on, 2) > 0
    return (is_live[:, None] & slot_on[None, :], doc_group[:, None] == doc_group[None, :])


def block_scores(q_block, mk_row, k_row, mem_ok, tok_ok, bias_block, score_scale):
    mem_raw = (
        jnp.einsum("hqe,hke->hqk", q_block, mk_row, preferred_element_type=jnp.float32)
        * score_scale
    )
    tok_raw = (
        jnp.einsum("hqe,hke->hqk", q_block, k_row, preferred_element_type=jnp.float32) * score_scale
        + bias_block
    )
    return (jnp.where(mem_ok[None], mem_raw, NEG_FILL), jnp.where(tok_ok[None], tok_raw, NEG_FILL))


def on_device(
    hidden_in,
    out_grad,
    seg_ids,
    row_len,
    slot_mask,
    mem_keys,
    mem_values,
    w_qkv,
    m_qkv,
    v_qkv,
    w_attn_out,
    m_attn_out,
    v_attn_out,
    w_up,
    m_up,
    v_up,
    w_down,
    m_down,
    v_down,
    gains,
    m_gains,
    v_gains,
    rel_table,
    m_rel,
    v_rel,
):
    qkv_low, attn_out_low, up_low, down_low = (
        lax.all_gather(w_qkv.astype(jnp.bfloat16), "dp", axis=1, tiled=True),
        lax.all_gather(w_attn_out.astype(jnp.bfloat16), "dp", axis=1, tiled=True),
        lax.all_gather(w_up.astype(jnp.bfloat16), "dp", axis=0, tiled=True),
        lax.all_gather(w_down.astype(jnp.bfloat16), "dp", axis=1, tiled=True),
    )
    row_count = hidden_in.shape[0]
    seq_span = seg_ids.shape[1]
    bucket_total, head_total = rel_table.shape
    head_local = head_total // lax.axis_size("mp")
    head_size = HEAD_DIM
    model_width = gains.shape[1]
    slots = mem_keys.shape[1]
    score_scale = head_size ** (-0.5)
    block_rows = min(512, seq_span)
    mp_index = lax.axis_index("mp")
    positions = jnp.arange(seq_span, dtype=jnp.int32)
    bucket_grid = bucket_of(positions[None, :] - positions[:, None])
    table_local = lax.dynamic_slice_in_dim(rel_table, mp_index * head_local, head_local, 1)
    rel_bias = jnp.zeros((head_local, seq_span, seq_span), jnp.float32)
    for bucket_number in range(bucket_total):
        rel_bias = rel_bias + jnp.where(
            (bucket_grid == bucket_number)[None], table_local[bucket_number][:, None, None], 0.0
        )
    qkv_heads = qkv_low.reshape(3, model_width, head_local, head_size)
    attn_out_heads = attn_out_low.reshape(head_local, head_size, model_width)
    inputs = hidden_in.astype(jnp.float32)
    inverse_one = rms_inverse(inputs)
    hat_one = inputs * inverse_one
    normed_one = (hat_one * gains[0]).astype(jnp.bfloat16)
    normed_full = lax.all_gather(normed_one, "mp", axis=1, tiled=True)
    project = jnp.einsum(
        "rsd,cdhe->crhse", normed_full, qkv_heads, preferred_element_type=jnp.float32
    ).astype(jnp.bfloat16)
    queries, key_new, value_new = (project[0], project[1], project[2])
    mem_key_rows = jnp.transpose(
        mem_keys.reshape(row_count, slots, head_local, head_size), (0, 2, 1, 3)
    )
    mem_value_rows = jnp.transpose(
        mem_values.reshape(row_count, slots, head_local, head_size), (0, 2, 1, 3)
    )

    def forward_row(packed):
        q_row, k_row, v_row, mk_row, mv_row, seg_row, length, pair_on = packed
        mem_allowed, tok_allowed = row_masks(seg_row, length, pair_on)
        contexts = []
        maxima = []
        for first_row in range(0, seq_span, block_rows):
            last_row = first_row + block_rows
            mem_s, tok_s = block_scores(
                q_row[:, first_row:last_row],
                mk_row,
                k_row,
                mem_allowed[first_row:last_row],
                tok_allowed[first_row:last_row],
                rel_bias[:, first_row:last_row],
                score_scale,
            )
            row_peak = jnp.maximum(
                jnp.max(mem_s, axis=-1, keepdims=True), jnp.max(tok_s, axis=-1, keepdims=True)
            )
            mem_exp = jnp.exp(mem_s - row_peak)
            tok_exp = jnp.exp(tok_s - row_peak)
            exp_total = jnp.sum(mem_exp, axis=-1, keepdims=True) + jnp.sum(
                tok_exp, axis=-1, keepdims=True
            )
            mem_prob = (mem_exp / exp_total).astype(jnp.bfloat16)
            tok_prob = (tok_exp / exp_total).astype(jnp.bfloat16)
            block_context = jnp.einsum(
                "hqk,hke->hqe", mem_prob, mv_row, preferred_element_type=jnp.float32
            )
            block_context = block_context + jnp.einsum(
                "hqk,hke->hqe", tok_prob, v_row, preferred_element_type=jnp.float32
            )
            contexts.append(block_context.astype(jnp.bfloat16))
            maxima.append((row_peak + jnp.log(exp_total))[:, :, 0])
        return (jnp.concatenate(contexts, axis=1), jnp.concatenate(maxima, axis=1))

    context, log_totals = lax.map(
        forward_row,
        (queries, key_new, value_new, mem_key_rows, mem_value_rows, seg_ids, row_len, slot_mask),
    )
    attn_term = jnp.einsum(
        "rhse,hed->rsd", context, attn_out_heads, preferred_element_type=jnp.float32
    )
    attn_local = lax.psum_scatter(attn_term, "mp", scatter_dimension=1, tiled=True)
    mid = inputs + attn_local
    inverse_two = rms_inverse(mid)
    hat_two = mid * inverse_two
    normed_two = (hat_two * gains[1]).astype(jnp.bfloat16)
    ffn_source = lax.all_gather(normed_two, "mp", axis=1, tiled=True)
    up_full, down_full = (up_low, down_low)
    pre_act = jnp.einsum("rsd,df->rsf", ffn_source, up_full, preferred_element_type=jnp.float32)
    act_value, act_back = jax.vjp(gelu_exact, pre_act)
    act_low = act_value.astype(jnp.bfloat16)
    ffn_term = jnp.einsum("rsf,fd->rsd", act_low, down_full, preferred_element_type=jnp.float32)
    ffn_local = lax.psum_scatter(
        ffn_term.astype(jnp.bfloat16), "mp", scatter_dimension=1, tiled=True
    ).astype(jnp.float32)
    output = (mid + ffn_local).astype(jnp.bfloat16)
    grad_top = out_grad.astype(jnp.float32)
    grad_source = lax.all_gather(out_grad, "mp", axis=1, tiled=True)
    down_grad = jnp.einsum("rsf,rsd->fd", act_low, grad_source, preferred_element_type=jnp.float32)
    grad_act = jnp.einsum("rsd,fd->rsf", grad_source, down_full, preferred_element_type=jnp.float32)
    grad_pre = act_back(grad_act)[0].astype(jnp.bfloat16)
    up_grad = jnp.einsum("rsd,rsf->df", ffn_source, grad_pre, preferred_element_type=jnp.float32)
    grad_normed_part = jnp.einsum(
        "rsf,df->rsd", grad_pre, up_full, preferred_element_type=jnp.float32
    )
    grad_normed_two = lax.psum_scatter(grad_normed_part, "mp", scatter_dimension=1, tiled=True)
    gain_two_grad = jnp.sum(grad_normed_two * hat_two, axis=(0, 1))
    grad_mid = grad_top + norm_back(grad_normed_two, hat_two, inverse_two, gains[1])
    grad_mid_low = grad_mid.astype(jnp.bfloat16)
    grad_attn_full = lax.all_gather(grad_mid_low, "mp", axis=1, tiled=True)
    attn_out_grad = jnp.einsum(
        "rhse,rsd->hed", context, grad_attn_full, preferred_element_type=jnp.float32
    )
    attn_out_grad = attn_out_grad.reshape(head_local * head_size, model_width)
    grad_context = jnp.einsum(
        "rsd,hed->rhse", grad_attn_full, attn_out_heads, preferred_element_type=jnp.float32
    ).astype(jnp.bfloat16)

    def backward_row(bias_total, packed):
        q_row, k_row, v_row, mk_row, mv_row, seg_row, length, pair_on, lse_row, grad_row = packed
        mem_allowed, tok_allowed = row_masks(seg_row, length, pair_on)
        key_acc = jnp.zeros(k_row.shape, jnp.float32)
        value_acc = jnp.zeros(v_row.shape, jnp.float32)
        query_parts = []
        bias_parts = []
        for first_row in range(0, seq_span, block_rows):
            last_row = first_row + block_rows
            q_block = q_row[:, first_row:last_row]
            mem_s, tok_s = block_scores(
                q_block,
                mk_row,
                k_row,
                mem_allowed[first_row:last_row],
                tok_allowed[first_row:last_row],
                rel_bias[:, first_row:last_row],
                score_scale,
            )
            lse_block = lse_row[:, first_row:last_row, None]
            mem_prob = jnp.exp(mem_s - lse_block)
            tok_prob = jnp.exp(tok_s - lse_block)
            grad_block = grad_row[:, first_row:last_row]
            mem_gprob = jnp.einsum(
                "hqe,hke->hqk", grad_block, mv_row, preferred_element_type=jnp.float32
            )
            tok_gprob = jnp.einsum(
                "hqe,hke->hqk", grad_block, v_row, preferred_element_type=jnp.float32
            )
            row_dot = jnp.sum(mem_prob * mem_gprob, axis=-1, keepdims=True) + jnp.sum(
                tok_prob * tok_gprob, axis=-1, keepdims=True
            )
            mem_gscore = (mem_prob * (mem_gprob - row_dot)).astype(jnp.bfloat16)
            tok_gscore = (tok_prob * (tok_gprob - row_dot)).astype(jnp.bfloat16)
            query_grad = jnp.einsum(
                "hqk,hke->hqe", mem_gscore, mk_row, preferred_element_type=jnp.float32
            )
            query_grad = query_grad + jnp.einsum(
                "hqk,hke->hqe", tok_gscore, k_row, preferred_element_type=jnp.float32
            )
            query_parts.append((query_grad * score_scale).astype(jnp.bfloat16))
            key_acc = key_acc + jnp.einsum(
                "hqk,hqe->hke", tok_gscore, q_block, preferred_element_type=jnp.float32
            )
            value_acc = value_acc + jnp.einsum(
                "hqk,hqe->hke",
                tok_prob.astype(jnp.bfloat16),
                grad_block,
                preferred_element_type=jnp.float32,
            )
            bias_parts.append(tok_gscore.astype(jnp.float32))
        bias_total = bias_total + jnp.concatenate(bias_parts, axis=1)
        row_grads = (
            jnp.concatenate(query_parts, axis=1),
            (key_acc * score_scale).astype(jnp.bfloat16),
            value_acc.astype(jnp.bfloat16),
        )
        return (bias_total, row_grads)

    bias_grad, (grad_q, grad_k, grad_v) = lax.scan(
        backward_row,
        jnp.zeros((head_local, seq_span, seq_span), jnp.float32),
        (
            queries,
            key_new,
            value_new,
            mem_key_rows,
            mem_value_rows,
            seg_ids,
            row_len,
            slot_mask,
            log_totals,
            grad_context,
        ),
    )
    grad_project = jnp.stack([grad_q, grad_k, grad_v])
    qkv_grad = jnp.einsum(
        "rsd,crhse->cdhe", normed_full, grad_project, preferred_element_type=jnp.float32
    )
    qkv_grad = qkv_grad.reshape(3, model_width, head_local * head_size)
    grad_normed_term = jnp.einsum(
        "crhse,cdhe->rsd", grad_project, qkv_heads, preferred_element_type=jnp.float32
    )
    grad_normed_one = lax.psum_scatter(
        grad_normed_term.astype(jnp.bfloat16), "mp", scatter_dimension=1, tiled=True
    ).astype(jnp.float32)
    gain_one_grad = jnp.sum(grad_normed_one * hat_one, axis=(0, 1))
    grad_input = grad_mid + norm_back(grad_normed_one, hat_one, inverse_one, gains[0])
    bucket_sums = []
    for bucket_number in range(bucket_total):
        bucket_sums.append(
            jnp.sum(jnp.where((bucket_grid == bucket_number)[None], bias_grad, 0.0), axis=(1, 2))
        )
    table_local_grad = jnp.stack(bucket_sums)
    table_grad = lax.dynamic_update_slice(
        jnp.zeros((bucket_total, head_total), jnp.float32),
        table_local_grad,
        (jnp.int32(0), mp_index * head_local),
    )
    gains_grad, table_grad = lax.psum(
        (jnp.stack([gain_one_grad, gain_two_grad]), table_grad), ("dp", "mp")
    )
    qkv_sum, attn_out_sum, up_sum, down_sum = (
        lax.psum_scatter(qkv_grad, "dp", scatter_dimension=1, tiled=True),
        lax.psum_scatter(attn_out_grad, "dp", scatter_dimension=1, tiled=True),
        lax.psum_scatter(up_grad, "dp", scatter_dimension=0, tiled=True),
        lax.psum_scatter(down_grad, "dp", scatter_dimension=1, tiled=True),
    )
    qkv_new, qkv_first, qkv_second = adamw(w_qkv, qkv_sum, m_qkv, v_qkv, MATRIX_RATE, WEIGHT_DECAY)
    attn_out_new, attn_out_first, attn_out_second = adamw(
        w_attn_out, attn_out_sum, m_attn_out, v_attn_out, MATRIX_RATE, WEIGHT_DECAY
    )
    up_new, up_first, up_second = adamw(w_up, up_sum, m_up, v_up, MATRIX_RATE, WEIGHT_DECAY)
    down_new, down_first, down_second = adamw(
        w_down, down_sum, m_down, v_down, MATRIX_RATE, WEIGHT_DECAY
    )
    gains_new, gains_first, gains_second = adamw(
        gains, gains_grad, m_gains, v_gains, SMALL_RATE, 0.0
    )
    rel_new, rel_first, rel_second = adamw(rel_table, table_grad, m_rel, v_rel, SMALL_RATE, 0.0)
    return (
        output,
        grad_input,
        qkv_new,
        qkv_first,
        qkv_second,
        qkv_new.astype(jnp.bfloat16),
        attn_out_new,
        attn_out_first,
        attn_out_second,
        attn_out_new.astype(jnp.bfloat16),
        up_new,
        up_first,
        up_second,
        up_new.astype(jnp.bfloat16),
        down_new,
        down_first,
        down_second,
        down_new.astype(jnp.bfloat16),
        gains_new,
        gains_first,
        gains_second,
        rel_new,
        rel_first,
        rel_second,
    )


BF = jnp.bfloat16
F32 = jnp.float32
MESH_ID = pl.DeviceIdType.MESH
BIG = 1e30
KEY_PAD = 128
WIDE = 256
KEY_STEP, QUERY_STEP = 256, 512
SQRT_HALF = 0.5**0.5
INV_SQRT_2PI = 0.3989422804014327
LINK_SEMS = 162
VMEM_LIMIT = 63 * 2**20


def dot(a, b):
    return lax.dot_general(a, b, (((1,), (0,)), ((), ())), preferred_element_type=F32)


def dot_t(a, b):
    return lax.dot_general(a, b, (((1,), (1,)), ((), ())), preferred_element_type=F32)


def split3(v):
    hi = v.astype(BF)
    rest = v - hi.astype(F32)
    mid = rest.astype(BF)
    low = (rest - mid.astype(F32)).astype(BF)
    return hi, mid, low


class Links:
    def __init__(self, send_sems, recv_sems):
        self.send_sems, self.recv_sems = send_sems, recv_sems
        self.count = 0
        self.sent = []

    def take(self, n=1):
        self.count += n
        return self.count - n

    def send(self, src, dst, device, send_at=None, recv_at=None, when=None, else_keep=False):
        at = self.take() if send_at is None else send_at
        recv_at = at if recv_at is None else recv_at
        copy = pltpu.make_async_remote_copy(
            src, dst, self.send_sems.at[at], self.recv_sems.at[recv_at], device_id=device, device_id_type=MESH_ID
        )
        if when is None:
            copy.start()
        else:

            @pl.when(when)
            def _():
                copy.start()

            if else_keep:

                @pl.when(jnp.logical_not(when))
                def _():
                    pltpu.make_async_copy(src, dst, self.recv_sems.at[recv_at]).start()

        self.sent.append((copy, when))
        return at

    def arrived(self, dst, k):
        pltpu.make_async_copy(dst, dst, self.recv_sems.at[k]).wait()

    def left(self, since, until=None):
        for n in range(since, len(self.sent) if until is None else until):
            if self.sent[n] is None:
                continue
            copy, when = self.sent[n]
            if when is None:
                copy.wait_send()
            else:
                pl.when(when)(copy.wait_send)
            self.sent[n] = None


class Place:
    def __init__(self):
        self.y, self.x = lax.axis_index("y"), lax.axis_index("x")
        self.c, self.z = lax.axis_index("c"), lax.axis_index("z")
        self.to_x, self.to_y = {"x": 1 - self.x}, {"y": 1 - self.y}
        self.to_c, self.to_xy = {"c": 1 - self.c}, {"x": 1 - self.x, "y": 1 - self.y}
        z = self.z
        self.near = (z, z + 1 - 2 * lax.rem(z, 2), jnp.where(z < 2, 2, 1), jnp.where(z < 2, 3, 0))
        self.inner = (z == 1) | (z == 2)

    def greet(self):
        barrier = pltpu.get_barrier_semaphore()
        peers = [self.to_x, self.to_y, self.to_c, self.to_xy]
        for z in self.near[1:]:
            peers.append({"z": z})
            peers.append({"z": z, "c": 1 - self.c})
        for peer in peers:
            pl.semaphore_signal(barrier, inc=1, device_id=peer, device_id_type=MESH_ID)
        self.greeted = len(peers)

    def meet(self):
        pl.semaphore_wait(pltpu.get_barrier_semaphore(), self.greeted)


class Gather:
    def __init__(self, place, links, shard, whole, local_sem):
        self.p, self.links, self.shard, self.whole, self.local_sem = place, links, shard, whole, local_sem
        self.at_z = links.take(4)
        self.k_x, self.k_y, self.k_d, self.k_c = {}, {}, {}, {}
        self.out = {k: [] for k in range(4)}

    def spot(self, k, y, x):
        return self.whole.at[self.p.near[k], y, x, self.p.c]

    def send(self, k, *args, **kwargs):
        self.out[k].append(len(self.links.sent))
        return self.links.send(*args, **kwargs)

    def start_z(self):
        p = self.p
        own = self.spot(0, p.y, p.x)
        for k in (2, 1, 3):
            self.links.send(
                self.shard, own, {"z": p.near[k]}, self.at_z + k, self.at_z + p.z, p.inner if k == 3 else None
            )

    def start_own(self):
        p = self.p
        own = self.spot(0, p.y, p.x)
        self.own_copy = pltpu.make_async_copy(self.shard, own, self.local_sem)
        self.own_copy.start()
        self.k_x[0] = self.links.send(self.shard, own, p.to_x)
        self.k_y[0] = self.links.send(self.shard, own, p.to_y)

    def column(self, k):
        p = self.p
        block = self.spot(k, p.y, p.x)
        self.links.arrived(block, self.at_z + p.near[k])
        self.k_x[k] = self.send(k, block, block, p.to_x)
        self.k_y[k] = self.send(k, block, block, p.to_y)
        if k == 3:
            self.send(3, block, block, {"z": p.near[1]}, self.at_z, self.at_z + p.near[3], p.inner)

    def forward(self, k):
        p = self.p
        from_x, from_y = self.spot(k, p.y, 1 - p.x), self.spot(k, 1 - p.y, p.x)
        if k % 2 == 0:
            self.links.arrived(from_x, self.k_x[k])
            self.k_d[k] = self.send(k, from_x, from_x, p.to_y)
            self.links.arrived(from_y, self.k_y[k])
        else:
            self.links.arrived(from_y, self.k_y[k])
            self.k_d[k] = self.send(k, from_y, from_y, p.to_x)
            self.links.arrived(from_x, self.k_x[k])

    def cross(self, k):
        p = self.p
        self.links.arrived(self.spot(k, 1 - p.y, 1 - p.x), self.k_d[k])
        if k == 0:
            self.own_copy.wait()
        half = self.whole.at[p.near[k], :, :, p.c]
        self.k_c[k] = self.send(k, half, half, p.to_c)

    def finish(self, k):
        p = self.p
        self.links.arrived(self.whole.at[p.near[k], :, :, 1 - p.c], self.k_c[k])

    def release(self, k):
        for n in self.out[k]:
            self.links.left(n, n + 1)


class Reduce:
    def __init__(self, place, links, grads, land):
        self.p, self.links, self.g = place, links, grads
        self.land_c, self.land_p, self.land_q, self.land_z = land
        half = grads.shape[4] // 2
        self.upper, self.lower = slice(0, half), slice(half, 2 * half)
        self.at, self.at_z = {}, links.take(4)

    def start(self, k):
        p = self.p
        self.at[k] = [self.links.send(self.g.at[p.near[k], :, :, 1 - p.c], self.land_c.at[k], p.to_c)]

    def add(self, at, part):
        self.g[at] = self.g[at] + part

    def core(self, k):
        p, links, block = self.p, self.links, self.p.near[k]
        every = slice(None)
        links.arrived(self.land_c.at[k], self.at[k][0])
        away_x, away_y = (every, 1 - p.x), (1 - p.y, every)
        stay_x, stay_y = (every, p.x), (p.y, every)
        for n, (there, rows, peer) in enumerate(((away_x, self.upper, p.to_x), (away_y, self.lower, p.to_y))):
            self.add((block, *there, p.c, rows), self.land_c[(k, *there, rows)])
            self.at[k].append(links.send(self.g.at[(block, *there, p.c, rows)], self.land_p.at[k, n], peer))
        for there, rows in ((stay_x, self.upper), (stay_y, self.lower)):
            self.add((block, *there, p.c, rows), self.land_c[(k, *there, rows)])

    def plane(self, k):
        p, links, block = self.p, self.links, self.p.near[k]
        every = slice(None)
        steps = (
            ((every, p.x), self.upper, (1 - p.y, p.x), p.to_y),
            ((p.y, every), self.lower, (p.y, 1 - p.x), p.to_x),
        )
        for n, (stay, rows, away, peer) in enumerate(steps):
            links.arrived(self.land_p.at[k, n], self.at[k][1 + n])
            self.add((block, *stay, p.c, rows), self.land_p[k, n])
            self.at[k].append(links.send(self.g.at[(block, *away, p.c, rows)], self.land_q.at[k, n], peer))

    def column(self, k):
        p, links = self.p, self.links
        here = (p.near[k], p.y, p.x, p.c)
        for n, rows in enumerate((self.upper, self.lower)):
            links.arrived(self.land_q.at[k, n], self.at[k][3 + n])
            self.add((*here, rows), self.land_q[k, n])
        if k == 0:
            return
        target, spot = p.near[k], p.z
        if k == 3:
            @pl.when(p.inner)
            def _():
                links.arrived(self.land_z.at[p.z], self.at_z + p.z)
                self.add(here, self.land_z[p.z])

            target = jnp.where(p.inner, p.near[3], p.near[1])
            spot = jnp.where(p.inner, p.z, p.near[1])
        links.send(self.g.at[here], self.land_z.at[spot], {"z": target}, self.at_z + k, self.at_z + spot)

    def finish(self, out):
        p = self.p
        total = self.g[p.z, p.y, p.x, p.c].astype(F32)
        for k in (1, 2):
            source = p.near[k]
            self.links.arrived(self.land_z.at[source], self.at_z + source)
            total = total + self.land_z[source].astype(F32)
        out[...] = total

        @pl.when(p.inner)
        def _():
            source = p.near[3]
            self.links.arrived(self.land_z.at[source], self.at_z + source)
            out[...] += self.land_z[source].astype(F32)


def near_third(key, block):
    if key < 4:
        return (key - block + 1, None) if abs(key - block) <= 1 else None
    if block == 3 and key == 4:
        return (2, 0)
    if block == 0 and key == 7:
        return (0, 1)
    return None


def near_tiles(keys, queries):
    tiles = []
    for row in range(0, keys.stop - keys.start, 128):
        for col in range(0, queries.stop - queries.start, 128):
            found = near_third((keys.start + row) // 128, (queries.start + col) // 128)
            if found is not None:
                tiles.append((row, col, *found))
    return tiles


def add_band(s, band, keys, queries, core):
    tiles = {(row, col): (third, need) for row, col, third, need in near_tiles(keys, queries)}
    rows = []
    for row in range(0, s.shape[0], 128):
        cols = []
        for col in range(0, s.shape[1], 128):
            part = s[row : row + 128, col : col + 128]
            if (row, col) in tiles:
                third, need = tiles[row, col]
                near = band[third * 128 : (third + 1) * 128, :]
                if need is not None:
                    near = near * jnp.where(core == need, 1.0, 0.0)
                part = part + near
            cols.append(part)
        rows.append(jnp.concatenate(cols, axis=1))
    return jnp.concatenate(rows, axis=0)


def far_masks(core, span):
    key = lax.broadcasted_iota(jnp.int32, (8, span), 0)
    block = lax.broadcasted_iota(jnp.int32, (8, span), 1) // 128
    other = key - 4
    left = ((key < 4) & (key <= block - 2)) | ((key >= 4) & (core == 1) & ~((block == 0) & (other == 3)))
    right = ((key < 4) & (key >= block + 2)) | ((key >= 4) & (core == 0) & ~((block == 3) & (other == 0)))
    return left, right


def rows_of(parts, span):
    row = lax.broadcasted_iota(jnp.int32, (8, span), 0)
    out = jnp.zeros((8, span), F32)
    for n, part in enumerate(parts):
        out = jnp.where(row == n, part.astype(F32), out)
    return out.astype(BF)


def far_rows(left, right, far_left, far_right):
    hi, mid, low = split3(jnp.where(left, far_left, jnp.where(right, far_right, 0.0)))
    return jnp.concatenate([hi.astype(F32), mid.astype(F32), low.astype(F32)], axis=0).astype(BF)


def fwd_head(R, h, core, far_left, far_right):
    span, keys = R.QT.shape[2], R.KVT.shape[2]
    toks = keys - KEY_PAD
    R.ka[0:64, :] = R.KVT[h, 0:64, :]
    R.Ka[...] = R.ka[...].T
    R.va[0:64, :] = R.KVT[h, 64:128, :]
    R.qa[0:64, :] = R.QT[h]
    left, right = far_masks(core, span)
    R.qa[80:104, :] = far_rows(left, right, far_left, far_right)
    R.band[...] = band_of(R.wave[pl.ds(h, 1), :])
    band = R.band
    last = slice(toks, toks + 32)
    for left_col in range(0, span, QUERY_STEP):
        cols = slice(left_col, left_col + QUERY_STEP)
        query = R.qa[:, cols]
        peak = None
        for first in range(0, toks, KEY_STEP):
            rows = slice(first, first + KEY_STEP)
            s = add_band(dot(R.Ka[rows, :], query), band, rows, cols, core)
            R.S[rows, :] = s
            top = jnp.max(s, axis=0, keepdims=True)
            peak = top if peak is None else jnp.maximum(peak, top)
        s = dot(R.Ka[last, :], query)
        R.S[last, :] = s
        peak = jnp.maximum(peak, jnp.max(s, axis=0, keepdims=True))
        for first in range(0, toks, KEY_STEP):
            rows = slice(first, first + KEY_STEP)
            R.P[rows, :] = jnp.exp(R.S[rows, :] - peak).astype(BF)
        R.P[last, :] = jnp.exp(R.S[last, :] - peak).astype(BF)
        o = dot(R.va[0:72, :], R.P[...])
        total = o[64:65, :]
        R.ctxT[h, :, cols] = (o[0:64, :] * (1.0 / total)).astype(BF)
        R.lse[pl.ds(h, 1), cols] = peak + jnp.log(total)


def bwd_head(R, h, j, core, far_left, far_right):
    span, keys = R.QT.shape[2], R.KVT.shape[2]
    toks = keys - KEY_PAD
    R.ka[0:64, :] = R.KVT[h, 0:64, :]
    R.Ka[...] = R.ka[...].T
    R.va[0:64, :] = R.KVT[h, 64:128, :]
    R.Va[...] = R.va[...].T
    R.qa[0:64, :] = R.QT[h]
    left, right = far_masks(core, span)
    R.qa[80:104, :] = far_rows(left, right, far_left, far_right)
    R.qa[72:80, :] = rows_of(split3(-R.lse[pl.ds(h, 1), :]), span)
    grad = R.dOT[h]
    R.da[0:64, :] = grad
    row_dot = jnp.sum(grad.astype(F32) * R.ctxT[h].astype(F32), axis=0, keepdims=True)
    R.da[64:72, :] = rows_of(split3(-row_dot), span)
    R.band[...] = band_of(R.wave[pl.ds(h, 1), :])
    band = R.band
    query_sum = {}
    near = [None, None, None]
    for first in range(0, toks + 1, KEY_STEP):
        is_mem = first == toks
        rows = slice(toks, toks + 32) if is_mem else slice(first, first + KEY_STEP)
        key_sum = value_sum = None
        for left_col in range(0, span, QUERY_STEP):
            cols = slice(left_col, left_col + QUERY_STEP)
            s = dot(R.Ka[rows, :], R.qa[:, cols])
            if not is_mem:
                s = add_band(s, band, rows, cols, core)
            p = jnp.exp(s)
            ds = p * dot(R.Va[rows, :], R.da[:, cols])
            ds_low = ds.astype(BF)
            if is_mem:
                filled = jnp.concatenate([ds_low, jnp.zeros((KEY_PAD - 32, QUERY_STEP), BF)], axis=0)
                part = dot(R.ka[0:96, toks:keys], filled)
            else:
                v = dot_t(p.astype(BF), R.da[0:64, cols])
                k = dot_t(ds_low, R.qa[0:64, cols])
                value_sum = v if value_sum is None else value_sum + v
                key_sum = k if key_sum is None else key_sum + k
                for row, col, third, need in near_tiles(rows, cols):
                    t = ds[row : row + 128, col : col + 128]
                    if need is not None:
                        t = t * jnp.where(core == need, 1.0, 0.0)
                    near[third] = t if near[third] is None else near[third] + t
                part = dot(R.ka[0:96, rows], ds_low)
            query_sum[left_col] = part if left_col not in query_sum else query_sum[left_col] + part
        if not is_mem:
            both = jnp.concatenate([key_sum, value_sum], axis=1)
            if first < span:
                R.kv_own[j, rows, :] = both
            else:
                R.kv_out[h, slice(first - span, first - span + KEY_STEP), :] = both.astype(BF)
    turned = jnp.concatenate(list(query_sum.values()), axis=1)
    R.dq[j] = (turned[0:64, :] * HEAD_DIM**-0.5).T.astype(BF)
    far = turned[80:88, :]
    lane = lax.broadcasted_iota(jnp.int32, (1, 128), 1)
    sum_left = jnp.sum(jnp.where(left, far, 0.0))
    sum_right = jnp.sum(jnp.where(right, far, 0.0))
    ends = jnp.where(lane == 0, sum_left, jnp.where(lane == 1, sum_right, 0.0))
    R.small[pl.ds(2 + h, 1), 0:640] = jnp.concatenate([unband(jnp.concatenate(near, axis=0)), ends], axis=1)


class Refs:
    def __init__(self, **refs):
        self.__dict__.update(refs)


def weights(R, n, z, cols):
    part = R.W[n, z, :, :, :, :, cols]
    return part.reshape(-1, part.shape[4])


class RowMove:
    def __init__(self, place, links, src, dst):
        self.links, self.dst = links, dst
        slot = lax.rem(place.z, 2)
        self.at = links.take(2)
        for i in (0, 1):
            target_z, target_c = 2 * place.c + i, place.z // 2
            links.send(
                src.at[i],
                dst.at[slot],
                {"c": target_c, "z": target_z},
                self.at + i,
                self.at + slot,
                (target_c != place.c) | (target_z != place.z),
                else_keep=True,
            )

    def wait(self, slot):
        self.links.arrived(self.dst.at[slot], self.at + slot)


def norm_parts(values):
    inverse = lax.rsqrt(jnp.mean(values * values, axis=-1, keepdims=True) + NORM_EPS)
    return inverse, values * inverse


def mask_rows(R, place):
    span, keys = R.QT.shape[2], R.KVT.shape[2]
    toks = keys - KEY_PAD
    mine = jnp.where(place.z // 2 == place.c, R.code[lax.rem(place.z, 2)], R.code_in[...])
    R.code_in[...] = mine
    own = R.code_in[:, pl.ds(pl.multiple_of(place.c * span, span), span)]
    other = R.code_in[:, pl.ds(pl.multiple_of((1 - place.c) * span, span), span)]
    line = jnp.concatenate([own, other, R.code_in[:, toks:keys]], axis=1)
    row = lax.broadcasted_iota(jnp.int32, (8, keys), 0)
    as_doc = (row - 1).astype(F32)
    kind = jnp.where(row < 5, jnp.where(line == as_doc, 1.0, 0.0), 0.0)
    kind = jnp.where((row == 5) & (line == 11.0), 1.0, kind)
    kind = jnp.where((row == 6) & (line >= 10.0), 1.0, kind)
    R.ka[64:72, :] = kind.astype(BF)
    R.ka[72:80, :] = jnp.where(row < 3, 1.0, 0.0).astype(BF)
    block = lax.broadcasted_iota(jnp.int32, (8, keys), 1) // 128
    hot = jnp.where((block == row) & (block < toks // 128), 1.0, 0.0)
    R.ka[80:104, :] = jnp.concatenate([hot, hot, hot], axis=0).astype(BF)
    R.ka[104:128, :] = jnp.zeros((24, keys), BF)
    R.va[64:72, :] = jnp.where(row < 3, 1.0, 0.0).astype(BF)
    R.va[72:128, :] = jnp.zeros((56, keys), BF)
    qrow = lax.broadcasted_iota(jnp.int32, (8, span), 0)
    hide = jnp.where((qrow < 5) & (own != (qrow - 1).astype(F32)), -BIG, 0.0)
    hide = jnp.where(qrow == 5, -BIG, hide)
    hide = jnp.where((qrow == 6) & (own == -1.0), -BIG, hide)
    R.qa[64:72, :] = hide.astype(BF)
    R.qa[72:128, :] = jnp.zeros((56, span), BF)
    R.da[64:128, :] = jnp.zeros((64, span), BF)
    R.P[toks + 32 : keys, :] = jnp.zeros((KEY_PAD - 32, QUERY_STEP), BF)


def band_of(wave):
    spread = jnp.broadcast_to(wave, (128, 512))
    parts = [pltpu.roll(spread, 128 * n, 1, stride=1, stride_axis=0)[:, 0:128] for n in range(3)]
    return jnp.concatenate(parts, axis=0)


def unband(near):
    empty = jnp.zeros((8, 128), F32)
    total = None
    for n in range(16):
        part = jnp.concatenate(
            [near[8 * n : 8 * n + 8], empty, near[256 + 8 * n : 264 + 8 * n], near[128 + 8 * n : 136 + 8 * n]], axis=1
        )
        if n:
            part = pltpu.roll(part, 512 - 8 * n, 1)
        total = part if total is None else total + part
    row = lax.broadcasted_iota(jnp.int32, (8, 512), 0)
    out = jnp.zeros((8, 512), F32)
    for n in range(8):
        out = out + jnp.where(row == n, total if n == 0 else pltpu.roll(total, 512 - n, 1), 0.0)
    return jnp.sum(out, axis=0, keepdims=True)


def prepare(R):
    rows, seq = R.seg_ids.shape
    slots, heads_wide = R.mem_keys.shape[1:]
    group = heads_wide // HEAD_DIM
    R.KVT[:, :, seq : seq + KEY_PAD] = jnp.zeros((R.KVT.shape[0], 128, KEY_PAD), BF)
    parts = []
    for j in range(group):
        cols = slice(j * HEAD_DIM, (j + 1) * HEAD_DIM)
        parts += [R.w_qkv[1, :, cols], R.w_qkv[2, :, cols]]
    parts += [R.w_qkv[0], R.w_attn_out[...].T]
    R.packed[0] = jnp.concatenate(parts, axis=1).astype(BF)
    R.packed[1] = R.w_up[...].astype(BF)
    R.packed[2] = R.w_down[...].astype(BF)
    place = lax.broadcasted_iota(jnp.int32, (1, seq), 1)
    pair = lax.broadcasted_iota(jnp.int32, (slots // 2, KEY_PAD), 0)
    lane = lax.broadcasted_iota(jnp.int32, (slots // 2, KEY_PAD), 1)
    spread = jnp.where(lane // 2 == pair, 1.0, 0.0)
    on = dot(jnp.where(R.slot_mask[...] > 0, 1.0, 0.0), spread)
    for r in range(rows):
        R.mem[r, 0:slots, :] = R.mem_keys[r]
        R.mem[r, slots : 2 * slots, :] = R.mem_values[r]
        docs = jnp.where(place < R.row_len[r], R.seg_ids[r : r + 1, :], -1).astype(F32)
        R.code[r, :, 0:seq] = jnp.broadcast_to(docs, (8, seq))
        R.code[r, :, seq : seq + KEY_PAD] = jnp.broadcast_to(jnp.where(on[r : r + 1] > 0.5, 10.0, 11.0), (8, KEY_PAD))
    heads = R.rel_table.shape[0]
    made = lax.dot_general(
        R.rel_table[...],
        R.hot[...],
        (((1,), (0,)), ((), ())),
        precision=lax.Precision.HIGHEST,
        preferred_element_type=F32,
    )
    R.wave[0:heads, :] = made


def update_kernel(names, *refs):
    R = Refs(**dict(zip(names, refs)))
    group = R.w_qkv.shape[2] // HEAD_DIM
    kv_cols, qkv_cols = group * 128, group * 192
    R.output_out[...] = R.output[...]
    R.grad_input[...] = R.grad_in[...].astype(F32)

    def step(name, gradient, at=Ellipsis, rate=MATRIX_RATE, decay=WEIGHT_DECAY, copy=True):
        ref = lambda kind: getattr(R, kind + "_" + name)
        new, first, second = adamw(ref("w")[at], gradient, ref("m")[at], ref("v")[at], rate, decay)
        ref("new")[at] = new
        ref("first")[at] = first
        ref("second")[at] = second
        if copy:
            ref("copy")[at] = new.astype(BF)

    sums = R.gsum[0]
    step("qkv", sums[:, kv_cols:qkv_cols], 0)
    for n in (0, 1):
        parts = [sums[:, j * 128 + n * 64 : j * 128 + n * 64 + HEAD_DIM] for j in range(group)]
        step("qkv", jnp.concatenate(parts, axis=1), 1 + n)
    step("attn_out", sums[:, qkv_cols:].T)
    step("up", R.gsum[1])
    step("down", R.gsum[2])
    step("gains", R.small[0:2, :], rate=SMALL_RATE, decay=0.0, copy=False)
    heads = R.w_rel.shape[0]
    along = lax.dot_general(
        R.small[2 : 2 + heads, 0:512],
        R.hot[...],
        (((1,), (1,)), ((), ())),
        precision=lax.Precision.HIGHEST,
        preferred_element_type=F32,
    )
    bucket = lax.broadcasted_iota(jnp.int32, along.shape, 1)
    ends = R.small[2 : 2 + heads, 512:640]
    along = along + jnp.where(bucket == 15, ends[:, 0:1], 0.0) + jnp.where(bucket == 31, ends[:, 1:2], 0.0)
    step("rel", along, rate=SMALL_RATE, decay=0.0, copy=False)


def layer_kernel(names, *refs):
    R = Refs(**dict(zip(names, refs)))
    place = Place()
    links = Links(R.send_sems, R.recv_sems)
    place.greet()
    prepare(R)
    place.meet()
    heads, span = R.QT.shape[0], R.QT.shape[2]
    width = R.xin.shape[2]
    group = heads // 4
    kv_cols, q_cols = group * 128, group * HEAD_DIM
    qkv_cols = kv_cols + q_cols
    slots = R.xin.shape[0]
    piece = R.xin.shape[1]

    near = place.near
    first, up, down = gather = [Gather(place, links, R.packed.at[n], R.W.at[n], R.local_sems.at[n]) for n in range(3)]
    first.start_z()
    first.start_own()
    up.start_z()
    up.start_own()
    down.start_own()
    k_code = links.send(R.code.at[lax.rem(place.z, 2)], R.code_in, place.to_c)
    at_mem = links.take(4)
    mem_spot = R.mem_in.at[place.z]
    for r in (0, 1):
        for c in (0, 1):
            links.send(
                R.mem.at[r],
                mem_spot,
                {"c": c, "z": 2 * place.c + r},
                at_mem + 2 * r + c,
                at_mem + place.z,
                (place.c != c) | (place.z != 2 * place.c + r),
                else_keep=True,
            )
    for k in (1, 2, 3):
        first.column(k)
    move_in = RowMove(place, links, R.hidden, R.xin)
    for k in range(4):
        first.forward(k)
    links.arrived(R.code_in, k_code)
    mask_rows(R, place)
    for k in (1, 2, 3):
        up.column(k)
    for k in range(4):
        first.cross(k)
    up.forward(0)
    up.forward(1)
    down.start_z()
    for s in range(slots):
        move_in.wait(s)
        _, hat = norm_parts(R.xin[s].astype(F32))
        R.na[s * piece : (s + 1) * piece, :] = (hat * R.gains[0:1, :]).astype(BF)

    def heads_of(k):
        return pl.ds(group * near[k], group)

    k_kv = []
    for k in range(4):
        first.finish(k)
        low = dot(R.na[...], weights(R, 0, near[k], slice(0, qkv_cols))).astype(BF)
        for j in range(group):
            R.KVT[group * near[k] + j, :, 0:span] = low[:, j * 128 : (j + 1) * 128].T
        turned = (low[:, kv_cols:qkv_cols].astype(F32) * HEAD_DIM**-0.5).astype(BF).T
        for j in range(group):
            R.QT[group * near[k] + j] = turned[j * HEAD_DIM : (j + 1) * HEAD_DIM, :]
        block = heads_of(k)
        k_kv.append(links.send(R.KVT.at[block, :, 0:span], R.KVT.at[block, :, span : 2 * span], place.to_c))
    up.forward(2)
    up.forward(3)
    move_grad = RowMove(place, links, R.out_grad, R.gin)
    for k in range(4):
        up.cross(k)

    for k in range(4):
        block = heads_of(k)
        links.arrived(R.KVT.at[block, :, span : 2 * span], k_kv[k])
        links.arrived(R.mem_in.at[near[k]], at_mem + near[k])
        slots_in = R.mem_in.shape[1] // 2
        turned = R.mem_in[near[k]].astype(F32).T.astype(BF)
        for j in range(group):
            for n in (0, 1):
                R.KVT[group * near[k] + j, n * HEAD_DIM : (n + 1) * HEAD_DIM, 2 * span : 2 * span + slots_in] = turned[
                    j * HEAD_DIM : (j + 1) * HEAD_DIM, n * slots_in : (n + 1) * slots_in
                ]

        @pl.loop(0, group)
        def _(j):
            h = group * near[k] + j
            fwd_head(R, h, place.c, R.far_bias[h, 15], R.far_bias[h, 31])

        if k == 0:
            for n in (1, 2, 3):
                down.column(n)
        elif k == 1:
            down.forward(0)
            down.forward(1)
        elif k == 2:
            down.forward(2)
            down.cross(0)
        else:
            down.forward(3)
            down.cross(1)

    for s in range(slots):
        rows = slice(s * piece, (s + 1) * piece)
        total = R.xin[s].astype(F32)
        for z in range(4):
            ctx = R.ctxT[group * z : group * (z + 1), :, rows].reshape(q_cols, piece).T
            total = total + dot_t(ctx, weights(R, 0, z, slice(qkv_cols, width)))
        R.mid[rows, :] = total
        _, hat = norm_parts(total)
        R.na[rows, :] = (hat * R.gains[1:2, :]).astype(BF)
    R.nT[...] = R.na[...].T

    for s in range(slots):
        move_grad.wait(s)
        R.gT[:, s * piece : (s + 1) * piece] = R.gin[s].T
    land = [[ref.at[n] for ref in (R.land_c, R.land_p, R.land_q, R.land_z)] for n in range(3)]
    qkv_sum, up_sum, down_sum = [Reduce(place, links, R.W.at[n], land[n]) for n in range(3)]
    down.cross(2)
    down.cross(3)
    for k in (3, 2, 1, 0):
        up.finish(k)
        down.finish(k)
        for n in range(width // WIDE):
            cols = slice(n * WIDE, (n + 1) * WIDE)
            pre = dot(R.na[...], weights(R, 1, near[k], cols))
            back = dot(R.gin[...].reshape(span, width), weights(R, 2, near[k], cols))
            phi = 0.5 + 0.5 * lax.erf(pre * SQRT_HALF)
            R.act[:, cols] = (pre * phi).astype(BF)
            slope = phi + pre * (jnp.exp(-0.5 * pre * pre) * INV_SQRT_2PI)
            R.gp[:, cols] = (back * slope).astype(BF)
        out_part = dot_t(R.act[...], weights(R, 2, near[k], slice(0, width)))
        back_part = dot_t(R.gp[...], weights(R, 1, near[k], slice(0, width)))
        if k == 3:
            R.acc[...] = out_part
            R.gacc[...] = back_part
        else:
            R.acc[...] += out_part
            R.gacc[...] += back_part
        up.release(k)
        R.W[1, near[k]] = dot(R.nT[...], R.gp[...]).astype(BF).reshape(R.W.shape[2:])
        up_sum.start(k)
        down.release(k)
        R.W[2, near[k]] = dot(R.gT[...], R.act[...]).astype(BF).reshape(R.W.shape[2:])
        down_sum.start(k)
        if k < 3:
            up_sum.core(k + 1)
            down_sum.core(k + 1)
    up_sum.plane(3)
    down_sum.plane(3)
    for s in range(slots):
        R.ob[s] = (R.mid[s * piece : (s + 1) * piece, :] + R.acc[s * piece : (s + 1) * piece, :]).astype(BF)
    move_out = RowMove(place, links, R.ob, R.output)

    gain_two = jnp.zeros((1, width), F32)
    for s in range(slots):
        rows = slice(s * piece, (s + 1) * piece)
        inverse, hat = norm_parts(R.mid[rows, :])
        grad = R.gacc[rows, :]
        gain_two = gain_two + jnp.sum(grad * hat, axis=0, keepdims=True)
        scaled = grad * R.gains[1:2, :]
        shift = hat * jnp.mean(scaled * hat, axis=-1, keepdims=True)
        top = R.gin[s].astype(F32) + inverse * (scaled - shift)
        R.mid[rows, :] = top
        R.na[rows, :] = top.astype(BF)
    R.small[...] = jnp.zeros_like(R.small)
    R.small[1:2, :] = gain_two
    R.gT[...] = R.na[...].T
    up_sum.core(0)
    down_sum.core(0)
    for k in range(4):
        first.release(k)
    for z in range(4):
        turned = dot(R.na[...], weights(R, 0, z, slice(qkv_cols, width))).astype(BF).T
        for j in range(group):
            R.dOT[group * z + j] = turned[j * HEAD_DIM : (j + 1) * HEAD_DIM, :]
        part = dot_t(R.gT[...], R.ctxT[group * z : group * (z + 1)].reshape(q_cols, span)).astype(BF)
        R.W[0, z, :, :, :, :, qkv_cols:] = part.reshape(2, 2, 2, width // 8, q_cols)
    for s in range(slots):
        _, hat = norm_parts(R.xin[s].astype(F32))
        R.nT[:, s * piece : (s + 1) * piece] = (hat * R.gains[0:1, :]).astype(BF).T

    def project_back(k):
        links.arrived(R.kv_in.at[heads_of(k)], k_back[k])
        parts = []
        for j in range(group):
            whole = R.kv_own[j] + R.kv_in[group * near[k] + j].astype(F32)
            parts.append(whole.astype(BF))
        for j in range(group):
            parts.append(R.dq[j])
        grads = jnp.concatenate(parts, axis=1)
        part = dot_t(grads, weights(R, 0, near[k], slice(0, qkv_cols)))
        if k == 3:
            R.gacc[...] = part
        else:
            R.gacc[...] += part
        if k == 0:
            rows_back()
        made = dot(R.nT[...], grads).astype(BF)
        R.W[0, near[k], :, :, :, :, 0:qkv_cols] = made.reshape(2, 2, 2, width // 8, qkv_cols)
        qkv_sum.start(k)

    def rows_back():
        gain_one = jnp.zeros((1, width), F32)
        for s in range(slots):
            rows = slice(s * piece, (s + 1) * piece)
            inverse, hat = norm_parts(R.xin[s].astype(F32))
            grad = R.gacc[rows, :]
            gain_one = gain_one + jnp.sum(grad * hat, axis=0, keepdims=True)
            scaled = grad * R.gains[0:1, :]
            shift = hat * jnp.mean(scaled * hat, axis=-1, keepdims=True)
            R.gin[s] = (R.mid[rows, :] + inverse * (scaled - shift)).astype(BF)
        moves.append(RowMove(place, links, R.gin, R.grad_in))
        R.small[0:1, :] = gain_one

    moves = []
    def both(stage, n):
        return [(up_sum, stage, n), (down_sum, stage, n)]

    ticks = (
        both("plane", 2) + both("column", 3),
        both("plane", 1) + both("column", 2),
        both("plane", 0) + both("column", 1) + [(qkv_sum, "core", 3)],
        both("column", 0),
        [(qkv_sum, "core", 2), (qkv_sum, "plane", 3)],
        [(up_sum, "finish", R.gsum.at[1]), (down_sum, "finish", R.gsum.at[2])],
        [(qkv_sum, "core", 1), (qkv_sum, "plane", 2), (qkv_sum, "column", 3)],
        [(qkv_sum, "plane", 1), (qkv_sum, "column", 2)],
    )
    k_back = {}
    for k in (3, 2, 1, 0):

        for part, bounds in enumerate(((0, 1), (1, group))):

            @pl.loop(*bounds)
            def _(j):
                h = group * near[k] + j
                bwd_head(R, h, j, place.c, R.far_bias[h, 15], R.far_bias[h, 31])

            if part == 1:
                k_back[k] = links.send(R.kv_out.at[heads_of(k)], R.kv_in.at[heads_of(k)], place.to_c)
            for chunk, stage, n in ticks[2 * (3 - k) + part]:
                getattr(chunk, stage)(n)
        project_back(k)

    at = links.send(R.small, R.small_in.at[0], place.to_c)
    links.arrived(R.small_in.at[0], at)
    R.small_in[0] = R.small_in[0] + R.small[...]
    at_small = links.take(3)
    for k, peer in enumerate((place.to_x, place.to_y, place.to_xy)):
        links.send(R.small_in.at[0], R.small_in.at[1 + k], peer, at_small + k)
    qkv_sum.core(0)
    for k in range(3):
        links.arrived(R.small_in.at[1 + k], at_small + k)
    row = R.small_in[0] + R.small_in[1]
    other = R.small_in[2] + R.small_in[3]
    R.small_z[place.z] = row + other
    own = R.small_z.at[place.z]
    at_small = links.take(4)
    for k in (1, 2, 3):
        links.send(own, own, {"z": near[k]}, at_small + k, at_small + place.z)
    qkv_sum.plane(0)
    qkv_sum.column(1)
    for k in (1, 2, 3):
        links.arrived(R.small_z.at[near[k]], at_small + near[k])
    R.small_sum[...] = (R.small_z[0] + R.small_z[1]) + (R.small_z[2] + R.small_z[3])
    qkv_sum.column(0)
    qkv_sum.finish(R.gsum.at[0])
    for s in range(slots):
        move_out.wait(s)
        moves[0].wait(s)
    links.left(0)


def wave_buckets():
    lane = np.arange(512)
    apart = np.where(lane < 128, -lane - 128, 384 - lane)
    far = np.abs(apart)
    bucket = np.where(far < 8, far, 8 + sum((far >= bound).astype(np.int32) for bound in FAR_BOUNDS))
    return bucket + np.where(apart > 0, 16, 0)


def on_moved(
    hidden_in,
    out_grad,
    seg_ids,
    row_len,
    slot_mask,
    mem_keys,
    mem_values,
    w_qkv,
    m_qkv,
    v_qkv,
    w_attn_out,
    m_attn_out,
    v_attn_out,
    w_up,
    m_up,
    v_up,
    w_down,
    m_down,
    v_down,
    gains,
    m_gains,
    v_gains,
    rel_table,
    m_rel,
    v_rel,
):
    rows, piece, width = hidden_in.shape
    seq = seg_ids.shape[1]
    span = seq // 2
    buckets, heads = rel_table.shape
    group = heads // 4
    shard = w_qkv.shape[1]
    w_down, m_down, v_down = w_down.T, m_down.T, v_down.T
    rel_table, m_rel, v_rel = rel_table.T, m_rel.T, v_rel.T
    hot = jnp.asarray(np.arange(buckets)[:, None] == wave_buckets()[None, :], F32)

    any_space = pl.BlockSpec(memory_space=pl.ANY)
    vmem = pl.BlockSpec(memory_space=pltpu.VMEM)
    smem = pl.BlockSpec(memory_space=pltpu.SMEM)
    keys = seq + KEY_PAD
    scratch = {
        "W": pltpu.VMEM((3, 4, 2, 2, 2, shard, width), BF),
        "land_c": pltpu.VMEM((3, 4, 2, 2, shard, width), BF),
        "land_p": pltpu.VMEM((3, 4, 2, 2, shard // 2, width), BF),
        "land_q": pltpu.VMEM((3, 4, 2, shard // 2, width), BF),
        "land_z": pltpu.VMEM((3, 4, shard, width), BF),
        "KVT": pltpu.VMEM((heads, 128, keys), BF),
        "QT": pltpu.VMEM((heads, HEAD_DIM, span), BF),
        "ctxT": pltpu.VMEM((heads, HEAD_DIM, span), BF),
        "dOT": pltpu.VMEM((heads, HEAD_DIM, span), BF),
        "lse": pltpu.VMEM((16, span), F32),
        "xin": pltpu.VMEM((2, piece, width), BF),
        "gin": pltpu.VMEM((2, piece, width), BF),
        "ob": pltpu.VMEM((2, piece, width), BF),
        "na": pltpu.VMEM((span, width), BF),
        "nT": pltpu.VMEM((width, span), BF),
        "gT": pltpu.VMEM((width, span), BF),
        "act": pltpu.VMEM((span, width), BF),
        "gp": pltpu.VMEM((span, width), BF),
        "mid": pltpu.VMEM((span, width), F32),
        "acc": pltpu.VMEM((span, width), F32),
        "gacc": pltpu.VMEM((span, width), F32),
        "kv_own": pltpu.VMEM((group, span, 128), F32),
        "kv_in": pltpu.VMEM((heads, span, 128), BF),
        "kv_out": pltpu.VMEM((heads, span, 128), BF),
        "dq": pltpu.VMEM((group, span, HEAD_DIM), BF),
        "S": pltpu.VMEM((seq + 32, QUERY_STEP), F32),
        "P": pltpu.VMEM((keys, QUERY_STEP), BF),
        "ka": pltpu.VMEM((128, keys), BF),
        "va": pltpu.VMEM((128, keys), BF),
        "Ka": pltpu.VMEM((keys, 128), BF),
        "Va": pltpu.VMEM((keys, 128), BF),
        "qa": pltpu.VMEM((128, span), BF),
        "da": pltpu.VMEM((128, span), BF),
        "band": pltpu.VMEM((384, 128), F32),
        "code": pltpu.VMEM((rows, 8, keys), F32),
        "packed": pltpu.VMEM((3, shard, width), BF),
        "mem": pltpu.VMEM((rows, 2 * mem_keys.shape[1], group * HEAD_DIM), BF),
        "mem_in": pltpu.VMEM((4, 2 * mem_keys.shape[1], group * HEAD_DIM), BF),
        "wave": pltpu.VMEM((16, 512), F32),
        "code_in": pltpu.VMEM((8, keys), F32),
        "small": pltpu.VMEM((16, width), F32),
        "small_in": pltpu.VMEM((4, 16, width), F32),
        "small_z": pltpu.VMEM((4, 16, width), F32),
        "send_sems": pltpu.SemaphoreType.DMA((LINK_SEMS,)),
        "recv_sems": pltpu.SemaphoreType.DMA((LINK_SEMS,)),
        "local_sems": pltpu.SemaphoreType.DMA((3,)),
    }
    operands = {
        "far_bias": (rel_table, smem),
        "rel_table": (rel_table, vmem),
        "row_len": (row_len, smem),
        "seg_ids": (seg_ids, vmem),
        "slot_mask": (slot_mask, vmem),
        "mem_keys": (mem_keys, vmem),
        "mem_values": (mem_values, vmem),
        "w_qkv": (w_qkv, vmem),
        "w_attn_out": (w_attn_out, vmem),
        "w_up": (w_up, vmem),
        "w_down": (w_down, vmem),
        "hot": (hot, vmem),
        "gains": (gains, vmem),
        "hidden": (hidden_in, any_space),
        "out_grad": (out_grad, any_space),
    }
    results = {
        "output": (jax.ShapeDtypeStruct(hidden_in.shape, BF), any_space),
        "grad_in": (jax.ShapeDtypeStruct(hidden_in.shape, BF), any_space),
        "gsum": (jax.ShapeDtypeStruct((3, shard, width), F32), vmem),
        "small_sum": (jax.ShapeDtypeStruct((16, width), F32), vmem),
    }
    names = [*operands, *results, *scratch]
    output, grad_input, gsum, small = pl.pallas_call(
        functools.partial(layer_kernel, names),
        out_shape=[shape for shape, _ in results.values()],
        in_specs=[spec for _, spec in operands.values()],
        out_specs=[spec for _, spec in results.values()],
        scratch_shapes=list(scratch.values()),
        compiler_params=pltpu.CompilerParams(
            collective_id=0, has_side_effects=True, vmem_limit_bytes=VMEM_LIMIT
        ),
    )(*[array for array, _ in operands.values()])
    inputs = {"output": output, "grad_in": grad_input, "gsum": gsum, "small": small, "hot": hot}
    results = {
        "output_out": jax.ShapeDtypeStruct(hidden_in.shape, BF),
        "grad_input": jax.ShapeDtypeStruct(hidden_in.shape, F32),
    }
    for name, w, m, v in (
        ("qkv", w_qkv, m_qkv, v_qkv),
        ("attn_out", w_attn_out, m_attn_out, v_attn_out),
        ("up", w_up, m_up, v_up),
        ("down", w_down, m_down, v_down),
        ("gains", gains, m_gains, v_gains),
        ("rel", rel_table, m_rel, v_rel),
    ):
        inputs |= {"w_" + name: w, "m_" + name: m, "v_" + name: v}
        kinds = ("new", "first", "second") if name in ("gains", "rel") else ("new", "first", "second", "copy")
        for kind in kinds:
            results[kind + "_" + name] = jax.ShapeDtypeStruct(w.shape, BF if kind == "copy" else F32)
    made = pl.pallas_call(
        functools.partial(update_kernel, [*inputs, *results]),
        out_shape=list(results.values()),
        in_specs=[vmem] * len(inputs),
        out_specs=[vmem] * len(results),
        compiler_params=pltpu.CompilerParams(vmem_limit_bytes=VMEM_LIMIT),
    )(*inputs.values())
    return tuple(array.T if name.endswith(("_down", "_rel")) else array for name, array in zip(results, made))


def solution(mesh):
    if dict(mesh.shape) == {"dp": 8, "mp": 4}:
        mesh = Mesh(mesh.devices.reshape(2, 2, 2, 4), ("y", "x", "c", "z"))
        return placed_on(mesh, on_moved, ("y", "x", "c"), "z")
    return placed_on(mesh, on_device, "dp", "mp")


def placed_on(mesh, body, dp, mp):
    placed = (
        P(dp, mp, None),
        P(dp, mp, None),
        P(dp, None),
        P(dp),
        P(dp, None),
        P(dp, None, mp),
        P(dp, None, mp),
        P(None, dp, mp),
        P(None, dp, mp),
        P(None, dp, mp),
        P(mp, dp),
        P(mp, dp),
        P(mp, dp),
        P(dp, mp),
        P(dp, mp),
        P(dp, mp),
        P(mp, dp),
        P(mp, dp),
        P(mp, dp),
        P(),
        P(),
        P(),
        P(),
        P(),
        P(),
    )
    return jax.shard_map(
        body,
        mesh=mesh,
        in_specs=placed,
        out_specs=(
            P(dp, mp, None),
            P(dp, mp, None),
            P(None, dp, mp),
            P(None, dp, mp),
            P(None, dp, mp),
            P(None, dp, mp),
            P(mp, dp),
            P(mp, dp),
            P(mp, dp),
            P(mp, dp),
            P(dp, mp),
            P(dp, mp),
            P(dp, mp),
            P(dp, mp),
            P(mp, dp),
            P(mp, dp),
            P(mp, dp),
            P(mp, dp),
            P(),
            P(),
            P(),
            P(),
            P(),
            P(),
        ),
        check_vma=False,
    )
```

```python
import functools

import jax
import jax.numpy as jnp
import numpy as np
from jax import lax
from jax.experimental import pallas as pl
from jax.experimental.pallas import tpu as pltpu
from jax.sharding import Mesh
from jax.sharding import PartitionSpec as P

HEAD_DIM = 64
STEP = 10


NORM_EPS = 1e-06
MOMENT_DECAY = 0.5
ADAM_EPS = 1e-08
MATRIX_RATE = 0.05
SMALL_RATE = 0.5
WEIGHT_DECAY = 0.01
FAR_BOUNDS = (12, 16, 23, 32, 46, 64, 91)
NEG_FILL = -1e30


def bucket_of(distance):
    far_dist = jnp.abs(distance)
    far_bucket = jnp.full(far_dist.shape, 8, jnp.int32)
    for far_bound in FAR_BOUNDS:
        far_bucket = far_bucket + (far_dist >= far_bound).astype(jnp.int32)
    one_side = jnp.where(far_dist < 8, far_dist, far_bucket)
    return one_side + jnp.where(distance > 0, 16, 0).astype(jnp.int32)


def gelu_exact(values):
    return jax.nn.gelu(values, approximate=False)


def rms_inverse(values):
    return lax.rsqrt(jnp.mean(values * values, axis=-1, keepdims=True) + NORM_EPS)


def norm_back(grad_out, normed_hat, inverse, gain_row):
    scaled = grad_out * gain_row
    return inverse * (scaled - normed_hat * jnp.mean(scaled * normed_hat, axis=-1, keepdims=True))


def adamw(weight, gradient, first_mom, second, step_rate, decay_rate):
    first_new = MOMENT_DECAY * first_mom + (1.0 - MOMENT_DECAY) * gradient
    second_new = MOMENT_DECAY * second + (1.0 - MOMENT_DECAY) * gradient * gradient
    bias_fix = 1.0 - MOMENT_DECAY**STEP
    update = first_new / bias_fix / (jnp.sqrt(second_new / bias_fix) + ADAM_EPS)
    return (weight - step_rate * (update + decay_rate * weight), first_new, second_new)


def row_masks(seg_row, length, pair_on):
    positions = jnp.arange(seg_row.shape[0], dtype=jnp.int32)
    is_live = positions < length
    doc_group = jnp.where(is_live, seg_row, -1).astype(jnp.int32)
    slot_on = jnp.repeat(pair_on, 2) > 0
    return (is_live[:, None] & slot_on[None, :], doc_group[:, None] == doc_group[None, :])


def block_scores(q_block, mk_row, k_row, mem_ok, tok_ok, bias_block, score_scale):
    mem_raw = (
        jnp.einsum("hqe,hke->hqk", q_block, mk_row, preferred_element_type=jnp.float32)
        * score_scale
    )
    tok_raw = (
        jnp.einsum("hqe,hke->hqk", q_block, k_row, preferred_element_type=jnp.float32) * score_scale
        + bias_block
    )
    return (jnp.where(mem_ok[None], mem_raw, NEG_FILL), jnp.where(tok_ok[None], tok_raw, NEG_FILL))


def on_device(
    hidden_in,
    out_grad,
    seg_ids,
    row_len,
    slot_mask,
    mem_keys,
    mem_values,
    w_qkv,
    m_qkv,
    v_qkv,
    w_attn_out,
    m_attn_out,
    v_attn_out,
    w_up,
    m_up,
    v_up,
    w_down,
    m_down,
    v_down,
    gains,
    m_gains,
    v_gains,
    rel_table,
    m_rel,
    v_rel,
):
    qkv_low, attn_out_low, up_low, down_low = (
        lax.all_gather(w_qkv.astype(jnp.bfloat16), "dp", axis=1, tiled=True),
        lax.all_gather(w_attn_out.astype(jnp.bfloat16), "dp", axis=1, tiled=True),
        lax.all_gather(w_up.astype(jnp.bfloat16), "dp", axis=0, tiled=True),
        lax.all_gather(w_down.astype(jnp.bfloat16), "dp", axis=1, tiled=True),
    )
    row_count = hidden_in.shape[0]
    seq_span = seg_ids.shape[1]
    bucket_total, head_total = rel_table.shape
    head_local = head_total // lax.axis_size("mp")
    head_size = HEAD_DIM
    model_width = gains.shape[1]
    slots = mem_keys.shape[1]
    score_scale = head_size ** (-0.5)
    block_rows = min(512, seq_span)
    mp_index = lax.axis_index("mp")
    positions = jnp.arange(seq_span, dtype=jnp.int32)
    bucket_grid = bucket_of(positions[None, :] - positions[:, None])
    table_local = lax.dynamic_slice_in_dim(rel_table, mp_index * head_local, head_local, 1)
    rel_bias = jnp.zeros((head_local, seq_span, seq_span), jnp.float32)
    for bucket_number in range(bucket_total):
        rel_bias = rel_bias + jnp.where(
            (bucket_grid == bucket_number)[None], table_local[bucket_number][:, None, None], 0.0
        )
    qkv_heads = qkv_low.reshape(3, model_width, head_local, head_size)
    attn_out_heads = attn_out_low.reshape(head_local, head_size, model_width)
    inputs = hidden_in.astype(jnp.float32)
    inverse_one = rms_inverse(inputs)
    hat_one = inputs * inverse_one
    normed_one = (hat_one * gains[0]).astype(jnp.bfloat16)
    normed_full = lax.all_gather(normed_one, "mp", axis=1, tiled=True)
    project = jnp.einsum(
        "rsd,cdhe->crhse", normed_full, qkv_heads, preferred_element_type=jnp.float32
    ).astype(jnp.bfloat16)
    queries, key_new, value_new = (project[0], project[1], project[2])
    mem_key_rows = jnp.transpose(
        mem_keys.reshape(row_count, slots, head_local, head_size), (0, 2, 1, 3)
    )
    mem_value_rows = jnp.transpose(
        mem_values.reshape(row_count, slots, head_local, head_size), (0, 2, 1, 3)
    )

    def forward_row(packed):
        q_row, k_row, v_row, mk_row, mv_row, seg_row, length, pair_on = packed
        mem_allowed, tok_allowed = row_masks(seg_row, length, pair_on)
        contexts = []
        maxima = []
        for first_row in range(0, seq_span, block_rows):
            last_row = first_row + block_rows
            mem_s, tok_s = block_scores(
                q_row[:, first_row:last_row],
                mk_row,
                k_row,
                mem_allowed[first_row:last_row],
                tok_allowed[first_row:last_row],
                rel_bias[:, first_row:last_row],
                score_scale,
            )
            row_peak = jnp.maximum(
                jnp.max(mem_s, axis=-1, keepdims=True), jnp.max(tok_s, axis=-1, keepdims=True)
            )
            mem_exp = jnp.exp(mem_s - row_peak)
            tok_exp = jnp.exp(tok_s - row_peak)
            exp_total = jnp.sum(mem_exp, axis=-1, keepdims=True) + jnp.sum(
                tok_exp, axis=-1, keepdims=True
            )
            mem_prob = (mem_exp / exp_total).astype(jnp.bfloat16)
            tok_prob = (tok_exp / exp_total).astype(jnp.bfloat16)
            block_context = jnp.einsum(
                "hqk,hke->hqe", mem_prob, mv_row, preferred_element_type=jnp.float32
            )
            block_context = block_context + jnp.einsum(
                "hqk,hke->hqe", tok_prob, v_row, preferred_element_type=jnp.float32
            )
            contexts.append(block_context.astype(jnp.bfloat16))
            maxima.append((row_peak + jnp.log(exp_total))[:, :, 0])
        return (jnp.concatenate(contexts, axis=1), jnp.concatenate(maxima, axis=1))

    context, log_totals = lax.map(
        forward_row,
        (queries, key_new, value_new, mem_key_rows, mem_value_rows, seg_ids, row_len, slot_mask),
    )
    attn_term = jnp.einsum(
        "rhse,hed->rsd", context, attn_out_heads, preferred_element_type=jnp.float32
    )
    attn_local = lax.psum_scatter(attn_term, "mp", scatter_dimension=1, tiled=True)
    mid = inputs + attn_local
    inverse_two = rms_inverse(mid)
    hat_two = mid * inverse_two
    normed_two = (hat_two * gains[1]).astype(jnp.bfloat16)
    ffn_source = lax.all_gather(normed_two, "mp", axis=1, tiled=True)
    up_full, down_full = (up_low, down_low)
    pre_act = jnp.einsum("rsd,df->rsf", ffn_source, up_full, preferred_element_type=jnp.float32)
    act_value, act_back = jax.vjp(gelu_exact, pre_act)
    act_low = act_value.astype(jnp.bfloat16)
    ffn_term = jnp.einsum("rsf,fd->rsd", act_low, down_full, preferred_element_type=jnp.float32)
    ffn_local = lax.psum_scatter(
        ffn_term.astype(jnp.bfloat16), "mp", scatter_dimension=1, tiled=True
    ).astype(jnp.float32)
    output = (mid + ffn_local).astype(jnp.bfloat16)
    grad_top = out_grad.astype(jnp.float32)
    grad_source = lax.all_gather(out_grad, "mp", axis=1, tiled=True)
    down_grad = jnp.einsum("rsf,rsd->fd", act_low, grad_source, preferred_element_type=jnp.float32)
    grad_act = jnp.einsum("rsd,fd->rsf", grad_source, down_full, preferred_element_type=jnp.float32)
    grad_pre = act_back(grad_act)[0].astype(jnp.bfloat16)
    up_grad = jnp.einsum("rsd,rsf->df", ffn_source, grad_pre, preferred_element_type=jnp.float32)
    grad_normed_part = jnp.einsum(
        "rsf,df->rsd", grad_pre, up_full, preferred_element_type=jnp.float32
    )
    grad_normed_two = lax.psum_scatter(grad_normed_part, "mp", scatter_dimension=1, tiled=True)
    gain_two_grad = jnp.sum(grad_normed_two * hat_two, axis=(0, 1))
    grad_mid = grad_top + norm_back(grad_normed_two, hat_two, inverse_two, gains[1])
    grad_mid_low = grad_mid.astype(jnp.bfloat16)
    grad_attn_full = lax.all_gather(grad_mid_low, "mp", axis=1, tiled=True)
    attn_out_grad = jnp.einsum(
        "rhse,rsd->hed", context, grad_attn_full, preferred_element_type=jnp.float32
    )
    attn_out_grad = attn_out_grad.reshape(head_local * head_size, model_width)
    grad_context = jnp.einsum(
        "rsd,hed->rhse", grad_attn_full, attn_out_heads, preferred_element_type=jnp.float32
    ).astype(jnp.bfloat16)

    def backward_row(bias_total, packed):
        q_row, k_row, v_row, mk_row, mv_row, seg_row, length, pair_on, lse_row, grad_row = packed
        mem_allowed, tok_allowed = row_masks(seg_row, length, pair_on)
        key_acc = jnp.zeros(k_row.shape, jnp.float32)
        value_acc = jnp.zeros(v_row.shape, jnp.float32)
        query_parts = []
        bias_parts = []
        for first_row in range(0, seq_span, block_rows):
            last_row = first_row + block_rows
            q_block = q_row[:, first_row:last_row]
            mem_s, tok_s = block_scores(
                q_block,
                mk_row,
                k_row,
                mem_allowed[first_row:last_row],
                tok_allowed[first_row:last_row],
                rel_bias[:, first_row:last_row],
                score_scale,
            )
            lse_block = lse_row[:, first_row:last_row, None]
            mem_prob = jnp.exp(mem_s - lse_block)
            tok_prob = jnp.exp(tok_s - lse_block)
            grad_block = grad_row[:, first_row:last_row]
            mem_gprob = jnp.einsum(
                "hqe,hke->hqk", grad_block, mv_row, preferred_element_type=jnp.float32
            )
            tok_gprob = jnp.einsum(
                "hqe,hke->hqk", grad_block, v_row, preferred_element_type=jnp.float32
            )
            row_dot = jnp.sum(mem_prob * mem_gprob, axis=-1, keepdims=True) + jnp.sum(
                tok_prob * tok_gprob, axis=-1, keepdims=True
            )
            mem_gscore = (mem_prob * (mem_gprob - row_dot)).astype(jnp.bfloat16)
            tok_gscore = (tok_prob * (tok_gprob - row_dot)).astype(jnp.bfloat16)
            query_grad = jnp.einsum(
                "hqk,hke->hqe", mem_gscore, mk_row, preferred_element_type=jnp.float32
            )
            query_grad = query_grad + jnp.einsum(
                "hqk,hke->hqe", tok_gscore, k_row, preferred_element_type=jnp.float32
            )
            query_parts.append((query_grad * score_scale).astype(jnp.bfloat16))
            key_acc = key_acc + jnp.einsum(
                "hqk,hqe->hke", tok_gscore, q_block, preferred_element_type=jnp.float32
            )
            value_acc = value_acc + jnp.einsum(
                "hqk,hqe->hke",
                tok_prob.astype(jnp.bfloat16),
                grad_block,
                preferred_element_type=jnp.float32,
            )
            bias_parts.append(tok_gscore.astype(jnp.float32))
        bias_total = bias_total + jnp.concatenate(bias_parts, axis=1)
        row_grads = (
            jnp.concatenate(query_parts, axis=1),
            (key_acc * score_scale).astype(jnp.bfloat16),
            value_acc.astype(jnp.bfloat16),
        )
        return (bias_total, row_grads)

    bias_grad, (grad_q, grad_k, grad_v) = lax.scan(
        backward_row,
        jnp.zeros((head_local, seq_span, seq_span), jnp.float32),
        (
            queries,
            key_new,
            value_new,
            mem_key_rows,
            mem_value_rows,
            seg_ids,
            row_len,
            slot_mask,
            log_totals,
            grad_context,
        ),
    )
    grad_project = jnp.stack([grad_q, grad_k, grad_v])
    qkv_grad = jnp.einsum(
        "rsd,crhse->cdhe", normed_full, grad_project, preferred_element_type=jnp.float32
    )
    qkv_grad = qkv_grad.reshape(3, model_width, head_local * head_size)
    grad_normed_term = jnp.einsum(
        "crhse,cdhe->rsd", grad_project, qkv_heads, preferred_element_type=jnp.float32
    )
    grad_normed_one = lax.psum_scatter(
        grad_normed_term.astype(jnp.bfloat16), "mp", scatter_dimension=1, tiled=True
    ).astype(jnp.float32)
    gain_one_grad = jnp.sum(grad_normed_one * hat_one, axis=(0, 1))
    grad_input = grad_mid + norm_back(grad_normed_one, hat_one, inverse_one, gains[0])
    bucket_sums = []
    for bucket_number in range(bucket_total):
        bucket_sums.append(
            jnp.sum(jnp.where((bucket_grid == bucket_number)[None], bias_grad, 0.0), axis=(1, 2))
        )
    table_local_grad = jnp.stack(bucket_sums)
    table_grad = lax.dynamic_update_slice(
        jnp.zeros((bucket_total, head_total), jnp.float32),
        table_local_grad,
        (jnp.int32(0), mp_index * head_local),
    )
    gains_grad, table_grad = lax.psum(
        (jnp.stack([gain_one_grad, gain_two_grad]), table_grad), ("dp", "mp")
    )
    qkv_sum, attn_out_sum, up_sum, down_sum = (
        lax.psum_scatter(qkv_grad, "dp", scatter_dimension=1, tiled=True),
        lax.psum_scatter(attn_out_grad, "dp", scatter_dimension=1, tiled=True),
        lax.psum_scatter(up_grad, "dp", scatter_dimension=0, tiled=True),
        lax.psum_scatter(down_grad, "dp", scatter_dimension=1, tiled=True),
    )
    qkv_new, qkv_first, qkv_second = adamw(w_qkv, qkv_sum, m_qkv, v_qkv, MATRIX_RATE, WEIGHT_DECAY)
    attn_out_new, attn_out_first, attn_out_second = adamw(
        w_attn_out, attn_out_sum, m_attn_out, v_attn_out, MATRIX_RATE, WEIGHT_DECAY
    )
    up_new, up_first, up_second = adamw(w_up, up_sum, m_up, v_up, MATRIX_RATE, WEIGHT_DECAY)
    down_new, down_first, down_second = adamw(
        w_down, down_sum, m_down, v_down, MATRIX_RATE, WEIGHT_DECAY
    )
    gains_new, gains_first, gains_second = adamw(
        gains, gains_grad, m_gains, v_gains, SMALL_RATE, 0.0
    )
    rel_new, rel_first, rel_second = adamw(rel_table, table_grad, m_rel, v_rel, SMALL_RATE, 0.0)
    return (
        output,
        grad_input,
        qkv_new,
        qkv_first,
        qkv_second,
        qkv_new.astype(jnp.bfloat16),
        attn_out_new,
        attn_out_first,
        attn_out_second,
        attn_out_new.astype(jnp.bfloat16),
        up_new,
        up_first,
        up_second,
        up_new.astype(jnp.bfloat16),
        down_new,
        down_first,
        down_second,
        down_new.astype(jnp.bfloat16),
        gains_new,
        gains_first,
        gains_second,
        rel_new,
        rel_first,
        rel_second,
    )


BF = jnp.bfloat16
F32 = jnp.float32
MESH_ID = pl.DeviceIdType.MESH
BIG = 1e30
KEY_PAD = 128
WIDE = 256
KEY_STEP, QUERY_STEP = 256, 512
SQRT_HALF = 0.5**0.5
INV_SQRT_2PI = 0.3989422804014327
LINK_SEMS = 137
VMEM_LIMIT = 63 * 2**20


def dot(a, b):
    return lax.dot_general(a, b, (((1,), (0,)), ((), ())), preferred_element_type=F32)


def dot_t(a, b):
    return lax.dot_general(a, b, (((1,), (1,)), ((), ())), preferred_element_type=F32)


def split3(v):
    hi = v.astype(BF)
    rest = v - hi.astype(F32)
    mid = rest.astype(BF)
    low = (rest - mid.astype(F32)).astype(BF)
    return hi, mid, low


class Links:
    def __init__(self, send_sems, recv_sems):
        self.send_sems, self.recv_sems = send_sems, recv_sems
        self.count = 0
        self.sent = []

    def take(self, n=1):
        self.count += n
        return self.count - n

    def send(self, src, dst, device, send_at=None, recv_at=None, when=None, else_keep=False):
        at = self.take() if send_at is None else send_at
        recv_at = at if recv_at is None else recv_at
        copy = pltpu.make_async_remote_copy(
            src, dst, self.send_sems.at[at], self.recv_sems.at[recv_at], device_id=device, device_id_type=MESH_ID
        )
        if when is None:
            copy.start()
        else:

            @pl.when(when)
            def _():
                copy.start()

            if else_keep:

                @pl.when(jnp.logical_not(when))
                def _():
                    pltpu.make_async_copy(src, dst, self.recv_sems.at[recv_at]).start()

        self.sent.append((copy, when))
        return at

    def arrived(self, dst, k):
        pltpu.make_async_copy(dst, dst, self.recv_sems.at[k]).wait()

    def left(self, since, until=None):
        for n in range(since, len(self.sent) if until is None else until):
            if self.sent[n] is None:
                continue
            copy, when = self.sent[n]
            if when is None:
                copy.wait_send()
            else:
                pl.when(when)(copy.wait_send)
            self.sent[n] = None


class Place:
    def __init__(self):
        self.y, self.x = lax.axis_index("y"), lax.axis_index("x")
        self.c, self.z = lax.axis_index("c"), lax.axis_index("z")
        self.to_x, self.to_y = {"x": 1 - self.x}, {"y": 1 - self.y}
        self.to_c, self.to_xy = {"c": 1 - self.c}, {"x": 1 - self.x, "y": 1 - self.y}
        z = self.z
        self.near = (z, z + 1 - 2 * lax.rem(z, 2), jnp.where(z < 2, 2, 1), jnp.where(z < 2, 3, 0))
        self.inner = (z == 1) | (z == 2)

    def greet(self):
        barrier = pltpu.get_barrier_semaphore()
        peers = [self.to_x, self.to_y, self.to_c, self.to_xy]
        for z in self.near[1:]:
            peers.append({"z": z})
            peers.append({"z": z, "c": 1 - self.c})
        for peer in peers:
            pl.semaphore_signal(barrier, inc=1, device_id=peer, device_id_type=MESH_ID)
        self.greeted = len(peers)

    def meet(self):
        pl.semaphore_wait(pltpu.get_barrier_semaphore(), self.greeted)


class Gather:
    def __init__(self, place, links, shard, whole, local_sem):
        self.p, self.links, self.shard, self.whole, self.local_sem = place, links, shard, whole, local_sem
        self.at_z = links.take(4)
        self.k_x, self.k_y, self.k_d, self.k_c = {}, {}, {}, {}
        self.out = {k: [] for k in range(4)}

    def spot(self, k, y, x):
        return self.whole.at[self.p.near[k], y, x, self.p.c]

    def send(self, k, *args, **kwargs):
        self.out[k].append(len(self.links.sent))
        return self.links.send(*args, **kwargs)

    def start_z(self):
        p = self.p
        own = self.spot(0, p.y, p.x)
        for k in (2, 1, 3):
            self.links.send(
                self.shard, own, {"z": p.near[k]}, self.at_z + k, self.at_z + p.z, p.inner if k == 3 else None
            )

    def start_own(self):
        p = self.p
        own = self.spot(0, p.y, p.x)
        self.own_copy = pltpu.make_async_copy(self.shard, own, self.local_sem)
        self.own_copy.start()
        self.k_x[0] = self.links.send(self.shard, own, p.to_x)
        self.k_y[0] = self.links.send(self.shard, own, p.to_y)

    def column(self, k):
        p = self.p
        block = self.spot(k, p.y, p.x)
        self.links.arrived(block, self.at_z + p.near[k])
        self.k_x[k] = self.send(k, block, block, p.to_x)
        self.k_y[k] = self.send(k, block, block, p.to_y)
        if k == 3:
            self.send(3, block, block, {"z": p.near[1]}, self.at_z, self.at_z + p.near[3], p.inner)

    def forward(self, k):
        p = self.p
        from_x, from_y = self.spot(k, p.y, 1 - p.x), self.spot(k, 1 - p.y, p.x)
        if k % 2 == 0:
            self.links.arrived(from_x, self.k_x[k])
            self.k_d[k] = self.send(k, from_x, from_x, p.to_y)
            self.links.arrived(from_y, self.k_y[k])
        else:
            self.links.arrived(from_y, self.k_y[k])
            self.k_d[k] = self.send(k, from_y, from_y, p.to_x)
            self.links.arrived(from_x, self.k_x[k])

    def cross(self, k):
        p = self.p
        self.links.arrived(self.spot(k, 1 - p.y, 1 - p.x), self.k_d[k])
        if k == 0:
            self.own_copy.wait()
        half = self.whole.at[p.near[k], :, :, p.c]
        self.k_c[k] = self.send(k, half, half, p.to_c)

    def finish(self, k):
        p = self.p
        self.links.arrived(self.whole.at[p.near[k], :, :, 1 - p.c], self.k_c[k])

    def release(self, k):
        for n in self.out[k]:
            self.links.left(n, n + 1)


class Reduce:
    def __init__(self, place, links, grads, land):
        self.p, self.links, self.g = place, links, grads
        self.land_c, self.land_p, self.land_q, self.land_z = land
        half = grads.shape[5] // 2
        self.upper, self.lower = slice(0, half), slice(half, 2 * half)
        self.at, self.at_z = {}, links.take(4)

    def start(self, k):
        p = self.p
        self.at[k] = [self.links.send(self.g.at[:, p.near[k], :, :, 1 - p.c], self.land_c.at[:, k], p.to_c)]

    def add(self, at, part):
        self.g[(slice(None), *at)] = self.g[(slice(None), *at)] + part

    def core(self, k):
        p, links, block = self.p, self.links, self.p.near[k]
        every = slice(None)
        links.arrived(self.land_c.at[:, k], self.at[k][0])
        away_x, away_y = (every, 1 - p.x), (1 - p.y, every)
        stay_x, stay_y = (every, p.x), (p.y, every)
        for n, (there, rows, peer) in enumerate(((away_x, self.upper, p.to_x), (away_y, self.lower, p.to_y))):
            self.add((block, *there, p.c, rows), self.land_c[(every, k, *there, rows)])
            self.at[k].append(links.send(self.g.at[(every, block, *there, p.c, rows)], self.land_p.at[:, k, n], peer))
        for there, rows in ((stay_x, self.upper), (stay_y, self.lower)):
            self.add((block, *there, p.c, rows), self.land_c[(every, k, *there, rows)])

    def plane(self, k):
        p, links, block = self.p, self.links, self.p.near[k]
        every = slice(None)
        steps = (
            ((every, p.x), self.upper, (1 - p.y, p.x), p.to_y),
            ((p.y, every), self.lower, (p.y, 1 - p.x), p.to_x),
        )
        for n, (stay, rows, away, peer) in enumerate(steps):
            links.arrived(self.land_p.at[:, k, n], self.at[k][1 + n])
            self.add((block, *stay, p.c, rows), self.land_p[:, k, n])
            self.at[k].append(links.send(self.g.at[(every, block, *away, p.c, rows)], self.land_q.at[:, k, n], peer))

    def column(self, k):
        p, links = self.p, self.links
        here = (p.near[k], p.y, p.x, p.c)
        for n, rows in enumerate((self.upper, self.lower)):
            links.arrived(self.land_q.at[:, k, n], self.at[k][3 + n])
            self.add((*here, rows), self.land_q[:, k, n])
        if k == 0:
            return
        target, spot = p.near[k], p.z
        if k == 3:
            @pl.when(p.inner)
            def _():
                links.arrived(self.land_z.at[:, p.z], self.at_z + p.z)
                self.add(here, self.land_z[:, p.z])

            target = jnp.where(p.inner, p.near[3], p.near[1])
            spot = jnp.where(p.inner, p.z, p.near[1])
        mine = self.g.at[(slice(None), *here)]
        links.send(mine, self.land_z.at[:, spot], {"z": target}, self.at_z + k, self.at_z + spot)

    def finish(self, out):
        p = self.p
        total = self.g[:, p.z, p.y, p.x, p.c].astype(F32)
        for k in (1, 2):
            source = p.near[k]
            self.links.arrived(self.land_z.at[:, source], self.at_z + source)
            total = total + self.land_z[:, source].astype(F32)
        out[...] = total

        @pl.when(p.inner)
        def _():
            source = p.near[3]
            self.links.arrived(self.land_z.at[:, source], self.at_z + source)
            out[...] += self.land_z[:, source].astype(F32)


def near_third(key, block):
    if key < 4:
        return (key - block + 1, None) if abs(key - block) <= 1 else None
    if block == 3 and key == 4:
        return (2, 0)
    if block == 0 and key == 7:
        return (0, 1)
    return None


def near_tiles(keys, queries):
    tiles = []
    for row in range(0, keys.stop - keys.start, 128):
        for col in range(0, queries.stop - queries.start, 128):
            found = near_third((keys.start + row) // 128, (queries.start + col) // 128)
            if found is not None:
                tiles.append((row, col, *found))
    return tiles


def add_band(s, band, keys, queries, core):
    tiles = {(row, col): (third, need) for row, col, third, need in near_tiles(keys, queries)}
    rows = []
    for row in range(0, s.shape[0], 128):
        cols = []
        for col in range(0, s.shape[1], 128):
            part = s[row : row + 128, col : col + 128]
            if (row, col) in tiles:
                third, need = tiles[row, col]
                near = band[third * 128 : (third + 1) * 128, :]
                if need is not None:
                    near = near * jnp.where(core == need, 1.0, 0.0)
                part = part + near
            cols.append(part)
        rows.append(jnp.concatenate(cols, axis=1))
    return jnp.concatenate(rows, axis=0)


def far_masks(core, span):
    key = lax.broadcasted_iota(jnp.int32, (8, span), 0)
    block = lax.broadcasted_iota(jnp.int32, (8, span), 1) // 128
    other = key - 4
    left = ((key < 4) & (key <= block - 2)) | ((key >= 4) & (core == 1) & ~((block == 0) & (other == 3)))
    right = ((key < 4) & (key >= block + 2)) | ((key >= 4) & (core == 0) & ~((block == 3) & (other == 0)))
    return left, right


def rows_of(parts, span):
    row = lax.broadcasted_iota(jnp.int32, (8, span), 0)
    out = jnp.zeros((8, span), F32)
    for n, part in enumerate(parts):
        out = jnp.where(row == n, part.astype(F32), out)
    return out.astype(BF)


def far_rows(left, right, far_left, far_right):
    hi, mid, low = split3(jnp.where(left, far_left, jnp.where(right, far_right, 0.0)))
    return jnp.concatenate([hi.astype(F32), mid.astype(F32), low.astype(F32)], axis=0).astype(BF)


def fwd_head(R, h, core, far_left, far_right):
    span, keys = R.QT.shape[2], R.KVT.shape[2]
    toks = keys - KEY_PAD
    R.ka[0:64, :] = R.KVT[h, 0:64, :]
    R.Ka[...] = R.ka[...].T
    R.va[0:64, :] = R.KVT[h, 64:128, :]
    R.qa[0:64, :] = R.QT[h]
    left, right = far_masks(core, span)
    R.qa[80:104, :] = far_rows(left, right, far_left, far_right)
    R.band[...] = band_of(R.wave[pl.ds(h, 1), :])
    band = R.band
    last = slice(toks, toks + 32)
    for left_col in range(0, span, QUERY_STEP):
        cols = slice(left_col, left_col + QUERY_STEP)
        query = R.qa[:, cols]
        peak = None
        for first in range(0, toks, KEY_STEP):
            rows = slice(first, first + KEY_STEP)
            s = add_band(dot(R.Ka[rows, :], query), band, rows, cols, core)
            R.S[rows, :] = s
            top = jnp.max(s, axis=0, keepdims=True)
            peak = top if peak is None else jnp.maximum(peak, top)
        s = dot(R.Ka[last, :], query)
        R.S[last, :] = s
        peak = jnp.maximum(peak, jnp.max(s, axis=0, keepdims=True))
        for first in range(0, toks, KEY_STEP):
            rows = slice(first, first + KEY_STEP)
            R.P[rows, :] = jnp.exp(R.S[rows, :] - peak).astype(BF)
        R.P[last, :] = jnp.exp(R.S[last, :] - peak).astype(BF)
        o = dot(R.va[0:72, :], R.P[...])
        total = o[64:65, :]
        R.ctxT[h, :, cols] = (o[0:64, :] * (1.0 / total)).astype(BF)
        R.lse[pl.ds(h, 1), cols] = peak + jnp.log(total)


def bwd_head(R, h, j, core, far_left, far_right):
    span, keys = R.QT.shape[2], R.KVT.shape[2]
    toks = keys - KEY_PAD
    R.ka[0:64, :] = R.KVT[h, 0:64, :]
    R.Ka[...] = R.ka[...].T
    R.va[0:64, :] = R.KVT[h, 64:128, :]
    R.Va[...] = R.va[...].T
    R.qa[0:64, :] = R.QT[h]
    left, right = far_masks(core, span)
    R.qa[80:104, :] = far_rows(left, right, far_left, far_right)
    R.qa[72:80, :] = rows_of(split3(-R.lse[pl.ds(h, 1), :]), span)
    grad = R.dOT[h]
    R.da[0:64, :] = grad
    row_dot = jnp.sum(grad.astype(F32) * R.ctxT[h].astype(F32), axis=0, keepdims=True)
    R.da[64:72, :] = rows_of(split3(-row_dot), span)
    R.band[...] = band_of(R.wave[pl.ds(h, 1), :])
    band = R.band
    query_sum = {}
    near = [None, None, None]
    for first in range(0, toks + 1, KEY_STEP):
        is_mem = first == toks
        rows = slice(toks, toks + 32) if is_mem else slice(first, first + KEY_STEP)
        key_sum = value_sum = None
        for left_col in range(0, span, QUERY_STEP):
            cols = slice(left_col, left_col + QUERY_STEP)
            s = dot(R.Ka[rows, :], R.qa[:, cols])
            if not is_mem:
                s = add_band(s, band, rows, cols, core)
            p = jnp.exp(s)
            ds = p * dot(R.Va[rows, :], R.da[:, cols])
            ds_low = ds.astype(BF)
            if is_mem:
                filled = jnp.concatenate([ds_low, jnp.zeros((KEY_PAD - 32, QUERY_STEP), BF)], axis=0)
                part = dot(R.ka[0:96, toks:keys], filled)
            else:
                v = dot_t(p.astype(BF), R.da[0:64, cols])
                k = dot_t(ds_low, R.qa[0:64, cols])
                value_sum = v if value_sum is None else value_sum + v
                key_sum = k if key_sum is None else key_sum + k
                for row, col, third, need in near_tiles(rows, cols):
                    t = ds[row : row + 128, col : col + 128]
                    if need is not None:
                        t = t * jnp.where(core == need, 1.0, 0.0)
                    near[third] = t if near[third] is None else near[third] + t
                part = dot(R.ka[0:96, rows], ds_low)
            query_sum[left_col] = part if left_col not in query_sum else query_sum[left_col] + part
        if not is_mem:
            both = jnp.concatenate([key_sum, value_sum], axis=1)
            if first < span:
                R.kv_own[j, rows, :] = both
            else:
                R.kv_out[h, slice(first - span, first - span + KEY_STEP), :] = both.astype(BF)
    turned = jnp.concatenate(list(query_sum.values()), axis=1)
    R.dq[j] = (turned[0:64, :] * HEAD_DIM**-0.5).T.astype(BF)
    far = turned[80:88, :]
    lane = lax.broadcasted_iota(jnp.int32, (1, 128), 1)
    sum_left = jnp.sum(jnp.where(left, far, 0.0))
    sum_right = jnp.sum(jnp.where(right, far, 0.0))
    ends = jnp.where(lane == 0, sum_left, jnp.where(lane == 1, sum_right, 0.0))
    R.small[pl.ds(2 + h, 1), 0:640] = jnp.concatenate([unband(jnp.concatenate(near, axis=0)), ends], axis=1)


class Refs:
    def __init__(self, **refs):
        self.__dict__.update(refs)


def weights(R, n, z, cols):
    part = R.W[n, z, :, :, :, :, cols]
    return part.reshape(-1, part.shape[4])


class RowMove:
    def __init__(self, place, links, src, dst):
        self.links, self.dst = links, dst
        slot = lax.rem(place.z, 2)
        self.at = links.take(2)
        for i in (0, 1):
            target_z, target_c = 2 * place.c + i, place.z // 2
            links.send(
                src.at[i],
                dst.at[slot],
                {"c": target_c, "z": target_z},
                self.at + i,
                self.at + slot,
                (target_c != place.c) | (target_z != place.z),
                else_keep=True,
            )

    def wait(self, slot):
        self.links.arrived(self.dst.at[slot], self.at + slot)


def norm_parts(values):
    inverse = lax.rsqrt(jnp.mean(values * values, axis=-1, keepdims=True) + NORM_EPS)
    return inverse, values * inverse


def mask_rows(R, place):
    span, keys = R.QT.shape[2], R.KVT.shape[2]
    toks = keys - KEY_PAD
    mine = jnp.where(place.z // 2 == place.c, R.code[lax.rem(place.z, 2)], R.code_in[...])
    R.code_in[...] = mine
    own = R.code_in[:, pl.ds(pl.multiple_of(place.c * span, span), span)]
    other = R.code_in[:, pl.ds(pl.multiple_of((1 - place.c) * span, span), span)]
    line = jnp.concatenate([own, other, R.code_in[:, toks:keys]], axis=1)
    row = lax.broadcasted_iota(jnp.int32, (8, keys), 0)
    as_doc = (row - 1).astype(F32)
    kind = jnp.where(row < 5, jnp.where(line == as_doc, 1.0, 0.0), 0.0)
    kind = jnp.where((row == 5) & (line == 11.0), 1.0, kind)
    kind = jnp.where((row == 6) & (line >= 10.0), 1.0, kind)
    R.ka[64:72, :] = kind.astype(BF)
    R.ka[72:80, :] = jnp.where(row < 3, 1.0, 0.0).astype(BF)
    block = lax.broadcasted_iota(jnp.int32, (8, keys), 1) // 128
    hot = jnp.where((block == row) & (block < toks // 128), 1.0, 0.0)
    R.ka[80:104, :] = jnp.concatenate([hot, hot, hot], axis=0).astype(BF)
    R.ka[104:128, :] = jnp.zeros((24, keys), BF)
    R.va[64:72, :] = jnp.where(row < 3, 1.0, 0.0).astype(BF)
    R.va[72:128, :] = jnp.zeros((56, keys), BF)
    qrow = lax.broadcasted_iota(jnp.int32, (8, span), 0)
    hide = jnp.where((qrow < 5) & (own != (qrow - 1).astype(F32)), -BIG, 0.0)
    hide = jnp.where(qrow == 5, -BIG, hide)
    hide = jnp.where((qrow == 6) & (own == -1.0), -BIG, hide)
    R.qa[64:72, :] = hide.astype(BF)
    R.qa[72:128, :] = jnp.zeros((56, span), BF)
    R.da[64:128, :] = jnp.zeros((64, span), BF)
    R.P[toks + 32 : keys, :] = jnp.zeros((KEY_PAD - 32, QUERY_STEP), BF)


def band_of(wave):
    spread = jnp.broadcast_to(wave, (128, 512))
    parts = [pltpu.roll(spread, 128 * n, 1, stride=1, stride_axis=0)[:, 0:128] for n in range(3)]
    return jnp.concatenate(parts, axis=0)


def unband(near):
    empty = jnp.zeros((8, 128), F32)
    total = None
    for n in range(16):
        part = jnp.concatenate(
            [near[8 * n : 8 * n + 8], empty, near[256 + 8 * n : 264 + 8 * n], near[128 + 8 * n : 136 + 8 * n]], axis=1
        )
        if n:
            part = pltpu.roll(part, 512 - 8 * n, 1)
        total = part if total is None else total + part
    row = lax.broadcasted_iota(jnp.int32, (8, 512), 0)
    out = jnp.zeros((8, 512), F32)
    for n in range(8):
        out = out + jnp.where(row == n, total if n == 0 else pltpu.roll(total, 512 - n, 1), 0.0)
    return jnp.sum(out, axis=0, keepdims=True)


def prepare(R):
    rows, seq = R.seg_ids.shape
    slots, heads_wide = R.mem_keys.shape[1:]
    group = heads_wide // HEAD_DIM
    R.KVT[:, :, seq : seq + KEY_PAD] = jnp.zeros((R.KVT.shape[0], 128, KEY_PAD), BF)
    parts = []
    for j in range(group):
        cols = slice(j * HEAD_DIM, (j + 1) * HEAD_DIM)
        parts += [R.w_qkv[1, :, cols], R.w_qkv[2, :, cols]]
    parts += [R.w_qkv[0], R.w_attn_out[...].T]
    R.packed[0] = jnp.concatenate(parts, axis=1).astype(BF)
    R.packed[1] = R.w_up[...].astype(BF)
    R.packed[2] = R.w_down[...].astype(BF)
    place = lax.broadcasted_iota(jnp.int32, (1, seq), 1)
    pair = lax.broadcasted_iota(jnp.int32, (slots // 2, KEY_PAD), 0)
    lane = lax.broadcasted_iota(jnp.int32, (slots // 2, KEY_PAD), 1)
    spread = jnp.where(lane // 2 == pair, 1.0, 0.0)
    on = dot(jnp.where(R.slot_mask[...] > 0, 1.0, 0.0), spread)
    for r in range(rows):
        R.mem[r, 0:slots, :] = R.mem_keys[r]
        R.mem[r, slots : 2 * slots, :] = R.mem_values[r]
        docs = jnp.where(place < R.row_len[r], R.seg_ids[r : r + 1, :], -1).astype(F32)
        R.code[r, :, 0:seq] = jnp.broadcast_to(docs, (8, seq))
        R.code[r, :, seq : seq + KEY_PAD] = jnp.broadcast_to(jnp.where(on[r : r + 1] > 0.5, 10.0, 11.0), (8, KEY_PAD))
    heads = R.rel_table.shape[0]
    made = lax.dot_general(
        R.rel_table[...],
        R.hot[...],
        (((1,), (0,)), ((), ())),
        precision=lax.Precision.HIGHEST,
        preferred_element_type=F32,
    )
    R.wave[0:heads, :] = made


def update_kernel(names, *refs):
    R = Refs(**dict(zip(names, refs)))
    group = R.w_qkv.shape[2] // HEAD_DIM
    kv_cols, qkv_cols = group * 128, group * 192
    R.output_out[...] = R.output[...]
    R.grad_input[...] = R.grad_in[...].astype(F32)

    def step(name, gradient, at=Ellipsis, rate=MATRIX_RATE, decay=WEIGHT_DECAY, copy=True):
        ref = lambda kind: getattr(R, kind + "_" + name)
        new, first, second = adamw(ref("w")[at], gradient, ref("m")[at], ref("v")[at], rate, decay)
        ref("new")[at] = new
        ref("first")[at] = first
        ref("second")[at] = second
        if copy:
            ref("copy")[at] = new.astype(BF)

    sums = R.gsum[0]
    step("qkv", sums[:, kv_cols:qkv_cols], 0)
    for n in (0, 1):
        parts = [sums[:, j * 128 + n * 64 : j * 128 + n * 64 + HEAD_DIM] for j in range(group)]
        step("qkv", jnp.concatenate(parts, axis=1), 1 + n)
    step("attn_out", sums[:, qkv_cols:].T)
    step("up", R.gsum[1])
    step("down", R.gsum[2])
    step("gains", R.small[0:2, :], rate=SMALL_RATE, decay=0.0, copy=False)
    heads = R.w_rel.shape[0]
    along = lax.dot_general(
        R.small[2 : 2 + heads, 0:512],
        R.hot[...],
        (((1,), (1,)), ((), ())),
        precision=lax.Precision.HIGHEST,
        preferred_element_type=F32,
    )
    bucket = lax.broadcasted_iota(jnp.int32, along.shape, 1)
    ends = R.small[2 : 2 + heads, 512:640]
    along = along + jnp.where(bucket == 15, ends[:, 0:1], 0.0) + jnp.where(bucket == 31, ends[:, 1:2], 0.0)
    step("rel", along, rate=SMALL_RATE, decay=0.0, copy=False)


def layer_kernel(names, *refs):
    R = Refs(**dict(zip(names, refs)))
    place = Place()
    links = Links(R.send_sems, R.recv_sems)
    place.greet()
    prepare(R)
    place.meet()
    heads, span = R.QT.shape[0], R.QT.shape[2]
    width = R.xin.shape[2]
    group = heads // 4
    kv_cols, q_cols = group * 128, group * HEAD_DIM
    qkv_cols = kv_cols + q_cols
    slots = R.xin.shape[0]
    piece = R.xin.shape[1]

    near = place.near
    first, up, down = gather = [Gather(place, links, R.packed.at[n], R.W.at[n], R.local_sems.at[n]) for n in range(3)]
    first.start_z()
    first.start_own()
    up.start_z()
    up.start_own()
    down.start_own()
    k_code = links.send(R.code.at[lax.rem(place.z, 2)], R.code_in, place.to_c)
    at_mem = links.take(4)
    mem_spot = R.mem_in.at[place.z]
    for r in (0, 1):
        for c in (0, 1):
            links.send(
                R.mem.at[r],
                mem_spot,
                {"c": c, "z": 2 * place.c + r},
                at_mem + 2 * r + c,
                at_mem + place.z,
                (place.c != c) | (place.z != 2 * place.c + r),
                else_keep=True,
            )
    for k in (1, 2, 3):
        first.column(k)
    move_in = RowMove(place, links, R.hidden, R.xin)
    for k in range(4):
        first.forward(k)
    links.arrived(R.code_in, k_code)
    mask_rows(R, place)
    for k in (1, 2, 3):
        up.column(k)
    for k in range(4):
        first.cross(k)
    up.forward(0)
    up.forward(1)
    down.start_z()
    for s in range(slots):
        move_in.wait(s)
        _, hat = norm_parts(R.xin[s].astype(F32))
        R.na[s * piece : (s + 1) * piece, :] = (hat * R.gains[0:1, :]).astype(BF)

    def heads_of(k):
        return pl.ds(group * near[k], group)

    k_kv = []
    for k in range(4):
        first.finish(k)
        low = dot(R.na[...], weights(R, 0, near[k], slice(0, qkv_cols))).astype(BF)
        for j in range(group):
            R.KVT[group * near[k] + j, :, 0:span] = low[:, j * 128 : (j + 1) * 128].T
        turned = (low[:, kv_cols:qkv_cols].astype(F32) * HEAD_DIM**-0.5).astype(BF).T
        for j in range(group):
            R.QT[group * near[k] + j] = turned[j * HEAD_DIM : (j + 1) * HEAD_DIM, :]
        block = heads_of(k)
        k_kv.append(links.send(R.KVT.at[block, :, 0:span], R.KVT.at[block, :, span : 2 * span], place.to_c))
    up.forward(2)
    up.forward(3)
    move_grad = RowMove(place, links, R.out_grad, R.gin)
    for k in range(4):
        up.cross(k)

    for k in range(4):
        block = heads_of(k)
        links.arrived(R.KVT.at[block, :, span : 2 * span], k_kv[k])
        links.arrived(R.mem_in.at[near[k]], at_mem + near[k])
        slots_in = R.mem_in.shape[1] // 2
        turned = R.mem_in[near[k]].astype(F32).T.astype(BF)
        for j in range(group):
            for n in (0, 1):
                R.KVT[group * near[k] + j, n * HEAD_DIM : (n + 1) * HEAD_DIM, 2 * span : 2 * span + slots_in] = turned[
                    j * HEAD_DIM : (j + 1) * HEAD_DIM, n * slots_in : (n + 1) * slots_in
                ]

        @pl.loop(0, group)
        def _(j):
            h = group * near[k] + j
            fwd_head(R, h, place.c, R.far_bias[h, 15], R.far_bias[h, 31])

        if k == 0:
            for n in (1, 2, 3):
                down.column(n)
        elif k == 1:
            down.forward(0)
            down.forward(1)
        elif k == 2:
            down.forward(2)
            down.cross(0)
        else:
            down.forward(3)
            down.cross(1)

    for s in range(slots):
        rows = slice(s * piece, (s + 1) * piece)
        total = R.xin[s].astype(F32)
        for z in range(4):
            ctx = R.ctxT[group * z : group * (z + 1), :, rows].reshape(q_cols, piece).T
            total = total + dot_t(ctx, weights(R, 0, z, slice(qkv_cols, width)))
        R.mid[rows, :] = total
        _, hat = norm_parts(total)
        R.na[rows, :] = (hat * R.gains[1:2, :]).astype(BF)
    R.nT[...] = R.na[...].T

    for s in range(slots):
        move_grad.wait(s)
        R.gT[:, s * piece : (s + 1) * piece] = R.gin[s].T
    def sum_of(chunks):
        land = [ref.at[chunks] for ref in (R.land_c, R.land_p, R.land_q, R.land_z)]
        return Reduce(place, links, R.W.at[chunks], land)

    qkv_sum, ffn_sum = sum_of(slice(0, 1)), sum_of(slice(1, 3))
    down.cross(2)
    down.cross(3)
    for k in (3, 2, 1, 0):
        up.finish(k)
        down.finish(k)
        for n in range(width // WIDE):
            cols = slice(n * WIDE, (n + 1) * WIDE)
            pre = dot(R.na[...], weights(R, 1, near[k], cols))
            back = dot(R.gin[...].reshape(span, width), weights(R, 2, near[k], cols))
            phi = 0.5 + 0.5 * lax.erf(pre * SQRT_HALF)
            R.act[:, cols] = (pre * phi).astype(BF)
            slope = phi + pre * (jnp.exp(-0.5 * pre * pre) * INV_SQRT_2PI)
            R.gp[:, cols] = (back * slope).astype(BF)
        out_part = dot_t(R.act[...], weights(R, 2, near[k], slice(0, width)))
        back_part = dot_t(R.gp[...], weights(R, 1, near[k], slice(0, width)))
        if k == 3:
            R.acc[...] = out_part
            R.gacc[...] = back_part
        else:
            R.acc[...] += out_part
            R.gacc[...] += back_part
        up.release(k)
        R.W[1, near[k]] = dot(R.nT[...], R.gp[...]).astype(BF).reshape(R.W.shape[2:])
        down.release(k)
        R.W[2, near[k]] = dot(R.gT[...], R.act[...]).astype(BF).reshape(R.W.shape[2:])
        ffn_sum.start(k)
        if k < 3:
            ffn_sum.core(k + 1)
    ffn_sum.plane(3)
    for s in range(slots):
        R.ob[s] = (R.mid[s * piece : (s + 1) * piece, :] + R.acc[s * piece : (s + 1) * piece, :]).astype(BF)
    move_out = RowMove(place, links, R.ob, R.output)

    gain_two = jnp.zeros((1, width), F32)
    for s in range(slots):
        rows = slice(s * piece, (s + 1) * piece)
        inverse, hat = norm_parts(R.mid[rows, :])
        grad = R.gacc[rows, :]
        gain_two = gain_two + jnp.sum(grad * hat, axis=0, keepdims=True)
        scaled = grad * R.gains[1:2, :]
        shift = hat * jnp.mean(scaled * hat, axis=-1, keepdims=True)
        top = R.gin[s].astype(F32) + inverse * (scaled - shift)
        R.mid[rows, :] = top
        R.na[rows, :] = top.astype(BF)
    R.small[...] = jnp.zeros_like(R.small)
    R.small[1:2, :] = gain_two
    R.gT[...] = R.na[...].T
    ffn_sum.core(0)
    for k in range(4):
        first.release(k)
    for z in range(4):
        turned = dot(R.na[...], weights(R, 0, z, slice(qkv_cols, width))).astype(BF).T
        for j in range(group):
            R.dOT[group * z + j] = turned[j * HEAD_DIM : (j + 1) * HEAD_DIM, :]
        part = dot_t(R.gT[...], R.ctxT[group * z : group * (z + 1)].reshape(q_cols, span)).astype(BF)
        R.W[0, z, :, :, :, :, qkv_cols:] = part.reshape(2, 2, 2, width // 8, q_cols)
    for s in range(slots):
        _, hat = norm_parts(R.xin[s].astype(F32))
        R.nT[:, s * piece : (s + 1) * piece] = (hat * R.gains[0:1, :]).astype(BF).T

    def project_back(k):
        links.arrived(R.kv_in.at[heads_of(k)], k_back[k])
        parts = []
        for j in range(group):
            whole = R.kv_own[j] + R.kv_in[group * near[k] + j].astype(F32)
            parts.append(whole.astype(BF))
        for j in range(group):
            parts.append(R.dq[j])
        grads = jnp.concatenate(parts, axis=1)
        part = dot_t(grads, weights(R, 0, near[k], slice(0, qkv_cols)))
        if k == 3:
            R.gacc[...] = part
        else:
            R.gacc[...] += part
        if k == 0:
            rows_back()
        made = dot(R.nT[...], grads).astype(BF)
        R.W[0, near[k], :, :, :, :, 0:qkv_cols] = made.reshape(2, 2, 2, width // 8, qkv_cols)
        qkv_sum.start(k)

    def rows_back():
        gain_one = jnp.zeros((1, width), F32)
        for s in range(slots):
            rows = slice(s * piece, (s + 1) * piece)
            inverse, hat = norm_parts(R.xin[s].astype(F32))
            grad = R.gacc[rows, :]
            gain_one = gain_one + jnp.sum(grad * hat, axis=0, keepdims=True)
            scaled = grad * R.gains[0:1, :]
            shift = hat * jnp.mean(scaled * hat, axis=-1, keepdims=True)
            R.gin[s] = (R.mid[rows, :] + inverse * (scaled - shift)).astype(BF)
        moves.append(RowMove(place, links, R.gin, R.grad_in))
        R.small[0:1, :] = gain_one

    moves = []
    ticks = (
        [(ffn_sum, "plane", 2)],
        [(ffn_sum, "column", 3), (ffn_sum, "plane", 1)],
        [(ffn_sum, "column", 2), (qkv_sum, "core", 3)],
        [(ffn_sum, "plane", 0), (ffn_sum, "column", 1)],
        [(qkv_sum, "plane", 3), (qkv_sum, "core", 2)],
        [(ffn_sum, "column", 0)],
        [(qkv_sum, "core", 1), (qkv_sum, "plane", 2), (qkv_sum, "column", 3)],
        [(ffn_sum, "finish", R.gsum.at[1:3]), (qkv_sum, "plane", 1), (qkv_sum, "column", 2)],
    )
    k_back = {}
    for k in (3, 2, 1, 0):

        for part, bounds in enumerate(((0, 1), (1, group))):

            @pl.loop(*bounds)
            def _(j):
                h = group * near[k] + j
                bwd_head(R, h, j, place.c, R.far_bias[h, 15], R.far_bias[h, 31])

            if part == 1:
                k_back[k] = links.send(R.kv_out.at[heads_of(k)], R.kv_in.at[heads_of(k)], place.to_c)
            for chunk, stage, n in ticks[2 * (3 - k) + part]:
                getattr(chunk, stage)(n)
        project_back(k)

    at = links.send(R.small, R.small_in.at[0], place.to_c)
    links.arrived(R.small_in.at[0], at)
    R.small_in[0] = R.small_in[0] + R.small[...]
    at_small = links.take(3)
    for k, peer in enumerate((place.to_x, place.to_y, place.to_xy)):
        links.send(R.small_in.at[0], R.small_in.at[1 + k], peer, at_small + k)
    qkv_sum.core(0)
    for k in range(3):
        links.arrived(R.small_in.at[1 + k], at_small + k)
    row = R.small_in[0] + R.small_in[1]
    other = R.small_in[2] + R.small_in[3]
    R.small_z[place.z] = row + other
    own = R.small_z.at[place.z]
    at_small = links.take(4)
    for k in (1, 2, 3):
        links.send(own, own, {"z": near[k]}, at_small + k, at_small + place.z)
    qkv_sum.plane(0)
    qkv_sum.column(1)
    for k in (1, 2, 3):
        links.arrived(R.small_z.at[near[k]], at_small + near[k])
    R.small_sum[...] = (R.small_z[0] + R.small_z[1]) + (R.small_z[2] + R.small_z[3])
    qkv_sum.column(0)
    qkv_sum.finish(R.gsum.at[0:1])
    for s in range(slots):
        move_out.wait(s)
        moves[0].wait(s)
    links.left(0)


def wave_buckets():
    lane = np.arange(512)
    apart = np.where(lane < 128, -lane - 128, 384 - lane)
    far = np.abs(apart)
    bucket = np.where(far < 8, far, 8 + sum((far >= bound).astype(np.int32) for bound in FAR_BOUNDS))
    return bucket + np.where(apart > 0, 16, 0)


def on_moved(
    hidden_in,
    out_grad,
    seg_ids,
    row_len,
    slot_mask,
    mem_keys,
    mem_values,
    w_qkv,
    m_qkv,
    v_qkv,
    w_attn_out,
    m_attn_out,
    v_attn_out,
    w_up,
    m_up,
    v_up,
    w_down,
    m_down,
    v_down,
    gains,
    m_gains,
    v_gains,
    rel_table,
    m_rel,
    v_rel,
):
    rows, piece, width = hidden_in.shape
    seq = seg_ids.shape[1]
    span = seq // 2
    buckets, heads = rel_table.shape
    group = heads // 4
    shard = w_qkv.shape[1]
    w_down, m_down, v_down = w_down.T, m_down.T, v_down.T
    rel_table, m_rel, v_rel = rel_table.T, m_rel.T, v_rel.T
    hot = jnp.asarray(np.arange(buckets)[:, None] == wave_buckets()[None, :], F32)

    any_space = pl.BlockSpec(memory_space=pl.ANY)
    vmem = pl.BlockSpec(memory_space=pltpu.VMEM)
    smem = pl.BlockSpec(memory_space=pltpu.SMEM)
    keys = seq + KEY_PAD
    scratch = {
        "W": pltpu.VMEM((3, 4, 2, 2, 2, shard, width), BF),
        "land_c": pltpu.VMEM((3, 4, 2, 2, shard, width), BF),
        "land_p": pltpu.VMEM((3, 4, 2, 2, shard // 2, width), BF),
        "land_q": pltpu.VMEM((3, 4, 2, shard // 2, width), BF),
        "land_z": pltpu.VMEM((3, 4, shard, width), BF),
        "KVT": pltpu.VMEM((heads, 128, keys), BF),
        "QT": pltpu.VMEM((heads, HEAD_DIM, span), BF),
        "ctxT": pltpu.VMEM((heads, HEAD_DIM, span), BF),
        "dOT": pltpu.VMEM((heads, HEAD_DIM, span), BF),
        "lse": pltpu.VMEM((16, span), F32),
        "xin": pltpu.VMEM((2, piece, width), BF),
        "gin": pltpu.VMEM((2, piece, width), BF),
        "ob": pltpu.VMEM((2, piece, width), BF),
        "na": pltpu.VMEM((span, width), BF),
        "nT": pltpu.VMEM((width, span), BF),
        "gT": pltpu.VMEM((width, span), BF),
        "act": pltpu.VMEM((span, width), BF),
        "gp": pltpu.VMEM((span, width), BF),
        "mid": pltpu.VMEM((span, width), F32),
        "acc": pltpu.VMEM((span, width), F32),
        "gacc": pltpu.VMEM((span, width), F32),
        "kv_own": pltpu.VMEM((group, span, 128), F32),
        "kv_in": pltpu.VMEM((heads, span, 128), BF),
        "kv_out": pltpu.VMEM((heads, span, 128), BF),
        "dq": pltpu.VMEM((group, span, HEAD_DIM), BF),
        "S": pltpu.VMEM((seq + 32, QUERY_STEP), F32),
        "P": pltpu.VMEM((keys, QUERY_STEP), BF),
        "ka": pltpu.VMEM((128, keys), BF),
        "va": pltpu.VMEM((128, keys), BF),
        "Ka": pltpu.VMEM((keys, 128), BF),
        "Va": pltpu.VMEM((keys, 128), BF),
        "qa": pltpu.VMEM((128, span), BF),
        "da": pltpu.VMEM((128, span), BF),
        "band": pltpu.VMEM((384, 128), F32),
        "code": pltpu.VMEM((rows, 8, keys), F32),
        "packed": pltpu.VMEM((3, shard, width), BF),
        "mem": pltpu.VMEM((rows, 2 * mem_keys.shape[1], group * HEAD_DIM), BF),
        "mem_in": pltpu.VMEM((4, 2 * mem_keys.shape[1], group * HEAD_DIM), BF),
        "wave": pltpu.VMEM((16, 512), F32),
        "code_in": pltpu.VMEM((8, keys), F32),
        "small": pltpu.VMEM((16, width), F32),
        "small_in": pltpu.VMEM((4, 16, width), F32),
        "small_z": pltpu.VMEM((4, 16, width), F32),
        "send_sems": pltpu.SemaphoreType.DMA((LINK_SEMS,)),
        "recv_sems": pltpu.SemaphoreType.DMA((LINK_SEMS,)),
        "local_sems": pltpu.SemaphoreType.DMA((3,)),
    }
    operands = {
        "far_bias": (rel_table, smem),
        "rel_table": (rel_table, vmem),
        "row_len": (row_len, smem),
        "seg_ids": (seg_ids, vmem),
        "slot_mask": (slot_mask, vmem),
        "mem_keys": (mem_keys, vmem),
        "mem_values": (mem_values, vmem),
        "w_qkv": (w_qkv, vmem),
        "w_attn_out": (w_attn_out, vmem),
        "w_up": (w_up, vmem),
        "w_down": (w_down, vmem),
        "hot": (hot, vmem),
        "gains": (gains, vmem),
        "hidden": (hidden_in, any_space),
        "out_grad": (out_grad, any_space),
    }
    results = {
        "output": (jax.ShapeDtypeStruct(hidden_in.shape, BF), any_space),
        "grad_in": (jax.ShapeDtypeStruct(hidden_in.shape, BF), any_space),
        "gsum": (jax.ShapeDtypeStruct((3, shard, width), F32), vmem),
        "small_sum": (jax.ShapeDtypeStruct((16, width), F32), vmem),
    }
    names = [*operands, *results, *scratch]
    output, grad_input, gsum, small = pl.pallas_call(
        functools.partial(layer_kernel, names),
        out_shape=[shape for shape, _ in results.values()],
        in_specs=[spec for _, spec in operands.values()],
        out_specs=[spec for _, spec in results.values()],
        scratch_shapes=list(scratch.values()),
        compiler_params=pltpu.CompilerParams(
            collective_id=0, has_side_effects=True, vmem_limit_bytes=VMEM_LIMIT
        ),
    )(*[array for array, _ in operands.values()])
    inputs = {"output": output, "grad_in": grad_input, "gsum": gsum, "small": small, "hot": hot}
    results = {
        "output_out": jax.ShapeDtypeStruct(hidden_in.shape, BF),
        "grad_input": jax.ShapeDtypeStruct(hidden_in.shape, F32),
    }
    for name, w, m, v in (
        ("qkv", w_qkv, m_qkv, v_qkv),
        ("attn_out", w_attn_out, m_attn_out, v_attn_out),
        ("up", w_up, m_up, v_up),
        ("down", w_down, m_down, v_down),
        ("gains", gains, m_gains, v_gains),
        ("rel", rel_table, m_rel, v_rel),
    ):
        inputs |= {"w_" + name: w, "m_" + name: m, "v_" + name: v}
        kinds = ("new", "first", "second") if name in ("gains", "rel") else ("new", "first", "second", "copy")
        for kind in kinds:
            results[kind + "_" + name] = jax.ShapeDtypeStruct(w.shape, BF if kind == "copy" else F32)
    made = pl.pallas_call(
        functools.partial(update_kernel, [*inputs, *results]),
        out_shape=list(results.values()),
        in_specs=[vmem] * len(inputs),
        out_specs=[vmem] * len(results),
        compiler_params=pltpu.CompilerParams(vmem_limit_bytes=VMEM_LIMIT),
    )(*inputs.values())
    return tuple(array.T if name.endswith(("_down", "_rel")) else array for name, array in zip(results, made))


def solution(mesh):
    if dict(mesh.shape) == {"dp": 8, "mp": 4}:
        mesh = Mesh(mesh.devices.reshape(2, 2, 2, 4), ("y", "x", "c", "z"))
        return placed_on(mesh, on_moved, ("y", "x", "c"), "z")
    return placed_on(mesh, on_device, "dp", "mp")


def placed_on(mesh, body, dp, mp):
    placed = (
        P(dp, mp, None),
        P(dp, mp, None),
        P(dp, None),
        P(dp),
        P(dp, None),
        P(dp, None, mp),
        P(dp, None, mp),
        P(None, dp, mp),
        P(None, dp, mp),
        P(None, dp, mp),
        P(mp, dp),
        P(mp, dp),
        P(mp, dp),
        P(dp, mp),
        P(dp, mp),
        P(dp, mp),
        P(mp, dp),
        P(mp, dp),
        P(mp, dp),
        P(),
        P(),
        P(),
        P(),
        P(),
        P(),
    )
    return jax.shard_map(
        body,
        mesh=mesh,
        in_specs=placed,
        out_specs=(
            P(dp, mp, None),
            P(dp, mp, None),
            P(None, dp, mp),
            P(None, dp, mp),
            P(None, dp, mp),
            P(None, dp, mp),
            P(mp, dp),
            P(mp, dp),
            P(mp, dp),
            P(mp, dp),
            P(dp, mp),
            P(dp, mp),
            P(dp, mp),
            P(dp, mp),
            P(mp, dp),
            P(mp, dp),
            P(mp, dp),
            P(mp, dp),
            P(),
            P(),
            P(),
            P(),
            P(),
            P(),
        ),
        check_vma=False,
    )
```
